128 devices in a mesh: shard: 16 (over x_hi, y, core), replica: 8 (over x_lo, z).
Axes of the slice: x: 4 (x_hi: 2, x_lo: 2; x = x_hi * 2 + x_lo), y: 4, z: 4, core: 2. Of those that a mesh axis runs over, the one named last changes fastest.
Arguments:
- tokens: bfloat16 [24576, 1024], P(('shard', 'replica')), may hold values from -6 to 6
- seq_lengths: int32 [128, 2], P(('shard', 'replica')), may hold values from 32 to 160, as said below
- routes: int32 [24576, 8], P(('shard', 'replica')), may hold values from 0 to 15, all different within a row; in each aligned block of 192 rows (0 to 191, 192 to 383, ...) at most 120 rows name the same one
- attn_gain: bfloat16 [1024], replicated, may hold values from 0.5 to 1.5
- ffn_gain: bfloat16 [1024], replicated, may hold values from 0.5 to 1.5
- w_query: bfloat16 [1024, 1024], P('shard'), may hold values from -0.1875 to 0.1875
- key_projection: bfloat16 [1024, 512], P('shard'), may hold values from -0.1875 to 0.1875
- value_projection: bfloat16 [1024, 512], P('shard'), may hold values from -0.1875 to 0.1875
- w_output: bfloat16 [1024, 1024], P('shard'), may hold values from -1.5 to 1.5
- w_router: bfloat16 [1024, 16], P('shard'), may hold values from -0.09375 to 0.09375
- w_in: bfloat16 [16, 1024, 1024], P('shard'), may hold values from -0.1875 to 0.1875
- w_out: bfloat16 [16, 512, 1024], P('shard'), may hold values from -1 to 1
- cotangent: bfloat16 [24576, 1024], P(('shard', 'replica')), may hold values from -6 to 6
Outputs:
- output: bfloat16 [24576, 1024], P(('shard', 'replica'))
- d_tokens: float32 [24576, 1024], P(('shard', 'replica'))
- d_attn_gain: float32 [1024], replicated
- d_ffn_gain: float32 [1024], replicated
- d_query: float32 [1024, 1024], P('shard')
- d_key: float32 [1024, 512], P('shard')
- d_value: float32 [1024, 512], P('shard')
- d_output: float32 [1024, 1024], P('shard')
- d_router: float32 [1024, 16], P('shard')
- d_in: float32 [16, 1024, 1024], P('shard')
- d_out: float32 [16, 512, 1024], P('shard')
The draws below stay inside these ranges and needn't reach their ends.
Inputs may be any that keep to these rules, and one draw needn't show every extreme that they name: `seq_lengths`: row b holds the lengths of the 2 sequences dealt to block b, laid end to end from its first row; they sum to at most 192, the rest of the block is padding, and some block is full. `routes`: each row names 8 different experts; in each aligned block of 192 rows no expert is named by more than 120 rows.
All inputs are finite; a program needn't handle non-finite values.
Results may differ from the reference program's by a relative error of at most 0.023.
Values may be sent and summed in bfloat16 or wider, within the bound.
A program may use at most 128 MiB of HBM per device.

```python
import math
import jax
import jax.numpy as jnp
import numpy as np
from jax import lax

MODEL_WIDTH = 1024
QUERY_HEADS = 16
KEY_VALUE_HEADS = 8
HEAD_SIZE = 64
H = 512
TOP = 8
E = 16
TOK_DEV = 192
MIN_LEN = 32
CAP = 120
TOKENS = 24576
DEVICES = 128


def draw_seq_lengths(key, part):
    key = jax.random.fold_in(key, 11)
    first_key, second_key, full_key = jax.random.split(key, 3)
    first_len = jax.random.randint(first_key, (DEVICES,), MIN_LEN, TOK_DEV - MIN_LEN + 1)
    spread = jax.random.randint(second_key, (DEVICES,), 0, 4096)
    second = MIN_LEN + spread * (TOK_DEV - first_len - MIN_LEN + 1) // 4096
    full_block = jax.random.randint(full_key, (), 0, DEVICES)
    picked = jnp.arange(DEVICES) == full_block
    first_len = jnp.where(picked, TOK_DEV - MIN_LEN, first_len)
    second = jnp.where(picked, MIN_LEN, second)
    return jnp.stack([first_len, second], axis=1).astype(jnp.int32)


def steps_of(own_key, extent, pieces, smallest, top_value):
    loudness, own = 1.0, jax.random.fold_in(own_key, 6)
    for axis_at, parts in pieces:
        heights = jnp.exp(jax.random.uniform(jax.random.fold_in(own, axis_at), (parts,), jnp.float32, smallest / len(pieces), top_value / len(pieces)))
        loudness = loudness * jnp.repeat(heights, extent[axis_at] // parts).reshape([-1 if axis == axis_at else 1 for axis in range(len(extent))])
    return loudness


def deal_out(own_key, own, number, rows, count, top, reach, slope):
    ranking = jax.random.permutation(own_key, count)
    packed, ordinary = portions_of(count, rows * top, reach, slope, True), portions_of(count, rows * top, reach, slope, False)
    places = jnp.arange(count)

    def named(sizes, offset_by):
        used = int((sizes > 0).sum())
        fixed = max(1, used // 4)
        moved = fixed + (places - fixed + offset_by * (used - fixed)) % max(1, count - fixed)
        return jnp.zeros((count,), jnp.int32).at[ranking[jnp.where(places < fixed, places, moved)]].set(jnp.asarray(sizes, jnp.int32))

    sizes = jnp.where(number % 4 == 0, named(packed, number // 4), named(ordinary, number - number // 4 - 1))
    mixed = jax.random.permutation(jax.random.fold_in(own, 3), count)
    giver, receiver = mixed[0:count // 2 * 2:2], mixed[1:count // 2 * 2:2]
    slack = jnp.minimum(sizes[giver] - 1, reach - sizes[receiver]) // 2
    slack = jnp.where((giver == ranking[0]) | (receiver == ranking[0]) | (sizes[receiver] == 0), 0, jnp.maximum(slack, 0))
    moved = jax.random.randint(jax.random.fold_in(own, 4), (count // 2,), 0, 1 << 20) % (slack + 1)
    sizes = sizes.at[giver].add(-moved).at[receiver].add(moved)
    labels = jnp.searchsorted(jnp.cumsum(sizes), jnp.arange(rows * top), side="right").astype(jnp.int32)
    table = labels.reshape(top, rows).T
    table = table[jax.random.permutation(jax.random.fold_in(own, 1), rows)]
    offset_by = jax.random.randint(jax.random.fold_in(own, 2), (rows, 1), 0, top)
    return jnp.take_along_axis(table, (jnp.arange(top)[None, :] + offset_by) % top, axis=1)


def portions_of(number_of, total, bound, lean, full):
    loads = [(1 << 20) // math.isqrt(standing ** lean) + 1 for standing in range(1, number_of + 1)]
    largest = bound if full else min(bound, max(-(-total // number_of), total * loads[0] // sum(loads)))
    least = 1 if total - largest >= number_of - 1 else 0
    holding, rest = [largest] + [least] * (number_of - 1), total - largest - least * (number_of - 1)
    while rest > 0:
        movable = [i for i in range(1, number_of) if holding[i] < largest] or [i for i in range(1, number_of) if holding[i] < bound]
        mass, budget = sum([loads[i] for i in movable]), rest
        for i in movable:
            extra = min(bound - holding[i], max(1, budget * loads[i] // mass), rest)
            holding[i] = holding[i] + extra
            rest = rest - extra
    return np.array(holding)


def noise(stream_key, extent, scale, bound, pieces=(), kind=jnp.bfloat16):
    values = jax.random.normal(stream_key, extent, jnp.float32) * scale
    if len(pieces) > 0:
        values = steps_of(stream_key, extent, pieces, -0.22, 0.18) * values
    return jnp.clip(values, min=-bound, max=bound).astype(kind)


def setup_inputs(seed: int = 0) -> dict:
    key_list = jax.random.split(jax.random.key(seed), 14)
    tokens = noise(key_list[0], (TOKENS, MODEL_WIDTH), 1.0, 6.0, ((0, 128),))
    seq_lengths = draw_seq_lengths(jax.random.fold_in(key_list[13], 71), 0)
    routes_keys = jax.random.split(jax.random.fold_in(key_list[2], 1), TOKENS // TOK_DEV)
    routes_turns = jax.random.permutation(jax.random.fold_in(key_list[2], 3), TOKENS // TOK_DEV)
    routes = jax.vmap(lambda own, number: deal_out(jax.random.fold_in(key_list[2], 2), own, number, TOK_DEV, E, TOP, CAP, 2))(routes_keys, routes_turns).reshape((TOKENS, TOP))
    attn_gain = jnp.clip(1.0 + 0.1 * jax.random.normal(key_list[3], (MODEL_WIDTH,), jnp.float32), 0.5, 1.5).astype(jnp.bfloat16)
    ffn_gain = jnp.clip(1.0 + 0.1 * jax.random.normal(key_list[4], (MODEL_WIDTH,), jnp.float32), 0.5, 1.5).astype(jnp.bfloat16)
    w_query = noise(key_list[5], (MODEL_WIDTH, QUERY_HEADS * HEAD_SIZE), MODEL_WIDTH ** -0.5, 0.1875, ((0, 16),))
    key_projection = noise(key_list[6], (MODEL_WIDTH, KEY_VALUE_HEADS * HEAD_SIZE), MODEL_WIDTH ** -0.5, 0.1875, ((0, 16),))
    value_projection = noise(key_list[7], (MODEL_WIDTH, KEY_VALUE_HEADS * HEAD_SIZE), MODEL_WIDTH ** -0.5, 0.1875, ((0, 16),))
    w_output = noise(key_list[8], (QUERY_HEADS * HEAD_SIZE, MODEL_WIDTH), (QUERY_HEADS * HEAD_SIZE // 64) ** -0.5, 1.5, ((0, 16),))
    w_router = noise(key_list[9], (MODEL_WIDTH, E), (4 * MODEL_WIDTH) ** -0.5, 0.09375, ((0, 16),))
    w_in = noise(key_list[10], (E, MODEL_WIDTH, 2 * H), MODEL_WIDTH ** -0.5, 0.1875, ((0, 16),))
    w_out = noise(key_list[11], (E, H, MODEL_WIDTH), (H // 16) ** -0.5, 1.0, ((0, 16),))
    cotangent = noise(key_list[12], (TOKENS, MODEL_WIDTH), 1.0, 6.0, ((0, 128),))
    return {"tokens": tokens, "seq_lengths": seq_lengths, "routes": routes, "attn_gain": attn_gain, "ffn_gain": ffn_gain, "w_query": w_query, "key_projection": key_projection, "value_projection": value_projection, "w_output": w_output, "w_router": w_router, "w_in": w_in, "w_out": w_out, "cotangent": cotangent}


EPS = 1e-06
ROPE_BASE = 10000.0
NEGATIVE = -1e+30
FULL_PRECISION = lax.Precision.HIGHEST

@jax.custom_vjp
def lower_cast(v):
    return lax.optimization_barrier(v.astype(jnp.bfloat16)).astype(jnp.float32)

@jax.custom_vjp
def lower_cast_backward(v):
    return v

def low_keep(v):
    return (lower_cast(v), None)

def low_pass(kept, grad):
    return (grad,)

def back_keep(v):
    return (v, None)

def back_low(kept, grad):
    return (lower_cast(grad),)
lower_cast.defvjp(low_keep, low_pass)
lower_cast_backward.defvjp(back_keep, back_low)

def norm_apply(value_rows, gain_vec):
    return value_rows * lax.rsqrt(lax.optimization_barrier(jnp.mean(value_rows * value_rows, axis=1, keepdims=True)) + EPS) * gain_vec

def layout(lengths, count_of_rows):
    row_index = jnp.arange(count_of_rows, dtype=jnp.int32)
    first_len = lengths[0].astype(jnp.int32)
    total_len = (lengths[0] + lengths[1]).astype(jnp.int32)
    doc_index = jnp.where(row_index < first_len, 0, jnp.where(row_index < total_len, 1, 2)).astype(jnp.int32)
    doc_start = jnp.where(row_index < first_len, 0, jnp.where(row_index < total_len, first_len, total_len)).astype(jnp.int32)
    allowed = (doc_index[:, None] == doc_index[None, :]) & (row_index[None, :] <= row_index[:, None])
    return (row_index - doc_start, row_index < total_len, allowed)

def tables(position, head_dim):
    half_dim = head_dim // 2
    frequency = jnp.exp(jnp.arange(half_dim, dtype=jnp.float32) * (-2.0 * math.log(ROPE_BASE) / head_dim))
    angles = position.astype(jnp.float32)[:, None] * frequency[None, :]
    return (jnp.cos(angles), jnp.sin(angles))

def rotary_apply(value_rows, cosine_table, sine_lookup, head_count, head_dim):
    count_of_rows = value_rows.shape[0]
    halves = value_rows.reshape(count_of_rows, head_count, 2, head_dim // 2)
    first_half = halves[:, :, 0]
    second = halves[:, :, 1]
    cos_rows = cosine_table[:, None, :]
    sin_rows = sine_lookup[:, None, :]
    turned = jnp.stack([first_half * cos_rows - second * sin_rows, second * cos_rows + first_half * sin_rows], axis=2)
    return turned.reshape(count_of_rows, head_count * head_dim)

def smooth_gate(value_rows):
    return value_rows * jax.nn.sigmoid(value_rows)

def softmax_last(score_matrix):
    largest = lax.optimization_barrier(jnp.max(score_matrix, axis=-1, keepdims=True))
    shifted = jnp.exp(score_matrix - largest)
    return shifted / lax.optimization_barrier(jnp.sum(shifted, axis=-1, keepdims=True))

def slots(routes, experts, capacity):
    flat_routes = routes.reshape(-1).astype(jnp.int32)
    onehot = (flat_routes[:, None] == jnp.arange(experts, dtype=jnp.int32)[None, :]).astype(jnp.int32)
    route_rank = lax.optimization_barrier(jnp.sum((jnp.cumsum(onehot, axis=0).astype(jnp.int32) - 1) * onehot, axis=1)).astype(jnp.int32)
    slot_index = (flat_routes * capacity + route_rank).astype(jnp.int32)
    source = jnp.zeros((experts * capacity,), jnp.int32).at[slot_index].set(jnp.arange(flat_routes.shape[0], dtype=jnp.int32))
    filled = jnp.zeros((experts * capacity,), jnp.int32).at[slot_index].set(1)
    return (slot_index, source, filled)

def block(params, inputs, lengths, routes):
    attn_gain, ffn_gain, w_query, key_projection, value_projection, w_output, w_router, w_in, w_out = params
    count_of_rows = inputs.shape[0]
    replica_group_size = QUERY_HEADS // KEY_VALUE_HEADS
    position, live_rows, allowed = layout(lengths, count_of_rows)
    live_mask = live_rows.astype(inputs.dtype)[:, None]
    cosine_table, sine_lookup = tables(position, HEAD_SIZE)
    first_normalized = lower_cast(norm_apply(inputs, attn_gain))
    query_matrix = lower_cast(rotary_apply(lower_cast_backward(jnp.dot(first_normalized, w_query, precision=FULL_PRECISION)), cosine_table, sine_lookup, QUERY_HEADS, HEAD_SIZE))
    key_rows = lower_cast(rotary_apply(lower_cast_backward(jnp.dot(first_normalized, key_projection, precision=FULL_PRECISION)), cosine_table, sine_lookup, KEY_VALUE_HEADS, HEAD_SIZE))
    value_rows = lower_cast(lower_cast_backward(jnp.dot(first_normalized, value_projection, precision=FULL_PRECISION)))
    heads_of_query = query_matrix.reshape(count_of_rows, KEY_VALUE_HEADS, replica_group_size, HEAD_SIZE)
    heads_of_key = key_rows.reshape(count_of_rows, KEY_VALUE_HEADS, HEAD_SIZE)
    heads_of_value = value_rows.reshape(count_of_rows, KEY_VALUE_HEADS, HEAD_SIZE)
    score_matrix = lower_cast_backward(jnp.einsum('ehla,jha->hlej', heads_of_query, heads_of_key, precision=FULL_PRECISION) * HEAD_SIZE ** (-0.5))
    score_matrix = jnp.where(allowed, score_matrix, NEGATIVE)
    attention_probability = softmax_last(score_matrix)
    mixture_heads = jnp.einsum('pjwi,ipx->wpjx', lower_cast(attention_probability), heads_of_value, precision=FULL_PRECISION).reshape(count_of_rows, QUERY_HEADS * HEAD_SIZE)
    mixture_heads = lower_cast(lower_cast_backward(mixture_heads))
    attn_out = lower_cast_backward(jnp.dot(mixture_heads, w_output, precision=FULL_PRECISION))
    hidden_one = inputs + live_mask * attn_out
    normed_second = lower_cast(norm_apply(hidden_one, ffn_gain))
    logits = lower_cast_backward(jnp.dot(normed_second, w_router, precision=FULL_PRECISION))
    route_pick = (routes[:, :, None] == jnp.arange(E, dtype=jnp.int32)[None, None, :]).astype(inputs.dtype)
    chosen = lax.optimization_barrier(jnp.sum(route_pick * logits[:, None, :], axis=2))
    gate_values = softmax_last(chosen)
    slot_index, source, filled = slots(routes, E, CAP)
    expert_rows = lower_cast_backward(normed_second[source // TOP] * filled.astype(inputs.dtype)[:, None]).reshape(E, CAP, MODEL_WIDTH)
    pre_act = lower_cast_backward(jnp.einsum('ecd,edf->ecf', expert_rows, w_in, precision=FULL_PRECISION))
    activation = lower_cast(smooth_gate(pre_act[..., :H]) * pre_act[..., H:])
    result = lower_cast(lower_cast_backward(jnp.einsum('ech,ehd->ecd', activation, w_out, precision=FULL_PRECISION))).reshape(E * CAP, MODEL_WIDTH)
    per_route = result[slot_index].reshape(count_of_rows, TOP, MODEL_WIDTH)
    expert_mix = lax.optimization_barrier(jnp.sum(gate_values[:, :, None] * per_route, axis=1))
    return hidden_one + live_mask * expert_mix

def reference(tokens, seq_lengths, routes, attn_gain, ffn_gain, w_query, key_projection, value_projection, w_output, w_router, w_in, w_out, cotangent):
    params = tuple((weight.astype(jnp.float32) for weight in (attn_gain, ffn_gain, w_query, key_projection, value_projection, w_output, w_router, w_in, w_out)))
    blocks = tokens.astype(jnp.float32).reshape(DEVICES, TOK_DEV, MODEL_WIDTH)
    block_routes = routes.reshape(DEVICES, TOK_DEV, TOP)
    block_step = jax.checkpoint(block)

    def forward(weights, inputs):
        return lax.map(lambda block_item: block_step(weights, block_item[0], block_item[1], block_item[2]), (inputs, seq_lengths, block_routes))
    output, pullback = jax.vjp(forward, params, blocks)
    gradients, block_grads = pullback(cotangent.astype(jnp.float32).reshape(DEVICES, TOK_DEV, MODEL_WIDTH))
    return (output.reshape(TOKENS, MODEL_WIDTH).astype(jnp.bfloat16), block_grads.reshape(TOKENS, MODEL_WIDTH), gradients[0], gradients[1], gradients[2], gradients[3], gradients[4], gradients[5], gradients[6], gradients[7], gradients[8])
```

```python
import functools
import math

import jax
import jax.numpy as jnp
from jax import lax
from jax.experimental import pallas as pl
from jax.experimental.pallas import tpu as pltpu
from jax.sharding import PartitionSpec as P

QUERY_HEADS = 16
KEY_VALUE_HEADS = 8
HEAD_SIZE = 64
H = 512
E = 16
CAP = 120
PACKED = 3328

EPS = 1e-06
ROPE_BASE = 10000.0
NEGATIVE = -1e30

MESH = pl.DeviceIdType.MESH


def place():
    me = lax.axis_index("shard")
    rep = lax.axis_index("replica")
    core = lax.rem(me, 2)
    y = lax.rem(me // 2, 4)
    high = me // 8
    return me, rep, core, y, high


def index_of(high, y, core):
    return (high * 4 + lax.rem(y, 4)) * 2 + core


def greet(targets):
    barrier = pltpu.get_barrier_semaphore()
    for target in targets:
        pl.semaphore_signal(barrier, inc=1, device_id=target, device_id_type=MESH)
    pl.semaphore_wait(barrier, len(targets))


def gather_kernel(cut, block_ref, out_ref, local_sem, send_sem, recv_sem):
    me, rep, core, y, high = place()
    rows = block_ref.shape[0]
    mate = (index_of(high, y, 1 - core), rep)
    up = (index_of(high, y + 1, core), rep)
    down = (index_of(high, y + 3, core), rep)
    across = (index_of(1 - high, y, core), rep)
    greet([mate, up, down, across])
    top, low = pl.ds(0, cut), pl.ds(cut, rows - cut)

    def remote(number, source, slot, span, target):
        return pltpu.make_async_remote_copy(
            src_ref=source,
            dst_ref=out_ref.at[slot, span],
            send_sem=send_sem.at[number],
            recv_sem=recv_sem.at[number],
            device_id=target,
            device_id_type=MESH,
        )

    whole = pl.ds(0, rows)
    other = index_of(1 - high, y, core)
    from_down = index_of(high, y + 3, core)
    from_up = index_of(high, y + 1, core)
    far = index_of(high, y + 2, core)
    other_down = index_of(1 - high, y + 3, core)
    other_up = index_of(1 - high, y + 1, core)
    other_far = index_of(1 - high, y + 2, core)
    own_across = remote(0, block_ref, me, whole, across)
    own_up = remote(1, block_ref, me, whole, up)
    own_down = remote(2, block_ref, me, whole, down)
    own_mate = remote(3, block_ref, me, whole, mate)
    copies = [own_across, own_up, own_down, own_mate]
    for copy in copies:
        copy.start()
    local = pltpu.make_async_copy(block_ref, out_ref.at[me], local_sem)
    local.start()

    def onward(number, slot, span, target):
        copy = remote(number, out_ref.at[slot, span], slot, span, target)
        copy.start()
        copies.append(copy)
        return copy

    own_up.wait_recv()
    far_up = onward(4, from_down, top, up)
    own_down.wait_recv()
    far_down = onward(5, from_up, low, down)
    own_across.wait_recv()
    other_to_up = onward(6, other, whole, up)
    other_to_down = onward(7, other, whole, down)
    mates = [own_mate]
    mates.append(onward(8, from_down, whole, mate))
    mates.append(onward(9, from_up, whole, mate))
    mates.append(onward(10, other, whole, mate))
    other_to_up.wait_recv()
    other_far_up = onward(11, other_down, top, up)
    other_to_down.wait_recv()
    other_far_down = onward(12, other_up, low, down)
    mates.append(onward(13, other_down, whole, mate))
    mates.append(onward(14, other_up, whole, mate))
    far_up.wait_recv()
    mates.append(onward(15, far, top, mate))
    far_down.wait_recv()
    mates.append(onward(16, far, low, mate))
    other_far_up.wait_recv()
    mates.append(onward(17, other_far, top, mate))
    other_far_down.wait_recv()
    mates.append(onward(18, other_far, low, mate))
    for copy in mates:
        copy.wait_recv()
    for copy in copies:
        copy.wait_send()
    local.wait()


def gather_rows(block, collective_id):
    rows, width = block.shape
    cut = (rows // 16 + 1) // 2 * 16
    return pl.pallas_call(
        functools.partial(gather_kernel, cut),
        out_shape=jax.ShapeDtypeStruct((16, rows, width), block.dtype),
        in_specs=[pl.BlockSpec(memory_space=pl.ANY)],
        out_specs=pl.BlockSpec(memory_space=pl.ANY),
        scratch_shapes=[
            pltpu.SemaphoreType.DMA,
            pltpu.SemaphoreType.DMA((19,)),
            pltpu.SemaphoreType.DMA((19,)),
        ],
        compiler_params=pltpu.CompilerParams(collective_id=collective_id, has_side_effects=True),
        cost_estimate=pl.CostEstimate(
            flops=0, bytes_accessed=16 * rows * width * 2 * 8, transcendentals=0
        ),
    )(block)


def add_rows(target, source, start, count):
    def body(step, carry):
        at = pl.ds(pl.multiple_of(start + step * 16, 16), 16)
        here = pl.ds(pl.multiple_of(step * 16, 16), 16)
        target[at, :] = (
            target[at, :].astype(jnp.float32) + source[here, :].astype(jnp.float32)
        ).astype(target.dtype)
        return carry

    lax.fori_loop(0, count // 16, body, 0)


def scatter_kernel(
    cut, blocks_ref, out_ref, sums, mates, near_up, near_down, far_up, far_down, cross,
    local_sem, send_sem, recv_sem,
):
    me, rep, core, y, high = place()
    rows = out_ref.shape[0]
    mate = (index_of(high, y, 1 - core), rep)
    up = (index_of(high, y + 1, core), rep)
    down = (index_of(high, y + 3, core), rep)
    across = (index_of(1 - high, y, core), rep)
    greet([mate, up, down, across])

    def remote(number, source, target_ref, target):
        return pltpu.make_async_remote_copy(
            src_ref=source,
            dst_ref=target_ref,
            send_sem=send_sem.at[number],
            recv_sem=recv_sem.at[number],
            device_id=target,
            device_id_type=MESH,
        )

    order = [4, 5, 2, 3, 6, 7, 0, 1]
    locals_, swaps, sends = {}, {}, []
    for slot in order:
        d, o = slot // 2, slot % 2
        side = 1 - high if o == 0 else high
        swap = remote(slot, blocks_ref.at[index_of(side, y + d, 1 - core)], mates.at[slot], mate)
        swap.start()
        swaps[slot] = swap
        sends.append(swap)
        local = pltpu.make_async_copy(
            blocks_ref.at[index_of(side, y + d, core)], sums.at[slot], local_sem.at[slot]
        )
        local.start()
        locals_[slot] = local

    def settle(slot):
        locals_[slot].wait()
        swaps[slot].wait_recv()
        add_rows(sums.at[slot], mates.at[slot], 0, rows)

    top, low = pl.ds(0, cut), pl.ds(cut, rows - cut)
    firsts = []
    for o in range(2):
        settle(4 + o)
        one = remote(8 + o, sums.at[4 + o, top], far_up.at[o], up)
        two = remote(10 + o, sums.at[4 + o, low], far_down.at[o], down)
        one.start()
        two.start()
        firsts.append((one, two))
        sends += [one, two]
    seconds = []
    for o in range(2):
        settle(2 + o)
        settle(6 + o)
        one, two = firsts[o]
        one.wait_recv()
        add_rows(sums.at[2 + o], far_up.at[o], 0, cut)
        one = remote(12 + o, sums.at[2 + o], near_up.at[o], up)
        one.start()
        two.wait_recv()
        add_rows(sums.at[6 + o], far_down.at[o], cut, rows - cut)
        two = remote(14 + o, sums.at[6 + o], near_down.at[o], down)
        two.start()
        seconds.append((one, two))
        sends += [one, two]
    for o in range(2):
        settle(o)
        one, two = seconds[o]
        one.wait_recv()
        add_rows(sums.at[o], near_up.at[o], 0, rows)
        two.wait_recv()
        add_rows(sums.at[o], near_down.at[o], 0, rows)
        if o == 0:
            last = remote(16, sums.at[0], cross, across)
            last.start()
            sends.append(last)
    last.wait_recv()

    def body(step, carry):
        at = pl.ds(pl.multiple_of(step * 16, 16), 16)
        out_ref[at, :] = (
            sums[1, at, :].astype(jnp.float32) + cross[at, :].astype(jnp.float32)
        ).astype(out_ref.dtype)
        return carry

    lax.fori_loop(0, rows // 16, body, 0)
    for copy in sends:
        copy.wait_send()


def scatter_rows(blocks, collective_id, out_type):
    count, rows, width = blocks.shape
    cut = (rows // 16 + 1) // 2 * 16
    kind = blocks.dtype
    return pl.pallas_call(
        functools.partial(scatter_kernel, cut),
        out_shape=jax.ShapeDtypeStruct((rows, width), out_type),
        in_specs=[pl.BlockSpec(memory_space=pl.ANY)],
        out_specs=pl.BlockSpec(memory_space=pltpu.VMEM),
        scratch_shapes=[
            pltpu.VMEM((8, rows, width), kind),
            pltpu.VMEM((8, rows, width), kind),
            pltpu.VMEM((2, rows, width), kind),
            pltpu.VMEM((2, rows, width), kind),
            pltpu.VMEM((2, cut, width), kind),
            pltpu.VMEM((2, rows - cut, width), kind),
            pltpu.VMEM((rows, width), kind),
            pltpu.SemaphoreType.DMA((8,)),
            pltpu.SemaphoreType.DMA((17,)),
            pltpu.SemaphoreType.DMA((17,)),
        ],
        compiler_params=pltpu.CompilerParams(
            collective_id=collective_id, has_side_effects=True, vmem_limit_bytes=40 * 1024 * 1024
        ),
        cost_estimate=pl.CostEstimate(
            flops=0, bytes_accessed=16 * rows * width * 2 * 8, transcendentals=0
        ),
    )(blocks)


def total_kernel(part_ref, out_ref, pieces, send_sem, recv_sem, send_back, recv_back):
    shard = lax.axis_index("shard")
    me = lax.axis_index("replica")
    rows, width = part_ref.shape
    others = [(shard, lax.rem(me + step, 8)) for step in range(1, 8)]
    greet(others)

    def piece(ref, which):
        half = width // 2
        return ref.at[
            pl.ds(pl.multiple_of((which // 2) * 16, 16), 16),
            pl.ds(pl.multiple_of(lax.rem(which, 2) * half, 128), half),
        ]

    firsts = []
    for step in range(1, 8):
        target = lax.rem(me + step, 8)
        copy = pltpu.make_async_remote_copy(
            src_ref=piece(part_ref, target),
            dst_ref=pieces.at[step - 1],
            send_sem=send_sem.at[step - 1],
            recv_sem=recv_sem.at[step - 1],
            device_id=(shard, target),
            device_id_type=MESH,
        )
        copy.start()
        firsts.append(copy)
    total = piece(part_ref, me)[...].astype(jnp.float32)
    for step in range(1, 8):
        firsts[step - 1].wait_recv()
        total = total + pieces[step - 1].astype(jnp.float32)
    piece(out_ref, me)[...] = total.astype(out_ref.dtype)
    seconds = []
    for step in range(1, 8):
        target = lax.rem(me + step, 8)
        copy = pltpu.make_async_remote_copy(
            src_ref=piece(out_ref, me),
            dst_ref=piece(out_ref, me),
            send_sem=send_back.at[step - 1],
            recv_sem=recv_back.at[step - 1],
            device_id=(shard, target),
            device_id_type=MESH,
        )
        copy.start()
        seconds.append(copy)
    for copy in seconds:
        copy.wait_recv()
    for copy in firsts + seconds:
        copy.wait_send()


def total_rows(part, collective_id):
    rows, width = part.shape
    return pl.pallas_call(
        total_kernel,
        out_shape=jax.ShapeDtypeStruct((rows, width), part.dtype),
        in_specs=[pl.BlockSpec(memory_space=pltpu.VMEM)],
        out_specs=pl.BlockSpec(memory_space=pltpu.VMEM),
        scratch_shapes=[
            pltpu.VMEM((7, 16, width // 2), part.dtype),
            pltpu.SemaphoreType.DMA((7,)),
            pltpu.SemaphoreType.DMA((7,)),
            pltpu.SemaphoreType.DMA((7,)),
            pltpu.SemaphoreType.DMA((7,)),
        ],
        compiler_params=pltpu.CompilerParams(collective_id=collective_id, has_side_effects=True),
    )(part)


def heads_first(rows, width):
    return rows.reshape(rows.shape[0], -1, width)


def rotate(value_rows, cosine_table, sine_table):
    count = value_rows.shape[0]
    halves = value_rows.reshape(count, -1, 2, HEAD_SIZE // 2)
    first, second = halves[:, :, 0], halves[:, :, 1]
    cos_rows, sin_rows = cosine_table[:, None, :], sine_table[:, None, :]
    turned = jnp.stack(
        [first * cos_rows - second * sin_rows, second * cos_rows + first * sin_rows], axis=2
    )
    return turned.reshape(count, -1)


def dot(a, b):
    return jnp.dot(a, b, preferred_element_type=jnp.float32)


def einsum(form, a, b):
    return jnp.einsum(form, a, b, preferred_element_type=jnp.float32)


def split_two(values):
    upper = values.astype(jnp.bfloat16)
    return upper, (values - upper.astype(jnp.float32)).astype(jnp.bfloat16)


def local(
    tokens,
    seq_lengths,
    routes,
    attn_gain,
    ffn_gain,
    w_query,
    key_projection,
    value_projection,
    w_output,
    w_router,
    w_in,
    w_out,
    cotangent,
):
    rows, width = tokens.shape
    group = QUERY_HEADS // KEY_VALUE_HEADS
    scale = HEAD_SIZE ** (-0.5)
    expert = lax.axis_index("shard")
    w_in, w_out = w_in[0], w_out[0]
    bf16, f32 = jnp.bfloat16, jnp.float32

    lengths = seq_lengths[0]
    row_index = jnp.arange(rows, dtype=jnp.int32)
    first_len, total_len = lengths[0], lengths[0] + lengths[1]
    doc = jnp.where(row_index < first_len, 0, jnp.where(row_index < total_len, 1, 2))
    start = jnp.where(
        row_index < first_len, 0, jnp.where(row_index < total_len, first_len, total_len)
    )
    allowed = (doc[:, None] == doc[None, :]) & (row_index[None, :] <= row_index[:, None])
    live = (row_index < total_len).astype(f32)[:, None]
    frequency = jnp.exp(
        jnp.arange(HEAD_SIZE // 2, dtype=f32) * (-2.0 * math.log(ROPE_BASE) / HEAD_SIZE)
    )
    angles = (row_index - start).astype(f32)[:, None] * frequency[None, :]
    cosine_table, sine_table = jnp.cos(angles), jnp.sin(angles)
    gain_first, gain_second = attn_gain.astype(f32), ffn_gain.astype(f32)

    packed = jnp.concatenate(
        [
            w_query,
            key_projection,
            value_projection,
            w_output,
            w_router,
            jnp.zeros((w_query.shape[0], PACKED - 3072 - E), bf16),
        ],
        axis=1,
    )
    weights = gather_rows(packed, 1).reshape(-1, PACKED)
    upstream = cotangent.astype(f32)
    mix_grad = (cotangent * live.astype(bf16)).astype(bf16)
    all_mix_grad = lax.all_gather(mix_grad, "shard", axis=0)

    inputs = tokens.astype(f32)
    scale_first = lax.rsqrt(jnp.mean(inputs * inputs, axis=1, keepdims=True) + EPS)
    normed_first = (inputs * scale_first * gain_first).astype(bf16)
    w_qkv, full_output, full_router = (
        weights[:, :2048],
        weights[:, 2048:3072],
        weights[:, 3072 : 3072 + E],
    )
    qkv = dot(normed_first, w_qkv)
    turned = rotate(qkv[:, :1536], cosine_table, sine_table).astype(bf16)
    query = turned[:, :1024].reshape(rows, KEY_VALUE_HEADS, group, HEAD_SIZE)
    key = turned[:, 1024:].reshape(rows, KEY_VALUE_HEADS, HEAD_SIZE)
    value = qkv[:, 1536:].astype(bf16).reshape(rows, KEY_VALUE_HEADS, HEAD_SIZE)
    scores = jnp.where(allowed, einsum("ehla,jha->hlej", query, key) * scale, NEGATIVE)
    largest = jnp.max(scores, axis=-1, keepdims=True)
    raised = jnp.exp(scores - largest)
    attn_prob = raised / jnp.sum(raised, axis=-1, keepdims=True)
    attn_prob_b = attn_prob.astype(bf16)
    mixed = einsum("pjwi,ipx->wpjx", attn_prob_b, value).reshape(rows, -1).astype(bf16)
    hidden_one = inputs + live * dot(mixed, full_output)
    scale_second = lax.rsqrt(jnp.mean(hidden_one * hidden_one, axis=1, keepdims=True) + EPS)
    normed_second = (hidden_one * scale_second * gain_second).astype(bf16)
    logits = dot(normed_second, full_router)
    named = jnp.any(routes[:, :, None] == jnp.arange(E, dtype=jnp.int32), axis=1)
    logits = jnp.where(named, logits, NEGATIVE)
    raised = jnp.exp(logits - jnp.max(logits, axis=1, keepdims=True))
    gates = raised / jnp.sum(raised, axis=1, keepdims=True)

    def side_rows(table):
        upper, lower = split_two(table)
        return jnp.concatenate(
            [jnp.pad(upper, ((0, 0), (0, 64))), jnp.pad(lower, ((0, 0), (0, 1024 - 448)))], axis=1
        )

    payload = jnp.concatenate([normed_second, side_rows(gates.T)], axis=0)
    arrived = gather_rows(payload, 2)
    own = lax.dynamic_slice(arrived, (0, rows + expert, 0), (16, 1, 448))[:, 0].astype(f32)
    own_gates = own[:, :rows] + own[:, 256 : 256 + rows]
    member = own_gates > 0
    earlier = (row_index[:, None] < row_index[None, :]).astype(bf16)
    rank = dot(member.astype(bf16), earlier).astype(jnp.int32)
    slot_of = jnp.where(member, rank, -1)
    pick = slot_of[:, None, :] == jnp.arange(CAP, dtype=jnp.int32)[None, :, None]
    pick_b = pick.astype(bf16)
    slot_gates = jnp.sum(jnp.where(pick, own_gates[:, None, :], 0.0), axis=2)[:, :, None]

    expert_rows = einsum("srt,std->srd", pick_b, arrived[:, :rows]).astype(bf16)
    mix_rows = einsum("srt,std->srd", pick_b, all_mix_grad).astype(bf16)
    expert_rows = expert_rows.reshape(16 * CAP, width)
    pre_act = dot(expert_rows, w_in)
    gate, up = pre_act[:, :H], pre_act[:, H:]
    sig = jax.nn.sigmoid(gate)
    silu = gate * sig
    activation = (silu * up).astype(bf16)
    expert_out = dot(activation, w_out).astype(bf16).astype(f32).reshape(16, CAP, width)
    mix_rows = mix_rows.astype(f32)
    slot_gate_grad = jnp.sum(expert_out * mix_rows, axis=2, keepdims=True)
    weighted = (slot_gates * expert_out).astype(bf16)
    route_grad = (slot_gates * mix_rows).astype(bf16).reshape(16 * CAP, width)
    activation_grad = einsum("rd,hd->rh", route_grad, w_out)
    pre_grad = jnp.concatenate(
        [activation_grad * up * sig * (1 + gate * (1 - sig)), activation_grad * silu], axis=1
    ).astype(bf16)
    grad_in = einsum("rd,rf->df", expert_rows, pre_grad)
    grad_out = einsum("rh,rd->hd", activation, route_grad)
    expert_grads = lax.psum(jnp.concatenate([grad_in, grad_out], axis=0).astype(bf16), "replica")
    row_grad = einsum("rf,df->rd", pre_grad, w_in).astype(bf16).reshape(16, CAP, width)
    returned = einsum(
        "srt,srd->std", pick_b, jnp.concatenate([weighted, row_grad], axis=2)
    ).astype(bf16)
    token_gate_grad = jnp.sum(jnp.where(pick, slot_gate_grad, 0.0), axis=1)
    upper, lower = split_two(token_gate_grad)
    side = jnp.concatenate(
        [jnp.pad(upper, ((0, 0), (0, 64))), jnp.pad(lower, ((0, 0), (0, 2048 - 448)))], axis=1
    )
    mine = (jnp.arange(E) == expert)[None, :, None]
    side = jnp.where(mine, side[:, None, :], 0).astype(bf16)
    back = scatter_rows(jnp.concatenate([returned, side], axis=1), 3, f32)

    output = (hidden_one + live * back[:rows, :width]).astype(bf16)
    gate_grad = (back[rows:, :rows] + back[rows:, 256 : 256 + rows]).T
    logit_grad = (gates * (gate_grad - jnp.sum(gates * gate_grad, axis=1, keepdims=True))).astype(
        bf16
    )
    normed_second_grad = back[:rows, width:] + einsum("te,de->td", logit_grad, full_router)
    d_router = einsum("td,te->de", normed_second, logit_grad)
    d_ffn_gain = jnp.sum(normed_second_grad * hidden_one * scale_second, axis=0)
    gained = normed_second_grad * gain_second
    hidden_grad = (
        upstream
        + scale_second * gained
        - hidden_one
        * scale_second**3
        * jnp.mean(gained * hidden_one, axis=1, keepdims=True)
    )
    attn_grad = (live * hidden_grad).astype(bf16)
    mixed_grad = einsum("td,cd->tc", attn_grad, full_output).astype(bf16)
    d_output = einsum("tc,td->cd", mixed, attn_grad).astype(bf16)
    mixed_grad = mixed_grad.reshape(rows, KEY_VALUE_HEADS, group, HEAD_SIZE)
    prob_grad = einsum("ehla,jha->hlej", mixed_grad, value)
    value_grad = einsum("uqeh,euqz->huz", attn_prob_b, mixed_grad).reshape(rows, -1).astype(bf16)
    row_dot = jnp.sum(attn_prob * prob_grad, axis=-1, keepdims=True)
    score_grad = (attn_prob * (prob_grad - row_dot)).astype(bf16)
    query_turned = einsum("pjwi,ipx->wpjx", score_grad, key).reshape(rows, -1) * scale
    key_turned = einsum("uqeh,euqz->huz", score_grad, query).reshape(rows, -1) * scale
    turned_back = rotate(
        jnp.concatenate([query_turned, key_turned], axis=1), cosine_table, -sine_table
    ).astype(bf16)
    qkv_grad = jnp.concatenate([turned_back, value_grad], axis=1)
    normed_first_grad = einsum("tc,dc->td", qkv_grad, w_qkv)
    d_qkv = einsum("td,tc->dc", normed_first, qkv_grad).astype(bf16)
    d_attn_gain = jnp.sum(normed_first_grad * inputs * scale_first, axis=0)
    gained = normed_first_grad * gain_first
    d_tokens = (
        hidden_grad
        + scale_first * gained
        - inputs * scale_first**3 * jnp.mean(gained * inputs, axis=1, keepdims=True)
    )
    share = w_query.shape[0]
    gains = jnp.concatenate([d_attn_gain, d_ffn_gain]).astype(bf16).reshape(share, -1)
    lanes = gains.shape[1]
    grads = jnp.concatenate(
        [
            d_qkv,
            d_output,
            d_router.astype(bf16),
            jnp.tile(gains, (16, 1)),
            jnp.zeros((1024, PACKED - 3072 - E - lanes), bf16),
        ],
        axis=1,
    )
    part = scatter_rows(grads.reshape(16, share, PACKED), 4, bf16)
    total = total_rows(part, 5).astype(f32)
    gains = total[:, 3072 + E : 3072 + E + lanes].reshape(2, width)
    expert_grads = expert_grads.astype(f32)
    return (
        output,
        d_tokens,
        gains[0],
        gains[1],
        total[:, :1024],
        total[:, 1024:1536],
        total[:, 1536:2048],
        total[:, 2048:3072],
        total[:, 3072 : 3072 + E],
        expert_grads[None, :width],
        expert_grads[None, width:],
    )


def solution(mesh):
    return jax.shard_map(
        local,
        mesh=mesh,
        in_specs=(
            P(("shard", "replica"), None),
            P(("shard", "replica"), None),
            P(("shard", "replica"), None),
            P(),
            P(),
            P("shard", None),
            P("shard", None),
            P("shard", None),
            P("shard", None),
            P("shard", None),
            P("shard", None, None),
            P("shard", None, None),
            P(("shard", "replica"), None),
        ),
        out_specs=(
            P(("shard", "replica"), None),
            P(("shard", "replica"), None),
            P(),
            P(),
            P("shard", None),
            P("shard", None),
            P("shard", None),
            P("shard", None),
            P("shard", None),
            P("shard", None, None),
            P("shard", None, None),
        ),
        check_vma=False,
    )
```

```python
import functools
import math

import jax
import jax.numpy as jnp
from jax import lax
from jax.experimental import pallas as pl
from jax.experimental.pallas import tpu as pltpu
from jax.sharding import PartitionSpec as P

QUERY_HEADS = 16
KEY_VALUE_HEADS = 8
HEAD_SIZE = 64
H = 512
E = 16
CAP = 120
PACKED = 3328

EPS = 1e-06
ROPE_BASE = 10000.0
NEGATIVE = -1e30

MESH = pl.DeviceIdType.MESH


def place():
    me = lax.axis_index("shard")
    rep = lax.axis_index("replica")
    core = lax.rem(me, 2)
    y = lax.rem(me // 2, 4)
    high = me // 8
    return me, rep, core, y, high


def index_of(high, y, core):
    return (high * 4 + lax.rem(y, 4)) * 2 + core


def greet(targets):
    barrier = pltpu.get_barrier_semaphore()
    for target in targets:
        pl.semaphore_signal(barrier, inc=1, device_id=target, device_id_type=MESH)
    pl.semaphore_wait(barrier, len(targets))


def gather_kernel(cut, block_ref, out_ref, local_sem, send_sem, recv_sem):
    me, rep, core, y, high = place()
    rows = block_ref.shape[0]
    mate = (index_of(high, y, 1 - core), rep)
    up = (index_of(high, y + 1, core), rep)
    down = (index_of(high, y + 3, core), rep)
    across = (index_of(1 - high, y, core), rep)
    greet([mate, up, down, across])
    top, low = pl.ds(0, cut), pl.ds(cut, rows - cut)

    def remote(number, source, slot, span, target):
        return pltpu.make_async_remote_copy(
            src_ref=source,
            dst_ref=out_ref.at[slot, span],
            send_sem=send_sem.at[number],
            recv_sem=recv_sem.at[number],
            device_id=target,
            device_id_type=MESH,
        )

    whole = pl.ds(0, rows)
    other = index_of(1 - high, y, core)
    from_down = index_of(high, y + 3, core)
    from_up = index_of(high, y + 1, core)
    far = index_of(high, y + 2, core)
    other_down = index_of(1 - high, y + 3, core)
    other_up = index_of(1 - high, y + 1, core)
    other_far = index_of(1 - high, y + 2, core)
    own_across = remote(0, block_ref, me, whole, across)
    own_up = remote(1, block_ref, me, whole, up)
    own_down = remote(2, block_ref, me, whole, down)
    own_mate = remote(3, block_ref, me, whole, mate)
    copies = [own_across, own_up, own_down, own_mate]
    for copy in copies:
        copy.start()
    local = pltpu.make_async_copy(block_ref, out_ref.at[me], local_sem)
    local.start()

    def onward(number, slot, span, target):
        copy = remote(number, out_ref.at[slot, span], slot, span, target)
        copy.start()
        copies.append(copy)
        return copy

    own_up.wait_recv()
    far_up = onward(4, from_down, top, up)
    own_down.wait_recv()
    far_down = onward(5, from_up, low, down)
    own_across.wait_recv()
    other_to_up = onward(6, other, whole, up)
    other_to_down = onward(7, other, whole, down)
    mates = [own_mate]
    mates.append(onward(8, from_down, whole, mate))
    mates.append(onward(9, from_up, whole, mate))
    mates.append(onward(10, other, whole, mate))
    other_to_up.wait_recv()
    other_far_up = onward(11, other_down, top, up)
    other_to_down.wait_recv()
    other_far_down = onward(12, other_up, low, down)
    mates.append(onward(13, other_down, whole, mate))
    mates.append(onward(14, other_up, whole, mate))
    far_up.wait_recv()
    mates.append(onward(15, far, top, mate))
    far_down.wait_recv()
    mates.append(onward(16, far, low, mate))
    other_far_up.wait_recv()
    mates.append(onward(17, other_far, top, mate))
    other_far_down.wait_recv()
    mates.append(onward(18, other_far, low, mate))
    for copy in mates:
        copy.wait_recv()
    for copy in copies:
        copy.wait_send()
    local.wait()


def gather_rows(block, collective_id):
    rows, width = block.shape
    cut = (rows // 16 + 1) // 2 * 16
    return pl.pallas_call(
        functools.partial(gather_kernel, cut),
        out_shape=jax.ShapeDtypeStruct((16, rows, width), block.dtype),
        in_specs=[pl.BlockSpec(memory_space=pl.ANY)],
        out_specs=pl.BlockSpec(memory_space=pl.ANY),
        scratch_shapes=[
            pltpu.SemaphoreType.DMA,
            pltpu.SemaphoreType.DMA((19,)),
            pltpu.SemaphoreType.DMA((19,)),
        ],
        compiler_params=pltpu.CompilerParams(collective_id=collective_id, has_side_effects=True),
        cost_estimate=pl.CostEstimate(
            flops=0, bytes_accessed=16 * rows * width * 2 * 8, transcendentals=0
        ),
    )(block)


def add_rows(target, source, start, count):
    def body(step, carry):
        at = pl.ds(pl.multiple_of(start + step * 16, 16), 16)
        here = pl.ds(pl.multiple_of(step * 16, 16), 16)
        target[at, :] = (
            target[at, :].astype(jnp.float32) + source[here, :].astype(jnp.float32)
        ).astype(target.dtype)
        return carry

    lax.fori_loop(0, count // 16, body, 0)


def scatter_kernel(
    cut, blocks_ref, out_ref, sums, mates, near_up, near_down, far_up, far_down, cross,
    local_sem, send_sem, recv_sem,
):
    me, rep, core, y, high = place()
    rows = out_ref.shape[0]
    mate = (index_of(high, y, 1 - core), rep)
    up = (index_of(high, y + 1, core), rep)
    down = (index_of(high, y + 3, core), rep)
    across = (index_of(1 - high, y, core), rep)
    greet([mate, up, down, across])

    def remote(number, source, target_ref, target):
        return pltpu.make_async_remote_copy(
            src_ref=source,
            dst_ref=target_ref,
            send_sem=send_sem.at[number],
            recv_sem=recv_sem.at[number],
            device_id=target,
            device_id_type=MESH,
        )

    order = [4, 5, 2, 3, 6, 7, 0, 1]
    locals_, swaps, sends = {}, {}, []
    for slot in order:
        d, o = slot // 2, slot % 2
        side = 1 - high if o == 0 else high
        swap = remote(slot, blocks_ref.at[index_of(side, y + d, 1 - core)], mates.at[slot], mate)
        swap.start()
        swaps[slot] = swap
        sends.append(swap)
        local = pltpu.make_async_copy(
            blocks_ref.at[index_of(side, y + d, core)], sums.at[slot], local_sem.at[slot]
        )
        local.start()
        locals_[slot] = local

    def settle(slot):
        locals_[slot].wait()
        swaps[slot].wait_recv()
        add_rows(sums.at[slot], mates.at[slot], 0, rows)

    top, low = pl.ds(0, cut), pl.ds(cut, rows - cut)
    firsts = []
    for o in range(2):
        settle(4 + o)
        one = remote(8 + o, sums.at[4 + o, top], far_up.at[o], up)
        two = remote(10 + o, sums.at[4 + o, low], far_down.at[o], down)
        one.start()
        two.start()
        firsts.append((one, two))
        sends += [one, two]
    seconds = []
    for o in range(2):
        settle(2 + o)
        settle(6 + o)
        one, two = firsts[o]
        one.wait_recv()
        add_rows(sums.at[2 + o], far_up.at[o], 0, cut)
        one = remote(12 + o, sums.at[2 + o], near_up.at[o], up)
        one.start()
        two.wait_recv()
        add_rows(sums.at[6 + o], far_down.at[o], cut, rows - cut)
        two = remote(14 + o, sums.at[6 + o], near_down.at[o], down)
        two.start()
        seconds.append((one, two))
        sends += [one, two]
    for o in range(2):
        settle(o)
        one, two = seconds[o]
        one.wait_recv()
        add_rows(sums.at[o], near_up.at[o], 0, rows)
        two.wait_recv()
        add_rows(sums.at[o], near_down.at[o], 0, rows)
        if o == 0:
            last = remote(16, sums.at[0], cross, across)
            last.start()
            sends.append(last)
    last.wait_recv()

    def body(step, carry):
        at = pl.ds(pl.multiple_of(step * 16, 16), 16)
        out_ref[at, :] = (
            sums[1, at, :].astype(jnp.float32) + cross[at, :].astype(jnp.float32)
        ).astype(out_ref.dtype)
        return carry

    lax.fori_loop(0, rows // 16, body, 0)
    for copy in sends:
        copy.wait_send()


def scatter_rows(blocks, collective_id, out_type):
    count, rows, width = blocks.shape
    cut = (rows // 16 + 1) // 2 * 16
    kind = blocks.dtype
    return pl.pallas_call(
        functools.partial(scatter_kernel, cut),
        out_shape=jax.ShapeDtypeStruct((rows, width), out_type),
        in_specs=[pl.BlockSpec(memory_space=pl.ANY)],
        out_specs=pl.BlockSpec(memory_space=pltpu.VMEM),
        scratch_shapes=[
            pltpu.VMEM((8, rows, width), kind),
            pltpu.VMEM((8, rows, width), kind),
            pltpu.VMEM((2, rows, width), kind),
            pltpu.VMEM((2, rows, width), kind),
            pltpu.VMEM((2, cut, width), kind),
            pltpu.VMEM((2, rows - cut, width), kind),
            pltpu.VMEM((rows, width), kind),
            pltpu.SemaphoreType.DMA((8,)),
            pltpu.SemaphoreType.DMA((17,)),
            pltpu.SemaphoreType.DMA((17,)),
        ],
        compiler_params=pltpu.CompilerParams(
            collective_id=collective_id, has_side_effects=True, vmem_limit_bytes=40 * 1024 * 1024
        ),
        cost_estimate=pl.CostEstimate(
            flops=0, bytes_accessed=16 * rows * width * 2 * 8, transcendentals=0
        ),
    )(blocks)


def total_kernel(part_ref, out_ref, pieces, send_sem, recv_sem, send_back, recv_back):
    shard = lax.axis_index("shard")
    me = lax.axis_index("replica")
    rows, width = part_ref.shape
    others = [(shard, lax.rem(me + step, 8)) for step in range(1, 8)]
    greet(others)

    def piece(ref, which):
        half = width // 2
        return ref.at[
            pl.ds(pl.multiple_of((which // 2) * 16, 16), 16),
            pl.ds(pl.multiple_of(lax.rem(which, 2) * half, 128), half),
        ]

    firsts = []
    for step in range(1, 8):
        target = lax.rem(me + step, 8)
        copy = pltpu.make_async_remote_copy(
            src_ref=piece(part_ref, target),
            dst_ref=pieces.at[step - 1],
            send_sem=send_sem.at[step - 1],
            recv_sem=recv_sem.at[step - 1],
            device_id=(shard, target),
            device_id_type=MESH,
        )
        copy.start()
        firsts.append(copy)
    total = piece(part_ref, me)[...].astype(jnp.float32)
    for step in range(1, 8):
        firsts[step - 1].wait_recv()
        total = total + pieces[step - 1].astype(jnp.float32)
    piece(out_ref, me)[...] = total.astype(out_ref.dtype)
    seconds = []
    for step in range(1, 8):
        target = lax.rem(me + step, 8)
        copy = pltpu.make_async_remote_copy(
            src_ref=piece(out_ref, me),
            dst_ref=piece(out_ref, me),
            send_sem=send_back.at[step - 1],
            recv_sem=recv_back.at[step - 1],
            device_id=(shard, target),
            device_id_type=MESH,
        )
        copy.start()
        seconds.append(copy)
    for copy in seconds:
        copy.wait_recv()
    for copy in firsts + seconds:
        copy.wait_send()


def total_rows(part, collective_id):
    rows, width = part.shape
    return pl.pallas_call(
        total_kernel,
        out_shape=jax.ShapeDtypeStruct((rows, width), part.dtype),
        in_specs=[pl.BlockSpec(memory_space=pltpu.VMEM)],
        out_specs=pl.BlockSpec(memory_space=pltpu.VMEM),
        scratch_shapes=[
            pltpu.VMEM((7, 16, width // 2), part.dtype),
            pltpu.SemaphoreType.DMA((7,)),
            pltpu.SemaphoreType.DMA((7,)),
            pltpu.SemaphoreType.DMA((7,)),
            pltpu.SemaphoreType.DMA((7,)),
        ],
        compiler_params=pltpu.CompilerParams(collective_id=collective_id, has_side_effects=True),
    )(part)


def contract(a, b, left, right):
    return lax.dot_general(
        a, b, (((left,), (right,)), ((), ())), preferred_element_type=jnp.float32
    )


UP_OF_STEP = (0, 3, 1, 0, 2, 3, 1, 2)
SIDE_OF_STEP = (0, 0, 0, 1, 0, 1, 1, 1)
SLOTS = 128


def select(table, step):
    value = jnp.int32(table[0])
    for place in range(1, len(table)):
        if table[place] != table[place - 1]:
            value = value + (table[place] - table[place - 1]) * jnp.minimum(
                jnp.maximum(step - (place - 1), 0), 1
            )
    return value


def expert_kernel(
    cut, payload_ref, mix_ref, w_in_ref, w_out_ref, back_ref, mixture_ref, grads_ref,
    arrived, mix_buf, w_in, w_out, blocks, weighted, rows_c, act_c, route_c, pre_c, mix_c, row_c,
    near_mate, near_up, near_down, far_up, far_down, cross,
    b_mate, b_near_up, b_near_down, b_far_up, b_far_down, b_cross,
    local_sem, mix_sem, send_sem, recv_sem, a_send, a_recv, b_send, b_recv,
):
    me, rep, core, y, high = place()
    width = payload_ref.shape[1]
    rows = payload_ref.shape[0]
    tokens = rows - 16
    mate = (index_of(high, y, 1 - core), rep)
    up = (index_of(high, y + 1, core), rep)
    down = (index_of(high, y + 3, core), rep)
    across = (index_of(1 - high, y, core), rep)

    def chip_of(step):
        side, turn = select(SIDE_OF_STEP, step), select(UP_OF_STEP, step)
        return lax.rem(high + side, 2) * 4 + lax.rem(y + turn, 4)

    load_in = pltpu.make_async_copy(w_in_ref, w_in, local_sem.at[0])
    load_out = pltpu.make_async_copy(w_out_ref, w_out, local_sem.at[1])
    load_own = pltpu.make_async_copy(payload_ref, arrived.at[me], local_sem.at[2])
    load_in.start()
    load_out.start()
    load_own.start()

    def load_mix(step):
        slot = lax.rem(step, 2)
        return pltpu.make_async_copy(
            mix_ref.at[pl.ds(chip_of(step) * 2, 2)], mix_buf.at[slot], mix_sem.at[slot]
        )

    load_mix(0).start()
    greet([mate, up, down, across])
    whole, top, low = pl.ds(0, rows), pl.ds(0, cut), pl.ds(cut, rows - cut)
    other = index_of(1 - high, y, core)
    from_down = index_of(high, y + 3, core)
    from_up = index_of(high, y + 1, core)
    far = index_of(high, y + 2, core)
    other_down = index_of(1 - high, y + 3, core)
    other_up = index_of(1 - high, y + 1, core)
    other_far = index_of(1 - high, y + 2, core)
    plan = {
        0: (me, whole, across),
        1: (me, whole, up),
        2: (me, whole, down),
        3: (me, whole, mate),
        4: (from_down, top, up),
        5: (from_up, low, down),
        6: (other, whole, up),
        7: (other, whole, down),
        8: (from_down, whole, mate),
        9: (from_up, whole, mate),
        10: (other, whole, mate),
        11: (other_down, top, up),
        12: (other_up, low, down),
        13: (other_down, whole, mate),
        14: (other_up, whole, mate),
        15: (far, top, mate),
        16: (far, low, mate),
        17: (other_far, top, mate),
        18: (other_far, low, mate),
    }

    def move(number):
        slot, span, target = plan[number]
        source = payload_ref if number < 4 else arrived.at[slot, span]
        return pltpu.make_async_remote_copy(
            src_ref=source,
            dst_ref=arrived.at[slot, span],
            send_sem=send_sem.at[number],
            recv_sem=recv_sem.at[number],
            device_id=target,
            device_id_type=MESH,
        )

    for number in range(4):
        move(number).start()
    load_in.wait()
    load_out.wait()
    load_own.wait()

    def picks(slot):
        side = arrived[slot, pl.ds(tokens, 16), :].astype(jnp.float32)
        line = lax.broadcasted_iota(jnp.int32, side.shape, 0)
        own = jnp.sum(jnp.where(line == me, side, 0.0), axis=0, keepdims=True)
        gates = own[:, :tokens] + own[:, 256 : 256 + tokens]
        place_of = own[:, 512 : 512 + tokens].astype(jnp.int32)
        pick = place_of == lax.broadcasted_iota(jnp.int32, (SLOTS, tokens), 0)
        return pick, gates

    def swap(step, source, buffer, sems):
        return pltpu.make_async_remote_copy(
            src_ref=source.at[2 * chip_of(step) + 1 - core],
            dst_ref=buffer.at[step],
            send_sem=sems[0].at[step],
            recv_sem=sems[1].at[step],
            device_id=mate,
            device_id_type=MESH,
        )

    def work(step, carry):
        @pl.when(step == 0)
        def _():
            move(3).wait_recv()

        @pl.when(step == 1)
        def _():
            move(1).wait_recv()
            move(4).start()
            move(8).start()
            move(2).wait_recv()
            move(5).start()
            move(9).start()
            move(0).wait_recv()
            for number in (6, 7, 10):
                move(number).start()
            move(8).wait_recv()

        @pl.when(step == 2)
        def _():
            move(9).wait_recv()

        @pl.when(step == 3)
        def _():
            move(10).wait_recv()

        @pl.when(step == 4)
        def _():
            move(6).wait_recv()
            move(11).start()
            move(13).start()
            move(7).wait_recv()
            move(12).start()
            move(14).start()
            move(4).wait_recv()
            move(15).start()
            move(5).wait_recv()
            move(16).start()
            move(15).wait_recv()
            move(16).wait_recv()

        @pl.when(step == 5)
        def _():
            move(13).wait_recv()

        @pl.when(step == 6)
        def _():
            move(14).wait_recv()

        @pl.when(step == 7)
        def _():
            move(11).wait_recv()
            move(17).start()
            move(12).wait_recv()
            move(18).start()
            move(17).wait_recv()
            move(18).wait_recv()

        @pl.when(step < 7)
        def _():
            load_mix(step + 1).start()

        load_mix(step).wait()
        buffer = lax.rem(step, 2)
        base = chip_of(step) * 2
        both = 2 * SLOTS
        at = pl.ds(pl.multiple_of(chip_of(step) * both, both), both)
        kept = []
        for b in range(2):
            pick, gates = picks(base + b)
            pick_b = pick.astype(jnp.bfloat16)
            slot_gates = jnp.sum(jnp.where(pick, gates, 0.0), axis=1, keepdims=True)
            here = pl.ds(b * SLOTS, SLOTS)
            there = pl.ds(pl.multiple_of(chip_of(step) * both + b * SLOTS, SLOTS), SLOTS)
            rows_c[there, :] = contract(
                pick_b, arrived[base + b, pl.ds(0, tokens), :], 1, 0
            ).astype(jnp.bfloat16)
            mix_rows = contract(pick_b, mix_buf[buffer, b], 1, 0)
            mix_c[here, :] = mix_rows.astype(jnp.bfloat16)
            route_c[there, :] = (slot_gates * mix_rows).astype(jnp.bfloat16)
            kept.append((pick, pick_b, slot_gates))
        slot_gates = jnp.concatenate([kept[0][2], kept[1][2]], axis=0)
        x, route = rows_c[at, :], route_c[at, :]

        def inner(tile, carry):
            left = pl.ds(pl.multiple_of(tile * 256, 256), 256)
            right = pl.ds(pl.multiple_of(512 + tile * 256, 256), 256)
            gate = contract(x, w_in[:, left], 1, 0)
            raised = contract(x, w_in[:, right], 1, 0)
            grad = contract(route, w_out[left, :], 1, 1)
            sig = 1.0 / (1.0 + jnp.exp(-gate))
            silu = gate * sig
            act_c[at, left] = (silu * raised).astype(jnp.bfloat16)
            pre_c[at, left] = (grad * raised * sig * (1.0 + gate * (1.0 - sig))).astype(
                jnp.bfloat16
            )
            pre_c[at, right] = (grad * silu).astype(jnp.bfloat16)
            return carry

        lax.fori_loop(0, 2, inner, 0)
        act, pre = act_c[at, :], pre_c[at, :]

        def outer(tile, total):
            span = pl.ds(pl.multiple_of(tile * 256, 256), 256)
            result = contract(act, w_out[:, span], 1, 0).astype(jnp.bfloat16).astype(jnp.float32)
            weighted[at, span] = (slot_gates * result).astype(jnp.bfloat16)
            row_c[:, span] = contract(pre, w_in[span, :], 1, 1).astype(jnp.bfloat16)
            return total + jnp.sum(
                result * mix_c[:, span].astype(jnp.float32), axis=1, keepdims=True
            )

        gate_grad = lax.fori_loop(0, 4, outer, jnp.zeros((both, 1), jnp.float32))
        for b in range(2):
            pick, pick_b, _ = kept[b]
            here = pl.ds(b * SLOTS, SLOTS)
            blocks[base + b, pl.ds(0, tokens), :] = contract(pick_b, row_c[here, :], 0, 0).astype(
                jnp.bfloat16
            )
            line_grad = jnp.sum(
                jnp.where(pick, gate_grad[b * SLOTS : (b + 1) * SLOTS], 0.0), axis=0, keepdims=True
            )
            upper = line_grad.astype(jnp.bfloat16).astype(jnp.float32)
            mine = lax.broadcasted_iota(jnp.int32, (16, tokens), 0) == me
            tail = pl.ds(tokens, 16)
            blocks[base + b, tail, :] = jnp.zeros((16, width), jnp.bfloat16)
            blocks[base + b, tail, pl.ds(0, tokens)] = jnp.where(mine, upper, 0.0).astype(
                jnp.bfloat16
            )
            blocks[base + b, tail, pl.ds(256, tokens)] = jnp.where(
                mine, line_grad - upper, 0.0
            ).astype(jnp.bfloat16)
        swap(step, blocks, near_mate, (a_send, a_recv)).start()
        return carry

    lax.fori_loop(0, 8, work, 0)
    for number in range(19):
        move(number).wait_send()

    class Sum:
        def __init__(self, source, bufs, sems, count, split):
            self.source, self.bufs, self.sems = source, bufs, sems
            self.count, self.split = count, split
            self.pending = {}

        def block(self, step):
            return self.source.at[2 * chip_of(jnp.int32(step)) + core]

        def settle(self, step):
            swap(jnp.int32(step), self.source, self.bufs[0], self.sems).wait_recv()
            add_rows(self.block(step), self.bufs[0].at[step], 0, self.count)

        def send(self, number, source, target_ref, target):
            copy = pltpu.make_async_remote_copy(
                src_ref=source,
                dst_ref=target_ref,
                send_sem=self.sems[0].at[number],
                recv_sem=self.sems[1].at[number],
                device_id=target,
                device_id_type=MESH,
            )
            copy.start()
            self.pending[number] = copy

        def first(self, o):
            step = (7, 4)[o]
            self.settle(step)
            block = self.block(step)
            spans = pl.ds(0, self.split), pl.ds(self.split, self.count - self.split)
            self.send(8 + o, block.at[spans[0]], self.bufs[3].at[o], up)
            self.send(10 + o, block.at[spans[1]], self.bufs[4].at[o], down)

        def second(self, o):
            above, below = (6, 2)[o], (5, 1)[o]
            self.settle(above)
            self.settle(below)
            self.pending[8 + o].wait_recv()
            add_rows(self.block(above), self.bufs[3].at[o], 0, self.split)
            self.send(12 + o, self.block(above), self.bufs[1].at[o], up)
            self.pending[10 + o].wait_recv()
            add_rows(self.block(below), self.bufs[4].at[o], self.split, self.count - self.split)
            self.send(14 + o, self.block(below), self.bufs[2].at[o], down)

        def third(self, o):
            step = (3, 0)[o]
            self.settle(step)
            self.pending[12 + o].wait_recv()
            add_rows(self.block(step), self.bufs[1].at[o], 0, self.count)
            self.pending[14 + o].wait_recv()
            add_rows(self.block(step), self.bufs[2].at[o], 0, self.count)
            if o == 0:
                self.send(16, self.block(step), self.bufs[5], across)

        def last(self, out_ref):
            self.pending[16].wait_recv()
            own, beside = self.block(0), self.bufs[5]

            def body(step, carry):
                span = pl.ds(pl.multiple_of(step * 16, 16), 16)
                out_ref[span, :] = own[span, :].astype(jnp.float32) + beside[span, :].astype(
                    jnp.float32
                )
                return carry

            lax.fori_loop(0, self.count // 16, body, 0)

        def finish(self):
            for step in range(8):
                swap(jnp.int32(step), self.source, self.bufs[0], self.sems).wait_send()
            for copy in self.pending.values():
                copy.wait_send()

    a = Sum(
        blocks, (near_mate, near_up, near_down, far_up, far_down, cross), (a_send, a_recv),
        rows, cut,
    )
    mixes = arrived.at[:, pl.ds(0, tokens)]
    b = Sum(
        mixes, (b_mate, b_near_up, b_near_down, b_far_up, b_far_down, b_cross), (b_send, b_recv),
        tokens, 96,
    )
    a.first(0)
    a.first(1)

    def spread(turn, carry):
        step = 7 - turn
        for b in range(2):
            slot = chip_of(step) * 2 + b
            pick, _ = picks(slot)
            here = pl.ds(pl.multiple_of(slot * SLOTS, SLOTS), SLOTS)
            arrived[slot, pl.ds(0, tokens), :] = contract(
                pick.astype(jnp.bfloat16), weighted[here, :], 0, 0
            ).astype(jnp.bfloat16)
        swap(step, mixes, b_mate, (b_send, b_recv)).start()
        return carry

    lax.fori_loop(0, 8, spread, 0)
    a.second(0)
    a.second(1)

    def grad_in(tile, carry):
        span = pl.ds(pl.multiple_of(tile * 256, 256), 256)
        grads_ref[span, :] = contract(rows_c[:, span], pre_c[...], 0, 0).astype(jnp.bfloat16)
        return carry

    def grad_out(tile, carry):
        span = pl.ds(pl.multiple_of(tile * 256, 256), 256)
        there = pl.ds(pl.multiple_of(width + tile * 256, 256), 256)
        grads_ref[there, :] = contract(act_c[:, span], route_c[...], 0, 0).astype(jnp.bfloat16)
        return carry

    b.first(0)
    b.first(1)
    lax.fori_loop(0, 2, grad_in, 0)
    a.third(0)
    a.third(1)
    b.second(0)
    lax.fori_loop(2, 4, grad_in, 0)
    b.second(1)
    a.last(back_ref)
    lax.fori_loop(0, 2, grad_out, 0)
    b.third(0)
    b.third(1)
    b.last(mixture_ref)
    a.finish()
    b.finish()


def expert_layer(payload, mix, w_in, w_out, collective_id):
    rows, width = payload.shape
    tokens = rows - 16
    hidden = w_out.shape[0]
    cut = (rows // 16 + 1) // 2 * 16
    half = 96
    kind = jnp.bfloat16
    slots = 16 * SLOTS
    dma = pltpu.SemaphoreType.DMA

    def sums(count, split):
        return [
            pltpu.VMEM((8, count, width), kind),
            pltpu.VMEM((2, count, width), kind),
            pltpu.VMEM((2, count, width), kind),
            pltpu.VMEM((2, split, width), kind),
            pltpu.VMEM((2, count - split, width), kind),
            pltpu.VMEM((count, width), kind),
        ]

    return pl.pallas_call(
        functools.partial(expert_kernel, cut),
        out_shape=(
            jax.ShapeDtypeStruct((rows, width), jnp.float32),
            jax.ShapeDtypeStruct((tokens, width), jnp.float32),
            jax.ShapeDtypeStruct((width + hidden, width), kind),
        ),
        in_specs=[
            pl.BlockSpec(memory_space=pltpu.VMEM),
            pl.BlockSpec(memory_space=pl.ANY),
            pl.BlockSpec(memory_space=pl.ANY),
            pl.BlockSpec(memory_space=pl.ANY),
        ],
        out_specs=(
            pl.BlockSpec(memory_space=pltpu.VMEM),
            pl.BlockSpec(memory_space=pltpu.VMEM),
            pl.BlockSpec(memory_space=pltpu.VMEM),
        ),
        scratch_shapes=[
            pltpu.VMEM((16, rows, width), kind),
            pltpu.VMEM((2, 2, tokens, width), kind),
            pltpu.VMEM((width, 2 * hidden), kind),
            pltpu.VMEM((hidden, width), kind),
            pltpu.VMEM((16, rows, width), kind),
            pltpu.VMEM((slots, width), kind),
            pltpu.VMEM((slots, width), kind),
            pltpu.VMEM((slots, hidden), kind),
            pltpu.VMEM((slots, width), kind),
            pltpu.VMEM((slots, 2 * hidden), kind),
            pltpu.VMEM((2 * SLOTS, width), kind),
            pltpu.VMEM((2 * SLOTS, width), kind),
            *sums(rows, cut),
            *sums(tokens, half),
            dma((3,)),
            dma((2,)),
            dma((19,)),
            dma((19,)),
            dma((17,)),
            dma((17,)),
            dma((17,)),
            dma((17,)),
        ],
        compiler_params=pltpu.CompilerParams(
            collective_id=collective_id, has_side_effects=True, vmem_limit_bytes=60 * 1024 * 1024
        ),
        cost_estimate=pl.CostEstimate(
            flops=24 * 10**9, bytes_accessed=10**8, transcendentals=10**6
        ),
    )(payload, mix, w_in, w_out)


def heads_first(rows, width):
    return rows.reshape(rows.shape[0], -1, width)


def rotate(value_rows, cosine_table, sine_table):
    count = value_rows.shape[0]
    halves = value_rows.reshape(count, -1, 2, HEAD_SIZE // 2)
    first, second = halves[:, :, 0], halves[:, :, 1]
    cos_rows, sin_rows = cosine_table[:, None, :], sine_table[:, None, :]
    turned = jnp.stack(
        [first * cos_rows - second * sin_rows, second * cos_rows + first * sin_rows], axis=2
    )
    return turned.reshape(count, -1)


def dot(a, b):
    return jnp.dot(a, b, preferred_element_type=jnp.float32)


def einsum(form, a, b):
    return jnp.einsum(form, a, b, preferred_element_type=jnp.float32)


def split_two(values):
    upper = values.astype(jnp.bfloat16)
    return upper, (values - upper.astype(jnp.float32)).astype(jnp.bfloat16)


def local(
    tokens,
    seq_lengths,
    routes,
    attn_gain,
    ffn_gain,
    w_query,
    key_projection,
    value_projection,
    w_output,
    w_router,
    w_in,
    w_out,
    cotangent,
):
    rows, width = tokens.shape
    group = QUERY_HEADS // KEY_VALUE_HEADS
    scale = HEAD_SIZE ** (-0.5)
    w_in, w_out = w_in[0], w_out[0]
    bf16, f32 = jnp.bfloat16, jnp.float32

    lengths = seq_lengths[0]
    row_index = jnp.arange(rows, dtype=jnp.int32)
    first_len, total_len = lengths[0], lengths[0] + lengths[1]
    doc = jnp.where(row_index < first_len, 0, jnp.where(row_index < total_len, 1, 2))
    start = jnp.where(
        row_index < first_len, 0, jnp.where(row_index < total_len, first_len, total_len)
    )
    allowed = (doc[:, None] == doc[None, :]) & (row_index[None, :] <= row_index[:, None])
    live = (row_index < total_len).astype(f32)[:, None]
    frequency = jnp.exp(
        jnp.arange(HEAD_SIZE // 2, dtype=f32) * (-2.0 * math.log(ROPE_BASE) / HEAD_SIZE)
    )
    angles = (row_index - start).astype(f32)[:, None] * frequency[None, :]
    cosine_table, sine_table = jnp.cos(angles), jnp.sin(angles)
    gain_first, gain_second = attn_gain.astype(f32), ffn_gain.astype(f32)

    packed = jnp.concatenate(
        [
            w_query,
            key_projection,
            value_projection,
            w_output,
            w_router,
            jnp.zeros((w_query.shape[0], PACKED - 3072 - E), bf16),
        ],
        axis=1,
    )
    weights = gather_rows(packed, 1).reshape(-1, PACKED)
    upstream = cotangent.astype(f32)
    mix_grad = (cotangent * live.astype(bf16)).astype(bf16)
    all_mix_grad = lax.all_gather(mix_grad, "shard", axis=0)

    inputs = tokens.astype(f32)
    scale_first = lax.rsqrt(jnp.mean(inputs * inputs, axis=1, keepdims=True) + EPS)
    normed_first = (inputs * scale_first * gain_first).astype(bf16)
    w_qkv, full_output, full_router = (
        weights[:, :2048],
        weights[:, 2048:3072],
        weights[:, 3072 : 3072 + E],
    )
    qkv = dot(normed_first, w_qkv)
    turned = rotate(qkv[:, :1536], cosine_table, sine_table).astype(bf16)
    query = turned[:, :1024].reshape(rows, KEY_VALUE_HEADS, group, HEAD_SIZE)
    key = turned[:, 1024:].reshape(rows, KEY_VALUE_HEADS, HEAD_SIZE)
    value = qkv[:, 1536:].astype(bf16).reshape(rows, KEY_VALUE_HEADS, HEAD_SIZE)
    scores = jnp.where(allowed, einsum("ehla,jha->hlej", query, key) * scale, NEGATIVE)
    largest = jnp.max(scores, axis=-1, keepdims=True)
    raised = jnp.exp(scores - largest)
    attn_prob = raised / jnp.sum(raised, axis=-1, keepdims=True)
    attn_prob_b = attn_prob.astype(bf16)
    mixed = einsum("pjwi,ipx->wpjx", attn_prob_b, value).reshape(rows, -1).astype(bf16)
    hidden_one = inputs + live * dot(mixed, full_output)
    scale_second = lax.rsqrt(jnp.mean(hidden_one * hidden_one, axis=1, keepdims=True) + EPS)
    normed_second = (hidden_one * scale_second * gain_second).astype(bf16)
    logits = dot(normed_second, full_router)
    named = jnp.any(routes[:, :, None] == jnp.arange(E, dtype=jnp.int32), axis=1)
    logits = jnp.where(named, logits, NEGATIVE)
    raised = jnp.exp(logits - jnp.max(logits, axis=1, keepdims=True))
    gates = raised / jnp.sum(raised, axis=1, keepdims=True)

    earlier = (row_index[:, None] > row_index[None, :]).astype(bf16)
    rank = dot(earlier, named.astype(bf16))
    place_of = jnp.where(named, rank, -1.0).T.astype(bf16)
    upper, lower = split_two(gates.T)
    gap = jnp.zeros((E, 64), bf16)
    side = jnp.concatenate(
        [upper, gap, lower, gap, place_of, jnp.zeros((E, width - 512 - rows), bf16)], axis=1
    )
    payload = jnp.concatenate([normed_second, side], axis=0)
    back, mixture, expert_grads = expert_layer(payload, all_mix_grad, w_in, w_out, 2)
    expert_grads = lax.psum(expert_grads, "replica")

    output = (hidden_one + live * mixture).astype(bf16)
    gate_grad = (back[rows:, :rows] + back[rows:, 256 : 256 + rows]).T
    logit_grad = (gates * (gate_grad - jnp.sum(gates * gate_grad, axis=1, keepdims=True))).astype(
        bf16
    )
    normed_second_grad = back[:rows] + einsum("te,de->td", logit_grad, full_router)
    d_router = einsum("td,te->de", normed_second, logit_grad)
    d_ffn_gain = jnp.sum(normed_second_grad * hidden_one * scale_second, axis=0)
    gained = normed_second_grad * gain_second
    hidden_grad = (
        upstream
        + scale_second * gained
        - hidden_one
        * scale_second**3
        * jnp.mean(gained * hidden_one, axis=1, keepdims=True)
    )
    attn_grad = (live * hidden_grad).astype(bf16)
    mixed_grad = einsum("td,cd->tc", attn_grad, full_output).astype(bf16)
    d_output = einsum("tc,td->cd", mixed, attn_grad).astype(bf16)
    mixed_grad = mixed_grad.reshape(rows, KEY_VALUE_HEADS, group, HEAD_SIZE)
    prob_grad = einsum("ehla,jha->hlej", mixed_grad, value)
    value_grad = einsum("uqeh,euqz->huz", attn_prob_b, mixed_grad).reshape(rows, -1).astype(bf16)
    row_dot = jnp.sum(attn_prob * prob_grad, axis=-1, keepdims=True)
    score_grad = (attn_prob * (prob_grad - row_dot)).astype(bf16)
    query_turned = einsum("pjwi,ipx->wpjx", score_grad, key).reshape(rows, -1) * scale
    key_turned = einsum("uqeh,euqz->huz", score_grad, query).reshape(rows, -1) * scale
    turned_back = rotate(
        jnp.concatenate([query_turned, key_turned], axis=1), cosine_table, -sine_table
    ).astype(bf16)
    qkv_grad = jnp.concatenate([turned_back, value_grad], axis=1)
    normed_first_grad = einsum("tc,dc->td", qkv_grad, w_qkv)
    d_qkv = einsum("td,tc->dc", normed_first, qkv_grad).astype(bf16)
    d_attn_gain = jnp.sum(normed_first_grad * inputs * scale_first, axis=0)
    gained = normed_first_grad * gain_first
    d_tokens = (
        hidden_grad
        + scale_first * gained
        - inputs * scale_first**3 * jnp.mean(gained * inputs, axis=1, keepdims=True)
    )
    share = w_query.shape[0]
    gains = jnp.concatenate([d_attn_gain, d_ffn_gain]).astype(bf16).reshape(share, -1)
    lanes = gains.shape[1]
    grads = jnp.concatenate(
        [
            d_qkv,
            d_output,
            d_router.astype(bf16),
            jnp.tile(gains, (16, 1)),
            jnp.zeros((1024, PACKED - 3072 - E - lanes), bf16),
        ],
        axis=1,
    )
    part = scatter_rows(grads.reshape(16, share, PACKED), 4, bf16)
    total = total_rows(part, 5).astype(f32)
    gains = total[:, 3072 + E : 3072 + E + lanes].reshape(2, width)
    expert_grads = expert_grads.astype(f32)
    return (
        output,
        d_tokens,
        gains[0],
        gains[1],
        total[:, :1024],
        total[:, 1024:1536],
        total[:, 1536:2048],
        total[:, 2048:3072],
        total[:, 3072 : 3072 + E],
        expert_grads[None, :width],
        expert_grads[None, width:],
    )


def solution(mesh):
    return jax.shard_map(
        local,
        mesh=mesh,
        in_specs=(
            P(("shard", "replica"), None),
            P(("shard", "replica"), None),
            P(("shard", "replica"), None),
            P(),
            P(),
            P("shard", None),
            P("shard", None),
            P("shard", None),
            P("shard", None),
            P("shard", None),
            P("shard", None, None),
            P("shard", None, None),
            P(("shard", "replica"), None),
        ),
        out_specs=(
            P(("shard", "replica"), None),
            P(("shard", "replica"), None),
            P(),
            P(),
            P("shard", None),
            P("shard", None),
            P("shard", None),
            P("shard", None),
            P("shard", None),
            P("shard", None, None),
            P("shard", None, None),
        ),
        check_vma=False,
    )
```

```python
import functools
import math

import jax
import jax.numpy as jnp
from jax import lax
from jax.experimental import pallas as pl
from jax.experimental.pallas import tpu as pltpu
from jax.sharding import PartitionSpec as P

QUERY_HEADS = 16
KEY_VALUE_HEADS = 8
HEAD_SIZE = 64
H = 512
E = 16
CAP = 120

EPS = 1e-06
ROPE_BASE = 10000.0
NEGATIVE = -1e30

MESH = pl.DeviceIdType.MESH


def place():
    me = lax.axis_index("shard")
    rep = lax.axis_index("replica")
    core = lax.rem(me, 2)
    y = lax.rem(me // 2, 4)
    high = me // 8
    return me, rep, core, y, high


def index_of(high, y, core):
    return (high * 4 + lax.rem(y, 4)) * 2 + core


def greet(targets):
    barrier = pltpu.get_barrier_semaphore()
    for target in targets:
        pl.semaphore_signal(barrier, inc=1, device_id=target, device_id_type=MESH)
    pl.semaphore_wait(barrier, len(targets))


def add_rows(target, source, start, count):
    def body(step, carry):
        at = pl.ds(pl.multiple_of(start + step * 16, 16), 16)
        here = pl.ds(pl.multiple_of(step * 16, 16), 16)
        target[at, :] = (
            target[at, :].astype(jnp.float32) + source[here, :].astype(jnp.float32)
        ).astype(target.dtype)
        return carry

    lax.fori_loop(0, count // 16, body, 0)


def contract(a, b, left, right):
    return lax.dot_general(
        a, b, (((left,), (right,)), ((), ())), preferred_element_type=jnp.float32
    )


UP_OF_STEP = (0, 3, 1, 0, 2, 3, 1, 2)
SIDE_OF_STEP = (0, 0, 0, 1, 0, 1, 1, 1)
SLOTS = 128


def select(table, step):
    value = jnp.int32(table[0])
    for place in range(1, len(table)):
        if table[place] != table[place - 1]:
            value = value + (table[place] - table[place - 1]) * jnp.minimum(
                jnp.maximum(step - (place - 1), 0), 1
            )
    return value


def expert_kernel(
    cut, payload_ref, mix_ref, w_in_ref, w_out_ref, back_ref, mixture_ref, grads_ref,
    arrived, mix_buf, w_in, w_out, blocks, weighted, rows_c, act_c, route_c, pre_c, mix_c, row_c,
    near_mate, near_up, near_down, far_up, far_down, cross,
    a_send, a_recv, local_sem, mix_sem, store_sem, send_sem, recv_sem,
):
    me, rep, core, y, high = place()
    width = payload_ref.shape[1]
    rows = payload_ref.shape[0]
    tokens = rows - 16
    mate = (index_of(high, y, 1 - core), rep)
    up = (index_of(high, y + 1, core), rep)
    down = (index_of(high, y + 3, core), rep)
    across = (index_of(1 - high, y, core), rep)

    load_in = pltpu.make_async_copy(w_in_ref, w_in, local_sem.at[0])
    load_out = pltpu.make_async_copy(w_out_ref, w_out, local_sem.at[1])
    load_own = pltpu.make_async_copy(payload_ref, arrived.at[me], local_sem.at[2])
    load_in.start()
    load_out.start()
    load_own.start()

    def load_mix(step):
        slot = lax.rem(step, 2)
        return pltpu.make_async_copy(
            mix_ref.at[pl.ds(chip_of(step) * 2, 2)], mix_buf.at[slot], mix_sem.at[slot]
        )

    load_mix(0).start()
    greet([mate, up, down, across])
    whole, top, low = pl.ds(0, rows), pl.ds(0, cut), pl.ds(cut, rows - cut)
    other = index_of(1 - high, y, core)
    from_down = index_of(high, y + 3, core)
    from_up = index_of(high, y + 1, core)
    far = index_of(high, y + 2, core)
    other_down = index_of(1 - high, y + 3, core)
    other_up = index_of(1 - high, y + 1, core)
    other_far = index_of(1 - high, y + 2, core)
    plan = {
        0: (me, whole, across),
        1: (me, whole, up),
        2: (me, whole, down),
        3: (me, whole, mate),
        4: (from_down, top, up),
        5: (from_up, low, down),
        6: (other, whole, up),
        7: (other, whole, down),
        8: (from_down, whole, mate),
        9: (from_up, whole, mate),
        10: (other, whole, mate),
        11: (other_down, top, up),
        12: (other_up, low, down),
        13: (other_down, whole, mate),
        14: (other_up, whole, mate),
        15: (far, top, mate),
        16: (far, low, mate),
        17: (other_far, top, mate),
        18: (other_far, low, mate),
    }

    def move(number):
        slot, span, target = plan[number]
        source = payload_ref if number < 4 else arrived.at[slot, span]
        return pltpu.make_async_remote_copy(
            src_ref=source,
            dst_ref=arrived.at[slot, span],
            send_sem=send_sem.at[number],
            recv_sem=recv_sem.at[number],
            device_id=target,
            device_id_type=MESH,
        )

    for number in range(4):
        move(number).start()
    load_in.wait()
    load_out.wait()
    load_own.wait()

    def picks(slot):
        side = arrived[slot, pl.ds(tokens, 16), :].astype(jnp.float32)
        line = lax.broadcasted_iota(jnp.int32, side.shape, 0)
        own = jnp.sum(jnp.where(line == me, side, 0.0), axis=0, keepdims=True)
        gates = own[:, :tokens] + own[:, 256 : 256 + tokens]
        place_of = own[:, 512 : 512 + tokens].astype(jnp.int32)
        pick = place_of == lax.broadcasted_iota(jnp.int32, (SLOTS, tokens), 0)
        return pick, gates

    a = Scatter(
        blocks, None, (near_mate, near_up, near_down, far_up, far_down, cross), (a_send, a_recv),
        cut,
    )

    def work(step, carry):
        @pl.when(step == 0)
        def _():
            move(3).wait_recv()

        @pl.when(step == 1)
        def _():
            move(1).wait_recv()
            move(4).start()
            move(8).start()
            move(2).wait_recv()
            move(5).start()
            move(9).start()
            move(0).wait_recv()
            for number in (6, 7, 10):
                move(number).start()
            move(8).wait_recv()

        @pl.when(step == 2)
        def _():
            move(9).wait_recv()

        @pl.when(step == 3)
        def _():
            move(10).wait_recv()

        @pl.when(step == 4)
        def _():
            move(6).wait_recv()
            move(11).start()
            move(13).start()
            move(7).wait_recv()
            move(12).start()
            move(14).start()
            move(4).wait_recv()
            move(15).start()
            move(5).wait_recv()
            move(16).start()
            move(15).wait_recv()
            move(16).wait_recv()

        @pl.when(step == 5)
        def _():
            move(13).wait_recv()

        @pl.when(step == 6)
        def _():
            move(14).wait_recv()

        @pl.when(step == 7)
        def _():
            move(11).wait_recv()
            move(17).start()
            move(12).wait_recv()
            move(18).start()
            move(17).wait_recv()
            move(18).wait_recv()

        @pl.when(step < 7)
        def _():
            load_mix(step + 1).start()

        load_mix(step).wait()
        buffer = lax.rem(step, 2)
        base = chip_of(step) * 2
        both = 2 * SLOTS
        at = pl.ds(pl.multiple_of(chip_of(step) * both, both), both)
        kept = []
        for b in range(2):
            pick, gates = picks(base + b)
            pick_b = pick.astype(jnp.bfloat16)
            slot_gates = jnp.sum(jnp.where(pick, gates, 0.0), axis=1, keepdims=True)
            here = pl.ds(b * SLOTS, SLOTS)
            there = pl.ds(pl.multiple_of(chip_of(step) * both + b * SLOTS, SLOTS), SLOTS)
            rows_c[there, :] = contract(
                pick_b, arrived[base + b, pl.ds(0, tokens), :], 1, 0
            ).astype(jnp.bfloat16)
            mix_rows = contract(pick_b, mix_buf[buffer, b], 1, 0)
            mix_c[here, :] = mix_rows.astype(jnp.bfloat16)
            route_c[there, :] = (slot_gates * mix_rows).astype(jnp.bfloat16)
            kept.append((pick, pick_b, slot_gates))
        slot_gates = jnp.concatenate([kept[0][2], kept[1][2]], axis=0)
        x, route = rows_c[at, :], route_c[at, :]

        def inner(tile, carry):
            left = pl.ds(pl.multiple_of(tile * 256, 256), 256)
            right = pl.ds(pl.multiple_of(512 + tile * 256, 256), 256)
            gate = contract(x, w_in[:, left], 1, 0)
            raised = contract(x, w_in[:, right], 1, 0)
            grad = contract(route, w_out[left, :], 1, 1)
            sig = 1.0 / (1.0 + jnp.exp(-gate))
            silu = gate * sig
            act_c[at, left] = (silu * raised).astype(jnp.bfloat16)
            pre_c[at, left] = (grad * raised * sig * (1.0 + gate * (1.0 - sig))).astype(
                jnp.bfloat16
            )
            pre_c[at, right] = (grad * silu).astype(jnp.bfloat16)
            return carry

        lax.fori_loop(0, 2, inner, 0)
        act, pre = act_c[at, :], pre_c[at, :]

        def outer(tile, total):
            span = pl.ds(pl.multiple_of(tile * 256, 256), 256)
            result = contract(act, w_out[:, span], 1, 0).astype(jnp.bfloat16).astype(jnp.float32)
            weighted[at, span] = (slot_gates * result).astype(jnp.bfloat16)
            row_c[:, span] = contract(pre, w_in[span, :], 1, 1).astype(jnp.bfloat16)
            return total + jnp.sum(
                result * mix_c[:, span].astype(jnp.float32), axis=1, keepdims=True
            )

        gate_grad = lax.fori_loop(0, 4, outer, jnp.zeros((both, 1), jnp.float32))
        for b in range(2):
            pick, pick_b, _ = kept[b]
            here = pl.ds(b * SLOTS, SLOTS)
            blocks[base + b, pl.ds(0, tokens), :] = contract(pick_b, row_c[here, :], 0, 0).astype(
                jnp.bfloat16
            )
            line_grad = jnp.sum(
                jnp.where(pick, gate_grad[b * SLOTS : (b + 1) * SLOTS], 0.0), axis=0, keepdims=True
            )
            upper = line_grad.astype(jnp.bfloat16).astype(jnp.float32)
            mine = lax.broadcasted_iota(jnp.int32, (16, tokens), 0) == me
            tail = pl.ds(tokens, 16)
            blocks[base + b, tail, :] = jnp.zeros((16, width), jnp.bfloat16)
            blocks[base + b, tail, pl.ds(0, tokens)] = jnp.where(mine, upper, 0.0).astype(
                jnp.bfloat16
            )
            blocks[base + b, tail, pl.ds(256, tokens)] = jnp.where(
                mine, line_grad - upper, 0.0
            ).astype(jnp.bfloat16)
        a.swap(step).start()
        return carry

    lax.fori_loop(0, 8, work, 0)
    for number in range(19):
        move(number).wait_send()

    a.first(0)
    a.first(1)

    def store(step):
        chip = chip_of(step) * 2
        return pltpu.make_async_copy(
            arrived.at[pl.ds(chip, 2), pl.ds(0, tokens)],
            mixture_ref.at[pl.ds(chip, 2)],
            store_sem.at[step],
        )

    def spread(step, carry):
        for b in range(2):
            slot = chip_of(step) * 2 + b
            pick, _ = picks(slot)
            here = pl.ds(pl.multiple_of(slot * SLOTS, SLOTS), SLOTS)
            arrived[slot, pl.ds(0, tokens), :] = contract(
                pick.astype(jnp.bfloat16), weighted[here, :], 0, 0
            ).astype(jnp.bfloat16)
        store(step).start()
        return carry

    def grad_in(tile, carry):
        span = pl.ds(pl.multiple_of(tile * 256, 256), 256)
        grads_ref[span, :] = contract(rows_c[:, span], pre_c[...], 0, 0).astype(jnp.bfloat16)
        return carry

    def grad_out(tile, carry):
        span = pl.ds(pl.multiple_of(tile * 256, 256), 256)
        there = pl.ds(pl.multiple_of(width + tile * 256, 256), 256)
        grads_ref[there, :] = contract(act_c[:, span], route_c[...], 0, 0).astype(jnp.bfloat16)
        return carry

    def give_back(span, value):
        back_ref[span, :] = value

    lax.fori_loop(0, 8, spread, 0)
    a.second(0)
    lax.fori_loop(0, 1, grad_in, 0)
    a.second(1)
    lax.fori_loop(1, 4, grad_in, 0)
    a.third(0)
    lax.fori_loop(0, 2, grad_out, 0)
    a.third(1)
    a.last(give_back)
    a.finish()

    def stored(step, carry):
        store(step).wait()
        return carry

    lax.fori_loop(0, 8, stored, 0)


def expert_layer(payload, mix, w_in, w_out, collective_id):
    rows, width = payload.shape
    tokens = rows - 16
    hidden = w_out.shape[0]
    cut = (rows // 16 + 1) // 2 * 16
    kind = jnp.bfloat16
    slots = 16 * SLOTS
    dma = pltpu.SemaphoreType.DMA

    return pl.pallas_call(
        functools.partial(expert_kernel, cut),
        out_shape=(
            jax.ShapeDtypeStruct((rows, width), jnp.float32),
            jax.ShapeDtypeStruct((16, tokens, width), kind),
            jax.ShapeDtypeStruct((width + hidden, width), kind),
        ),
        in_specs=[
            pl.BlockSpec(memory_space=pl.ANY),
            pl.BlockSpec(memory_space=pl.ANY),
            pl.BlockSpec(memory_space=pl.ANY),
            pl.BlockSpec(memory_space=pl.ANY),
        ],
        out_specs=(
            pl.BlockSpec(memory_space=pltpu.VMEM),
            pl.BlockSpec(memory_space=pl.ANY),
            pl.BlockSpec(memory_space=pltpu.VMEM),
        ),
        scratch_shapes=[
            pltpu.VMEM((16, rows, width), kind),
            pltpu.VMEM((2, 2, tokens, width), kind),
            pltpu.VMEM((width, 2 * hidden), kind),
            pltpu.VMEM((hidden, width), kind),
            pltpu.VMEM((16, rows, width), kind),
            pltpu.VMEM((slots, width), kind),
            pltpu.VMEM((slots, width), kind),
            pltpu.VMEM((slots, hidden), kind),
            pltpu.VMEM((slots, width), kind),
            pltpu.VMEM((slots, 2 * hidden), kind),
            pltpu.VMEM((2 * SLOTS, width), kind),
            pltpu.VMEM((2 * SLOTS, width), kind),
            *scatter_scratch(rows, width, cut),
            dma((3,)),
            dma((2,)),
            dma((8,)),
            dma((19,)),
            dma((19,)),
        ],
        compiler_params=pltpu.CompilerParams(
            collective_id=collective_id, has_side_effects=True, vmem_limit_bytes=60 * 1024 * 1024
        ),
        cost_estimate=pl.CostEstimate(
            flops=24 * 10**9, bytes_accessed=10**8, transcendentals=10**6
        ),
    )(payload, mix, w_in, w_out)


class Spots:
    def __init__(self, axis):
        me, rep, core, y, high = place()
        self.paired = axis == "shard"
        if self.paired:
            self.bits = (high, y, core)
            device = lambda slot: (slot, rep)
        else:
            self.bits = (rep // 4, lax.rem(rep, 4), None)
            device = lambda slot: (me, slot)
        self.targets = {
            "up": device(self.slot(0, 1)),
            "down": device(self.slot(0, 3)),
            "across": device(self.slot(1, 0)),
        }
        if self.paired:
            self.targets["mate"] = device(self.slot(0, 0, True))

    def slot(self, side, rise, swapped=False):
        high, ring, core = self.bits
        chip = lax.rem(high + side, 2) * 4 + lax.rem(ring + rise, 4)
        if not self.paired:
            return chip
        return 2 * chip + (1 - core if swapped else core)

    def of_step(self, step, swapped=False):
        return self.slot(select(SIDE_OF_STEP, step), select(UP_OF_STEP, step), swapped)


def neighbours():
    return list(Spots("shard").targets.values())


class Gather:
    def __init__(self, slots, split, sems, axis="shard", own=None):
        spots = Spots(axis)
        self.spots, self.slots, self.sems, self.own = spots, slots, sems, own
        rows = slots.shape[1]
        whole, top, low = pl.ds(0, rows), pl.ds(0, split), pl.ds(split, rows - split)
        me, other, far = spots.slot(0, 0), spots.slot(1, 0), spots.slot(0, 2)
        from_down, from_up = spots.slot(0, 3), spots.slot(0, 1)
        other_down, other_up = spots.slot(1, 3), spots.slot(1, 1)
        other_far = spots.slot(1, 2)
        self.plan = (
            (me, whole, "across"),
            (me, whole, "up"),
            (me, whole, "down"),
            (me, whole, "mate"),
            (from_down, top, "up"),
            (from_up, low, "down"),
            (other, whole, "up"),
            (other, whole, "down"),
            (from_down, whole, "mate"),
            (from_up, whole, "mate"),
            (other, whole, "mate"),
            (other_down, top, "up"),
            (other_up, low, "down"),
            (other_down, whole, "mate"),
            (other_up, whole, "mate"),
            (far, top, "mate"),
            (far, low, "mate"),
            (other_far, top, "mate"),
            (other_far, low, "mate"),
        )

    def used(self, numbers):
        return [n for n in numbers if self.plan[n][2] in self.spots.targets]

    def move(self, number):
        slot, span, target = self.plan[number]
        target_ref = self.slots.at[slot, span]
        return pltpu.make_async_remote_copy(
            src_ref=self.own if self.own is not None and number < 4 else target_ref,
            dst_ref=target_ref,
            send_sem=self.sems[0].at[number],
            recv_sem=self.sems[1].at[number],
            device_id=self.spots.targets[target],
            device_id_type=MESH,
        )

    def start(self, *numbers):
        for number in self.used(numbers):
            self.move(number).start()

    def arrive(self, *numbers):
        for number in self.used(numbers):
            self.move(number).wait_recv()

    def begin(self):
        self.start(0, 1, 2, 3)

    def first(self):
        self.arrive(1)
        self.start(4, 8)
        self.arrive(2)
        self.start(5, 9)
        self.arrive(0)
        self.start(6, 7, 10)

    def second(self):
        self.arrive(6)
        self.start(11, 13)
        self.arrive(7)
        self.start(12, 14)
        self.arrive(4)
        self.start(15)
        self.arrive(5)
        self.start(16)

    def third(self):
        self.arrive(11)
        self.start(17)
        self.arrive(12)
        self.start(18)

    def complete(self):
        self.arrive(3, 8, 9, 10, 13, 14, 15, 16, 17, 18)

    def finish(self):
        for number in self.used(range(19)):
            self.move(number).wait_send()


def rows_of(lengths_ref, shape):
    row = lax.broadcasted_iota(jnp.int32, shape, 0)
    first = lengths_ref[0, 0]
    total = first + lengths_ref[0, 1]
    start = jnp.where(row < first, 0, jnp.where(row < total, first, total))
    return row, start, row < total


def turn(value, cosine, sine):
    width = value.shape[1]
    lane = lax.rem(lax.broadcasted_iota(jnp.int32, value.shape, 1), HEAD_SIZE)
    beside = jnp.where(
        lane < HEAD_SIZE // 2,
        pltpu.roll(value, width - HEAD_SIZE // 2, 1),
        pltpu.roll(value, HEAD_SIZE // 2, 1),
    )
    return value * cosine + beside * sine


def norm_scale(value):
    return lax.rsqrt(jnp.mean(value * value, axis=1, keepdims=True) + EPS)


def unit(size):
    return (
        lax.broadcasted_iota(jnp.int32, (size, size), 0)
        == lax.broadcasted_iota(jnp.int32, (size, size), 1)
    ).astype(jnp.bfloat16)


def flat(ref, lanes):
    value = ref[:, :, lanes]
    return value.reshape(value.shape[0] * value.shape[1], value.shape[2])


class Loads:
    def __init__(self, sems):
        self.sems, self.copies = sems, []

    def add(self, source, target):
        copy = pltpu.make_async_copy(source, target, self.sems.at[len(self.copies)])
        copy.start()
        self.copies.append(copy)
        return copy

    def wait(self, *numbers):
        for number in numbers:
            self.copies[number].wait()


def front_kernel(
    tokens_any, lengths_ref, routes_any, gain_one_any, gain_two_any,
    query_any, key_any, value_any, output_any, router_any,
    payload_out, hidden_out, normed_out, qkv_out, mixed_out, prob_out, gates_out,
    cosine_out, sine_out, all_qkv_out, all_out_out,
    tokens_ref, routes_ref, gain_one_ref, gain_two_ref, router_ref,
    payload_ref, hidden_ref, normed_ref, qkv_ref, mixed_ref, prob_ref, gates_ref,
    cosine_ref, sine_ref, all_qkv, all_out,
    load_sem, store_sem, q_send, q_recv, o_send, o_recv,
):
    me = lax.axis_index("shard")
    rows, width = tokens_ref.shape
    f32, bf16 = jnp.float32, jnp.bfloat16
    half = KEY_VALUE_HEADS * HEAD_SIZE
    loads, stores = Loads(load_sem), Loads(store_sem)
    loads.add(query_any, all_qkv.at[me, :, pl.ds(0, width)])
    loads.add(key_any, all_qkv.at[me, :, pl.ds(width, half)])
    loads.add(value_any, all_qkv.at[me, :, pl.ds(width + half, half)])
    loads.add(output_any, all_out.at[me, :, pl.ds(0, width)])
    loads.add(router_any, router_ref)
    loads.add(tokens_any, tokens_ref)
    loads.add(routes_any, routes_ref)
    loads.add(gain_one_any, gain_one_ref)
    loads.add(gain_two_any, gain_two_ref)
    greet(neighbours())
    one = Gather(all_qkv, 32, (q_send, q_recv))
    two = Gather(all_out, 32, (o_send, o_recv))
    loads.wait(0, 1, 2)
    one.begin()
    loads.wait(4)
    pad = jnp.zeros((128 - E, router_ref.shape[1]), bf16)
    all_out[me, :, pl.ds(width, 128)] = contract(
        jnp.concatenate([router_ref[...], pad], axis=0), unit(128), 0, 0
    ).astype(bf16)
    all_out[me, :, pl.ds(width + 128, 128)] = jnp.zeros((router_ref.shape[1], 128), bf16)
    loads.wait(3)
    two.begin()
    loads.wait(5, 6, 7, 8)

    inputs = tokens_ref[...].astype(f32)
    normed_ref[...] = (inputs * norm_scale(inputs) * gain_one_ref[...].astype(f32).reshape(1, width)).astype(bf16)
    row, start, _ = rows_of(lengths_ref, (rows, 128))
    lane = lax.broadcasted_iota(jnp.int32, (rows, 128), 1)
    frequency = jnp.exp(
        lax.rem(lane, HEAD_SIZE // 2).astype(f32) * (-2.0 * math.log(ROPE_BASE) / HEAD_SIZE)
    )
    angle = (row - start).astype(f32) * frequency
    cosine_ref[...] = jnp.cos(angle)
    sine = jnp.sin(angle)
    sine_ref[...] = jnp.where(lax.rem(lane, HEAD_SIZE) < HEAD_SIZE // 2, -sine, sine)
    square = (rows, rows)
    across_row = lax.broadcasted_iota(jnp.int32, square, 0)
    across_col = lax.broadcasted_iota(jnp.int32, square, 1)
    earlier = (across_row > across_col).astype(bf16)
    expert = lax.broadcasted_iota(jnp.int32, (128, rows), 0)
    named = expert < 0
    for k in range(routes_ref.shape[0]):
        named = named | (routes_ref[k : k + 1, :] == expert)
    token = lax.broadcasted_iota(jnp.int32, (128, rows), 1)
    used = named & (token < lengths_ref[0, 0] + lengths_ref[0, 1])
    rank = contract(used.astype(bf16), earlier, 1, 1)
    place_of = jnp.where(used, rank, -1.0)
    eye = unit(rows)
    named = contract(eye, named.astype(bf16), 1, 1) > 0.5
    one.first()
    two.first()
    one.second()
    two.second()
    one.third()
    one.complete()
    stores.add(all_qkv, all_qkv_out)

    normed = normed_ref[...]
    cosine, signed = cosine_ref[...], sine_ref[...]
    for tile in range(4):
        lanes = pl.ds(tile * 512, 512)
        part = contract(normed, flat(all_qkv, lanes), 1, 0)
        if tile < 3:
            part = turn(part, jnp.tile(cosine, (1, 4)), jnp.tile(signed, (1, 4)))
        qkv_ref[:, lanes] = part.astype(bf16)
    two.third()
    _, start_row, _ = rows_of(lengths_ref, square)
    allowed = (across_col >= start_row) & (across_col <= across_row)
    both = jnp.concatenate([allowed, allowed], axis=0)
    for g in range(KEY_VALUE_HEADS):
        key = qkv_ref[:, pl.ds(width + g * HEAD_SIZE, HEAD_SIZE)]
        value = qkv_ref[:, pl.ds(width + half + g * HEAD_SIZE, HEAD_SIZE)]
        query = jnp.concatenate(
            [qkv_ref[:, pl.ds((2 * g + p) * HEAD_SIZE, HEAD_SIZE)] for p in range(2)], axis=0
        )
        scores = jnp.where(both, contract(query, key, 1, 1) * HEAD_SIZE**-0.5, NEGATIVE)
        raised = jnp.exp(scores - jnp.max(scores, axis=1, keepdims=True))
        prob = raised / jnp.sum(raised, axis=1, keepdims=True)
        prob_ref[g] = prob
        mixed = contract(prob.astype(bf16), value, 1, 0).astype(bf16)
        for p in range(2):
            mixed_ref[:, pl.ds((2 * g + p) * HEAD_SIZE, HEAD_SIZE)] = mixed[
                p * rows : (p + 1) * rows
            ]
    two.complete()
    for source, target in (
        (all_out, all_out_out), (normed_ref, normed_out), (qkv_ref, qkv_out),
        (mixed_ref, mixed_out), (prob_ref, prob_out), (cosine_ref, cosine_out),
        (sine_ref, sine_out),
    ):
        stores.add(source, target)
    _, _, live = rows_of(lengths_ref, (rows, 1))
    hidden = inputs + live.astype(f32) * contract(
        mixed_ref[...], flat(all_out, pl.ds(0, width)), 1, 0
    )
    hidden_ref[...] = hidden
    stores.add(hidden_ref, hidden_out)
    normed_two = (hidden * norm_scale(hidden) * gain_two_ref[...].astype(f32).reshape(1, width)).astype(bf16)
    payload_ref[pl.ds(0, rows), :] = normed_two
    logits = contract(normed_two, flat(all_out, pl.ds(width, 128)), 1, 0)
    logits = jnp.where(named, logits, NEGATIVE)
    raised = jnp.exp(logits - jnp.max(logits, axis=1, keepdims=True))
    gates = raised / jnp.sum(raised, axis=1, keepdims=True)
    gates_ref[...] = gates
    upper = gates.astype(bf16)
    lower = (gates - upper.astype(f32)).astype(bf16)
    tail = pl.ds(rows, E)
    payload_ref[tail, :] = jnp.zeros((E, width), bf16)
    for spot, table in enumerate((upper, lower)):
        payload_ref[tail, pl.ds(spot * 256, rows)] = contract(table, eye, 0, 0)[:E].astype(bf16)
    payload_ref[tail, pl.ds(512, rows)] = place_of[:E].astype(bf16)
    stores.add(gates_ref, gates_out)
    stores.add(payload_ref, payload_out)
    stores.wait(*range(11))
    one.finish()
    two.finish()


def front_layer(
    tokens, lengths, routes, gain_one, gain_two, query, key, value, output, router, collective_id
):
    rows, width = tokens.shape
    share = query.shape[0]
    f32, bf16 = jnp.float32, jnp.bfloat16
    dma = pltpu.SemaphoreType.DMA
    shape = jax.ShapeDtypeStruct
    kept = (
        shape((rows + E, width), bf16),
        shape((rows, width), f32),
        shape((rows, width), bf16),
        shape((rows, 2 * width), bf16),
        shape((rows, width), bf16),
        shape((KEY_VALUE_HEADS, 2 * rows, rows), f32),
        shape((rows, 128), f32),
        shape((rows, 128), f32),
        shape((rows, 128), f32),
        shape((16, share, 2 * width), bf16),
        shape((16, share, width + 256), bf16),
    )
    anywhere = pl.BlockSpec(memory_space=pl.ANY)
    inputs = (
        tokens, lengths, routes.T, gain_one, gain_two, query, key, value, output, router.T,
    )
    taken = [inputs[place] for place in (0, 2, 3, 4, 9)]
    return pl.pallas_call(
        front_kernel,
        out_shape=kept,
        in_specs=[anywhere, pl.BlockSpec(memory_space=pltpu.SMEM)] + [anywhere] * 8,
        out_specs=(anywhere,) * 11,
        scratch_shapes=[pltpu.VMEM(value.shape, value.dtype) for value in (*taken, *kept)]
        + [dma((9,)), dma((11,)), dma((19,)), dma((19,)), dma((19,)), dma((19,))],
        compiler_params=pltpu.CompilerParams(
            collective_id=collective_id, has_side_effects=True, vmem_limit_bytes=48 * 1024 * 1024
        ),
        cost_estimate=pl.CostEstimate(
            flops=24 * 10**9, bytes_accessed=10**8, transcendentals=10**6
        ),
    )(*inputs)


def chip_of(step):
    _, _, _, y, high = place()
    side, rise = select(SIDE_OF_STEP, step), select(UP_OF_STEP, step)
    return lax.rem(high + side, 2) * 4 + lax.rem(y + rise, 4)


class Scatter:
    def __init__(self, source, sums, bufs, sems, split, local_sem=None, axis="shard"):
        self.source, self.sums, self.bufs, self.sems = source, sums, bufs, sems
        self.count, self.split, self.local_sem = bufs[5].shape[0], split, local_sem
        self.spots = Spots(axis)
        self.pending = {}

    def block(self, step):
        if self.sums is None:
            return self.source.at[self.spots.of_step(step)]
        return self.sums.at[step]

    def load(self, step):
        return pltpu.make_async_copy(
            self.source.at[self.spots.of_step(step)], self.sums.at[step], self.local_sem.at[step]
        )

    def swap(self, step):
        return pltpu.make_async_remote_copy(
            src_ref=self.source.at[self.spots.of_step(step, True)],
            dst_ref=self.bufs[0].at[step],
            send_sem=self.sems[0].at[step],
            recv_sem=self.sems[1].at[step],
            device_id=self.spots.targets["mate"],
            device_id_type=MESH,
        )

    def begin(self):
        for step in (7, 4, 6, 5, 2, 1, 3, 0):
            if self.spots.paired:
                self.swap(jnp.int32(step)).start()
            if self.sums is not None:
                self.load(jnp.int32(step)).start()

    def settle(self, step):
        step = jnp.int32(step)
        if self.sums is not None:
            self.load(step).wait()
        if self.spots.paired:
            self.swap(step).wait_recv()
            add_rows(self.block(step), self.bufs[0].at[step], 0, self.count)

    def send(self, number, source, target_ref, target):
        copy = pltpu.make_async_remote_copy(
            src_ref=source,
            dst_ref=target_ref,
            send_sem=self.sems[0].at[number],
            recv_sem=self.sems[1].at[number],
            device_id=self.spots.targets[target],
            device_id_type=MESH,
        )
        copy.start()
        self.pending[number] = copy

    def first(self, o):
        step = (7, 4)[o]
        self.settle(step)
        block = self.block(jnp.int32(step))
        spans = pl.ds(0, self.split), pl.ds(self.split, self.count - self.split)
        self.send(8 + o, block.at[spans[0]], self.bufs[3].at[o], "up")
        self.send(10 + o, block.at[spans[1]], self.bufs[4].at[o], "down")

    def second(self, o):
        above, below = (6, 2)[o], (5, 1)[o]
        self.settle(above)
        self.settle(below)
        above, below = self.block(jnp.int32(above)), self.block(jnp.int32(below))
        self.pending[8 + o].wait_recv()
        add_rows(above, self.bufs[3].at[o], 0, self.split)
        self.send(12 + o, above, self.bufs[1].at[o], "up")
        self.pending[10 + o].wait_recv()
        add_rows(below, self.bufs[4].at[o], self.split, self.count - self.split)
        self.send(14 + o, below, self.bufs[2].at[o], "down")

    def third(self, o):
        step = (3, 0)[o]
        self.settle(step)
        block = self.block(jnp.int32(step))
        self.pending[12 + o].wait_recv()
        add_rows(block, self.bufs[1].at[o], 0, self.count)
        self.pending[14 + o].wait_recv()
        add_rows(block, self.bufs[2].at[o], 0, self.count)
        if o == 0:
            self.send(16, block, self.bufs[5], "across")

    def last(self, emit):
        self.pending[16].wait_recv()
        own, beside = self.block(jnp.int32(0)), self.bufs[5]

        def body(step, carry):
            span = pl.ds(pl.multiple_of(step * 16, 16), 16)
            emit(span, own[span, :].astype(jnp.float32) + beside[span, :].astype(jnp.float32))
            return carry

        lax.fori_loop(0, self.count // 16, body, 0)

    def finish(self):
        for step in range(8 if self.spots.paired else 0):
            self.swap(jnp.int32(step)).wait_send()
        for copy in self.pending.values():
            copy.wait_send()


def scatter_scratch(count, width, split, swapped=8):
    kind = jnp.bfloat16
    return [
        pltpu.VMEM((swapped, count, width), kind),
        pltpu.VMEM((2, count, width), kind),
        pltpu.VMEM((2, count, width), kind),
        pltpu.VMEM((2, split, width), kind),
        pltpu.VMEM((2, count - split, width), kind),
        pltpu.VMEM((count, width), kind),
        pltpu.SemaphoreType.DMA((17,)),
        pltpu.SemaphoreType.DMA((17,)),
    ]


class Total:
    def __init__(self, source, out, pieces, sems, piece):
        self.source, self.out, self.pieces = source, out, pieces
        self.sems, self.piece = sems, piece
        self.shard, self.me = lax.axis_index("shard"), lax.axis_index("replica")

    def copy(self, way, step):
        target = lax.rem(self.me + step, 8)
        if way == 0:
            source, place_of = self.piece(self.source, target), self.pieces.at[step - 1]
        else:
            source = place_of = self.piece(self.out, self.me)
        return pltpu.make_async_remote_copy(
            src_ref=source,
            dst_ref=place_of,
            send_sem=self.sems[2 * way].at[step - 1],
            recv_sem=self.sems[2 * way + 1].at[step - 1],
            device_id=(self.shard, target),
            device_id_type=MESH,
        )

    def begin(self):
        for step in range(1, 8):
            self.copy(0, step).start()

    def middle(self):
        for step in range(1, 8):
            self.copy(0, step).wait_recv()
        own = self.piece(self.source, self.me)
        result = self.piece(self.out, self.me)

        def body(turn_of, carry):
            span = pl.ds(pl.multiple_of(turn_of * 16, 16), 16)
            total = own[span, :].astype(jnp.float32)
            for step in range(7):
                total = total + self.pieces[step, span, :].astype(jnp.float32)
            result[span, :] = total.astype(jnp.bfloat16)
            return carry

        lax.fori_loop(0, self.pieces.shape[1] // 16, body, 0)
        for step in range(1, 8):
            self.copy(1, step).start()

    def end(self):
        for step in range(1, 8):
            self.copy(1, step).wait_recv()

    def finish(self):
        for step in range(1, 8):
            self.copy(0, step).wait_send()
            self.copy(1, step).wait_send()


def total_scratch(rows, width):
    dma = pltpu.SemaphoreType.DMA
    return [pltpu.VMEM((7, rows, width), jnp.bfloat16), dma((7,)), dma((7,)), dma((7,)), dma((7,))]


def quarter(ref, which):
    half = ref.shape[1] // 2
    return ref.at[
        pl.ds(pl.multiple_of((which // 2) * 16, 16), 16),
        pl.ds(pl.multiple_of(lax.rem(which, 2) * half, 128), half),
    ]


def norm_back(value, scale, gain, grad):
    gained = grad * gain
    return scale * gained - value * scale**3 * jnp.mean(gained * value, axis=1, keepdims=True)


def rear_kernel(
    lengths_ref, tokens_any, cotangent_any, gain_one_any, gain_two_any, payload_any, hidden_any,
    normed_any, qkv_any, mixed_any, prob_any, gates_any, cosine_any, sine_any, all_qkv_any,
    all_out_any, back_any, mixes_ref, grads_ref,
    output_ref, d_tokens_ref, d_gain_one_ref, d_gain_two_ref, d_query_ref, d_key_ref,
    d_value_ref, d_output_ref, d_router_ref, d_expert_ref,
    tokens_ref, cotangent_ref, gain_one_ref, gain_two_ref, payload_ref, hidden_ref,
    normed_ref, qkv_ref, mixed_ref, prob_ref, gates_ref, cosine_ref, sine_ref, all_qkv,
    all_out, back_ref,
    *scratch,
):
    scratch = list(scratch)

    def take(count):
        taken = scratch[:count]
        del scratch[:count]
        return taken

    load_sem, own_sem = take(2)
    mix_sums, mix_local = take(2)
    mix_bufs, mix_sems = take(6), take(2)
    (one_blocks,) = take(1)
    one_bufs, one_sems = take(6), take(2)
    (two_blocks,) = take(1)
    two_bufs, two_sems = take(6), take(2)
    expert_sums, expert_local = take(2)
    expert_bufs, expert_sems = take(6), take(2)
    expert_own, spread_send, spread_recv = take(3)
    (one_pieces,), one_total_sems = take(1), take(4)
    (two_pieces,), two_total_sems = take(1), take(4)
    one_part, two_part, one_total, two_total = take(4)
    mixed_grad_ref, turned_ref, qkv_grad_ref, first_grad_ref, hidden_grad_ref = take(5)
    f32, bf16 = jnp.float32, jnp.bfloat16
    rows, width = tokens_ref.shape
    half = KEY_VALUE_HEADS * HEAD_SIZE
    shard, me = lax.axis_index("shard"), lax.axis_index("replica")
    loads = Loads(load_sem)
    early = (
        (back_any, back_ref), (hidden_any, hidden_ref), (gates_any, gates_ref),
        (cotangent_any, cotangent_ref), (gain_two_any, gain_two_ref), (all_out_any, all_out),
        (mixed_any, mixed_ref), (payload_any, payload_ref),
    )
    late = (
        (qkv_any, qkv_ref), (prob_any, prob_ref), (cosine_any, cosine_ref), (sine_any, sine_ref),
        (all_qkv_any, all_qkv), (normed_any, normed_ref), (tokens_any, tokens_ref),
        (gain_one_any, gain_one_ref),
    )
    for source, target in early + late:
        loads.add(source, target)
    greet(neighbours() + [(shard, lax.rem(me + step, 8)) for step in range(1, 8)])
    mixes = Scatter(mixes_ref, mix_sums, mix_bufs, mix_sems, 96, mix_local)
    one = Scatter(one_blocks, None, one_bufs, one_sems, 32)
    two = Scatter(two_blocks, None, two_bufs, two_sems, 32)
    experts = Scatter(
        grads_ref, expert_sums, expert_bufs, expert_sems, 96, expert_local, "replica"
    )
    spread = Gather(d_expert_ref, 96, (spread_send, spread_recv), "replica", expert_own)
    one_sum = Total(one_part, one_total, one_pieces, one_total_sems, quarter)
    two_sum = Total(two_part, two_total, two_pieces, two_total_sems, quarter)
    mixes.begin()
    experts.begin()
    experts.first(0)
    experts.first(1)
    loads.wait(*range(len(early)))

    _, _, live = rows_of(lengths_ref, (rows, 1))
    live = live.astype(f32)
    eye = unit(rows)
    line = back_ref[pl.ds(rows, E), :]
    gap = jnp.zeros((128 - E, rows), bf16)

    def columns(part):
        return contract(eye, jnp.concatenate([part.astype(bf16), gap], axis=0), 1, 1)

    gate_grad = columns(line[:, :rows]) + columns(line[:, 256 : 256 + rows])
    gates = gates_ref[...]
    logit_grad = (gates * (gate_grad - jnp.sum(gates * gate_grad, axis=1, keepdims=True))).astype(
        bf16
    )
    second_grad = back_ref[pl.ds(0, rows), :] + contract(
        logit_grad, flat(all_out, pl.ds(width, 128)), 1, 1
    )
    hidden = hidden_ref[...]
    scale_two = norm_scale(hidden)
    d_gain_two = jnp.sum(second_grad * hidden * scale_two, axis=0, keepdims=True)
    hidden_grad = cotangent_ref[...].astype(f32) + norm_back(
        hidden, scale_two, gain_two_ref[...].astype(f32).reshape(1, width), second_grad
    )
    hidden_grad_ref[...] = hidden_grad
    attn_grad = (live * hidden_grad).astype(bf16)

    def weights_of(ref, tile, lanes):
        value = ref[4 * tile : 4 * tile + 4, :, :lanes]
        return value.reshape(256, lanes)

    for tile in range(4):
        span = pl.ds(tile * 256, 256)
        mixed_grad_ref[:, span] = contract(
            attn_grad, weights_of(all_out, tile, width), 1, 1
        ).astype(bf16)
        one_blocks[4 * tile : 4 * tile + 4, :, :width] = (
            contract(mixed_ref[:, span], attn_grad, 0, 0).astype(bf16).reshape(4, 64, width)
        )
        one_blocks[4 * tile : 4 * tile + 4, :, width : width + 128] = (
            contract(payload_ref[pl.ds(0, rows), span], logit_grad, 0, 0)
            .astype(bf16)
            .reshape(4, 64, 128)
        )
    one_blocks[:, :, width + 128 :] = jnp.zeros((16, 64, 128), bf16)
    one.begin()
    mixes.first(0)
    mixes.first(1)

    def heads(ref, g):
        return jnp.concatenate(
            [ref[:, pl.ds((2 * g + p) * HEAD_SIZE, HEAD_SIZE)] for p in range(2)], axis=0
        )

    def head_back(g):
        mixed_grad, query = heads(mixed_grad_ref, g), heads(qkv_ref, g)
        key = qkv_ref[:, pl.ds(width + g * HEAD_SIZE, HEAD_SIZE)]
        value = qkv_ref[:, pl.ds(width + half + g * HEAD_SIZE, HEAD_SIZE)]
        prob = prob_ref[g]
        prob_grad = contract(mixed_grad, value, 1, 1)
        qkv_grad_ref[:, pl.ds(width + half + g * HEAD_SIZE, HEAD_SIZE)] = contract(
            prob.astype(bf16), mixed_grad, 0, 0
        ).astype(bf16)
        score_grad = prob * (prob_grad - jnp.sum(prob * prob_grad, axis=1, keepdims=True))
        score_grad = score_grad.astype(bf16)
        query_grad = contract(score_grad, key, 1, 0) * HEAD_SIZE**-0.5
        for p in range(2):
            turned_ref[:, pl.ds((2 * g + p) * HEAD_SIZE, HEAD_SIZE)] = query_grad[
                p * rows : (p + 1) * rows
            ]
        turned_ref[:, pl.ds(width + g * HEAD_SIZE, HEAD_SIZE)] = (
            contract(score_grad, query, 0, 0) * HEAD_SIZE**-0.5
        )

    loads.wait(*range(len(early), len(early + late)))
    for g in range(2):
        head_back(g)
    experts.second(0)
    for g in range(2, 4):
        head_back(g)
    mixes.second(0)
    for g in range(4, 6):
        head_back(g)
    experts.second(1)
    mixes.second(1)
    one.first(0)
    one.first(1)
    for g in range(6, 8):
        head_back(g)
    cosine, signed = cosine_ref[...], -sine_ref[...]
    for tile in range(3):
        lanes = pl.ds(tile * 512, 512)
        qkv_grad_ref[:, lanes] = turn(
            turned_ref[:, lanes], jnp.tile(cosine, (1, 4)), jnp.tile(signed, (1, 4))
        ).astype(bf16)
    mixes.third(0)
    qkv_grad = qkv_grad_ref[...]
    for tile in range(4):
        span = pl.ds(tile * 256, 256)
        first_grad_ref[:, span] = contract(qkv_grad, weights_of(all_qkv, tile, 2 * width), 1, 1)
        two_blocks[4 * tile : 4 * tile + 4, :, : 2 * width] = (
            contract(normed_ref[:, span], qkv_grad, 0, 0).astype(bf16).reshape(4, 64, 2 * width)
        )
    inputs = tokens_ref[...].astype(f32)
    scale_one = norm_scale(inputs)
    first_grad = first_grad_ref[...]
    d_gain_one = jnp.sum(first_grad * inputs * scale_one, axis=0, keepdims=True)
    two_blocks[:, :, 2 * width :] = jnp.zeros((16, 64, 256), bf16)
    pieces = [
        gain[:, 128 * part : 128 * part + 128]
        for gain in (d_gain_one, d_gain_two)
        for part in range(8)
    ]
    gain_tile = jnp.concatenate(pieces, axis=0).astype(bf16)
    for block in range(16):
        two_blocks[block, pl.ds(0, 16), pl.ds(2 * width, 128)] = gain_tile
    two.begin()
    experts.third(0)
    one.second(0)
    mixes.third(1)
    one.second(1)
    two.first(0)
    two.first(1)
    experts.third(1)
    d_tokens_ref[...] = hidden_grad_ref[...] + norm_back(
        inputs, scale_one, gain_one_ref[...].astype(f32).reshape(1, width), first_grad
    )

    def give_output(span, value):
        row = lax.broadcasted_iota(jnp.int32, (16, 1), 0) + span.start
        alive = (row < lengths_ref[0, 0] + lengths_ref[0, 1]).astype(f32)
        output_ref[span, :] = (hidden_ref[span, :] + alive * value).astype(bf16)

    def give(ref):
        def emit(span, value):
            ref[span, :] = value.astype(bf16)

        return emit

    experts.last(give(expert_own))
    own_store = pltpu.make_async_copy(expert_own, d_expert_ref.at[me], own_sem)
    own_store.start()
    spread.begin()
    mixes.last(give_output)

    one.third(0)
    two.second(0)
    one.third(1)
    two.second(1)
    spread.first()
    one.last(give(one_part))
    one_sum.begin()
    two.third(0)
    two.third(1)
    spread.second()
    one_sum.middle()
    two.last(give(two_part))
    two_sum.begin()
    one_sum.end()
    d_output_ref[...] = one_total[:, pl.ds(0, width)].astype(f32)
    d_router_ref[...] = one_total[:, pl.ds(width, 128)].astype(f32)
    two_sum.middle()
    spread.third()
    two_sum.end()
    d_query_ref[...] = two_total[:, pl.ds(0, width)].astype(f32)
    d_key_ref[...] = two_total[:, pl.ds(width, half)].astype(f32)
    d_value_ref[...] = two_total[:, pl.ds(width + half, half)].astype(f32)
    gains = two_total[pl.ds(0, 16), pl.ds(2 * width, 128)].astype(f32)
    d_gain_one_ref[...] = gains[:8]
    d_gain_two_ref[...] = gains[8:]
    spread.complete()
    own_store.wait()
    for user in (mixes, one, two, experts, spread, one_sum, two_sum):
        user.finish()


def rear_layer(
    tokens, lengths, cotangent, gain_one, gain_two, kept, back, mixes, grads, collective_id
):
    rows, width = tokens.shape
    half = KEY_VALUE_HEADS * HEAD_SIZE
    f32, bf16 = jnp.float32, jnp.bfloat16
    vmem = pl.BlockSpec(memory_space=pltpu.VMEM)
    anywhere = pl.BlockSpec(memory_space=pl.ANY)
    dma = pltpu.SemaphoreType.DMA
    shape = jax.ShapeDtypeStruct
    wide_one, wide_two = width + 256, 2 * width + 256
    slab = grads.shape[0] // 8
    inputs = (tokens, cotangent, gain_one, gain_two, *kept, back)
    return pl.pallas_call(
        rear_kernel,
        out_shape=(
            shape((rows, width), bf16),
            shape((rows, width), f32),
            shape((8, 128), f32),
            shape((8, 128), f32),
            shape((64, width), f32),
            shape((64, half), f32),
            shape((64, half), f32),
            shape((64, width), f32),
            shape((64, 128), f32),
            shape((8, slab, width), bf16),
        ),
        in_specs=[pl.BlockSpec(memory_space=pltpu.SMEM)] + [anywhere] * (len(inputs) + 2),
        out_specs=(vmem,) * 9 + (anywhere,),
        scratch_shapes=[
            *(pltpu.VMEM(value.shape, value.dtype) for value in inputs),
            dma((len(inputs),)),
            dma,
            pltpu.VMEM((8, rows, width), bf16),
            dma((8,)),
            *scatter_scratch(rows, width, 96),
            pltpu.VMEM((16, 64, wide_one), bf16),
            *scatter_scratch(64, wide_one, 32),
            pltpu.VMEM((16, 64, wide_two), bf16),
            *scatter_scratch(64, wide_two, 32),
            pltpu.VMEM((8, slab, width), bf16),
            dma((8,)),
            *scatter_scratch(slab, width, 96, 1),
            pltpu.VMEM((slab, width), bf16),
            dma((19,)),
            dma((19,)),
            *total_scratch(16, wide_one // 2),
            *total_scratch(16, wide_two // 2),
            pltpu.VMEM((64, wide_one), bf16),
            pltpu.VMEM((64, wide_two), bf16),
            pltpu.VMEM((64, wide_one), bf16),
            pltpu.VMEM((64, wide_two), bf16),
            pltpu.VMEM((rows, width), bf16),
            pltpu.VMEM((rows, width + half), f32),
            pltpu.VMEM((rows, 2 * width), bf16),
            pltpu.VMEM((rows, width), f32),
            pltpu.VMEM((rows, width), f32),
        ],
        compiler_params=pltpu.CompilerParams(
            collective_id=collective_id, has_side_effects=True, vmem_limit_bytes=60 * 1024 * 1024
        ),
        cost_estimate=pl.CostEstimate(
            flops=24 * 10**9, bytes_accessed=10**8, transcendentals=10**6
        ),
    )(lengths, *inputs, mixes, grads.reshape(8, slab, width))


def local(
    tokens,
    seq_lengths,
    routes,
    attn_gain,
    ffn_gain,
    w_query,
    key_projection,
    value_projection,
    w_output,
    w_router,
    w_in,
    w_out,
    cotangent,
):
    rows, width = tokens.shape
    all_cotangent = lax.all_gather(cotangent, "shard", axis=0)
    payload, *kept = front_layer(
        tokens, seq_lengths, routes, attn_gain, ffn_gain,
        w_query, key_projection, value_projection, w_output, w_router, 1,
    )
    back, mixes, expert_grads = expert_layer(payload, all_cotangent, w_in[0], w_out[0], 2)
    (
        output, d_tokens, d_attn_gain, d_ffn_gain, d_query, d_key, d_value, d_output, d_router,
        expert_grads,
    ) = rear_layer(
        tokens, seq_lengths, cotangent, attn_gain, ffn_gain,
        (payload, *kept), back, mixes, expert_grads, 3,
    )
    expert_grads = expert_grads.reshape(-1, width)
    return (
        output,
        d_tokens,
        d_attn_gain.reshape(width),
        d_ffn_gain.reshape(width),
        d_query,
        d_key,
        d_value,
        d_output,
        d_router[:, :E],
        expert_grads[:width].astype(jnp.float32)[None],
        expert_grads[width:].astype(jnp.float32)[None],
    )


def solution(mesh):
    return jax.shard_map(
        local,
        mesh=mesh,
        in_specs=(
            P(("shard", "replica"), None),
            P(("shard", "replica"), None),
            P(("shard", "replica"), None),
            P(),
            P(),
            P("shard", None),
            P("shard", None),
            P("shard", None),
            P("shard", None),
            P("shard", None),
            P("shard", None, None),
            P("shard", None, None),
            P(("shard", "replica"), None),
        ),
        out_specs=(
            P(("shard", "replica"), None),
            P(("shard", "replica"), None),
            P(),
            P(),
            P("shard", None),
            P("shard", None),
            P("shard", None),
            P("shard", None),
            P("shard", None),
            P("shard", None, None),
            P("shard", None, None),
        ),
        check_vma=False,
    )
```

```python
import functools
import math

import jax
import jax.numpy as jnp
from jax import lax
from jax.experimental import pallas as pl
from jax.experimental.pallas import tpu as pltpu
from jax.sharding import PartitionSpec as P

QUERY_HEADS = 16
KEY_VALUE_HEADS = 8
HEAD_SIZE = 64
H = 512
E = 16
CAP = 120

EPS = 1e-06
ROPE_BASE = 10000.0
NEGATIVE = -1e30

MESH = pl.DeviceIdType.MESH


def place():
    me = lax.axis_index("shard")
    rep = lax.axis_index("replica")
    core = lax.rem(me, 2)
    y = lax.rem(me // 2, 4)
    high = me // 8
    return me, rep, core, y, high


def index_of(high, y, core):
    return (high * 4 + lax.rem(y, 4)) * 2 + core


def greet(targets):
    barrier = pltpu.get_barrier_semaphore()
    for target in targets:
        pl.semaphore_signal(barrier, inc=1, device_id=target, device_id_type=MESH)
    pl.semaphore_wait(barrier, len(targets))


def add_rows(target, source, start, count):
    def body(step, carry):
        at = pl.ds(pl.multiple_of(start + step * 16, 16), 16)
        here = pl.ds(pl.multiple_of(step * 16, 16), 16)
        target[at, :] = (
            target[at, :].astype(jnp.float32) + source[here, :].astype(jnp.float32)
        ).astype(target.dtype)
        return carry

    lax.fori_loop(0, count // 16, body, 0)


def contract(a, b, left, right):
    return lax.dot_general(
        a, b, (((left,), (right,)), ((), ())), preferred_element_type=jnp.float32
    )


UP_OF_STEP = (0, 3, 1, 0, 2, 3, 1, 2)
SIDE_OF_STEP = (0, 0, 0, 1, 0, 1, 1, 1)
SLOTS = 128


def select(table, step):
    value = jnp.int32(table[0])
    for place in range(1, len(table)):
        if table[place] != table[place - 1]:
            value = value + (table[place] - table[place - 1]) * jnp.minimum(
                jnp.maximum(step - (place - 1), 0), 1
            )
    return value


def expert_kernel(
    cut, payload_ref, mix_ref, w_in_ref, w_out_ref, back_ref, mixture_ref, grads_ref,
    arrived, mix_buf, w_in, w_out, blocks, weighted, rows_c, act_c, route_c, pre_c, mix_c, row_c,
    near_mate, near_up, near_down, far_up, far_down, cross,
    a_send, a_recv, local_sem, mix_sem, store_sem, send_sem, recv_sem,
):
    me = lax.axis_index("shard")
    width = payload_ref.shape[1]
    rows = payload_ref.shape[0]
    tokens = rows - 16
    load_in = pltpu.make_async_copy(w_in_ref, w_in, local_sem.at[0])
    load_out = pltpu.make_async_copy(w_out_ref, w_out, local_sem.at[1])
    load_own = pltpu.make_async_copy(payload_ref, arrived.at[me], local_sem.at[2])
    load_in.start()
    load_out.start()
    load_own.start()

    def load_mix(step):
        slot = lax.rem(step, 2)
        return pltpu.make_async_copy(
            mix_ref.at[pl.ds(chip_of(step) * 2, 2)], mix_buf.at[slot], mix_sem.at[slot]
        )

    load_mix(0).start()
    greet(neighbours())
    gather = Gather(arrived, cut, 96, (send_sem, recv_sem), own=payload_ref)
    gather.begin()
    load_in.wait()
    load_out.wait()
    load_own.wait()

    def picks(slot):
        side = arrived[slot, pl.ds(tokens, 16), :].astype(jnp.float32)
        line = lax.broadcasted_iota(jnp.int32, side.shape, 0)
        own = jnp.sum(jnp.where(line == me, side, 0.0), axis=0, keepdims=True)
        gates = own[:, :tokens] + own[:, 256 : 256 + tokens]
        place_of = own[:, 512 : 512 + tokens].astype(jnp.int32)
        pick = place_of == lax.broadcasted_iota(jnp.int32, (SLOTS, tokens), 0)
        return pick, gates

    a = Scatter(
        blocks, None, (near_mate, near_up, near_down, far_up, far_down, cross), (a_send, a_recv),
        cut,
    )

    def work(step, carry):
        @pl.when(step == 0)
        def _():
            gather.arrive(3)

        @pl.when(step == 1)
        def _():
            gather.first()
            gather.arrive(8)

        @pl.when(step == 2)
        def _():
            gather.arrive(9)

        @pl.when(step == 3)
        def _():
            gather.arrive(10)

        @pl.when(step == 4)
        def _():
            gather.second()
            gather.arrive(15, 16)

        @pl.when(step == 5)
        def _():
            gather.arrive(13)

        @pl.when(step == 6)
        def _():
            gather.arrive(14)

        @pl.when(step == 7)
        def _():
            gather.third()
            gather.arrive(17, 18)

        @pl.when(step < 7)
        def _():
            load_mix(step + 1).start()

        load_mix(step).wait()
        buffer = lax.rem(step, 2)
        base = chip_of(step) * 2
        both = 2 * SLOTS
        at = pl.ds(pl.multiple_of(chip_of(step) * both, both), both)
        kept = []
        for b in range(2):
            pick, gates = picks(base + b)
            pick_b = pick.astype(jnp.bfloat16)
            slot_gates = jnp.sum(jnp.where(pick, gates, 0.0), axis=1, keepdims=True)
            here = pl.ds(b * SLOTS, SLOTS)
            there = pl.ds(pl.multiple_of(chip_of(step) * both + b * SLOTS, SLOTS), SLOTS)
            rows_c[there, :] = contract(
                pick_b, arrived[base + b, pl.ds(0, tokens), :], 1, 0
            ).astype(jnp.bfloat16)
            mix_rows = contract(pick_b, mix_buf[buffer, b], 1, 0)
            mix_c[here, :] = mix_rows.astype(jnp.bfloat16)
            route_c[there, :] = (slot_gates * mix_rows).astype(jnp.bfloat16)
            kept.append((pick, pick_b, slot_gates))
        slot_gates = jnp.concatenate([kept[0][2], kept[1][2]], axis=0)
        x, route = rows_c[at, :], route_c[at, :]

        def inner(tile, carry):
            left = pl.ds(pl.multiple_of(tile * 256, 256), 256)
            right = pl.ds(pl.multiple_of(512 + tile * 256, 256), 256)
            gate = contract(x, w_in[:, left], 1, 0)
            raised = contract(x, w_in[:, right], 1, 0)
            grad = contract(route, w_out[left, :], 1, 1)
            sig = 1.0 / (1.0 + jnp.exp(-gate))
            silu = gate * sig
            act_c[at, left] = (silu * raised).astype(jnp.bfloat16)
            pre_c[at, left] = (grad * raised * sig * (1.0 + gate * (1.0 - sig))).astype(
                jnp.bfloat16
            )
            pre_c[at, right] = (grad * silu).astype(jnp.bfloat16)
            return carry

        lax.fori_loop(0, 2, inner, 0)
        act, pre = act_c[at, :], pre_c[at, :]

        def outer(tile, total):
            span = pl.ds(pl.multiple_of(tile * 256, 256), 256)
            result = contract(act, w_out[:, span], 1, 0).astype(jnp.bfloat16).astype(jnp.float32)
            weighted[at, span] = (slot_gates * result).astype(jnp.bfloat16)
            row_c[:, span] = contract(pre, w_in[span, :], 1, 1).astype(jnp.bfloat16)
            return total + jnp.sum(
                result * mix_c[:, span].astype(jnp.float32), axis=1, keepdims=True
            )

        gate_grad = lax.fori_loop(0, 4, outer, jnp.zeros((both, 1), jnp.float32))
        for b in range(2):
            pick, pick_b, _ = kept[b]
            here = pl.ds(b * SLOTS, SLOTS)
            blocks[base + b, pl.ds(0, tokens), :] = contract(pick_b, row_c[here, :], 0, 0).astype(
                jnp.bfloat16
            )
            line_grad = jnp.sum(
                jnp.where(pick, gate_grad[b * SLOTS : (b + 1) * SLOTS], 0.0), axis=0, keepdims=True
            )
            upper = line_grad.astype(jnp.bfloat16).astype(jnp.float32)
            mine = lax.broadcasted_iota(jnp.int32, (16, tokens), 0) == me
            tail = pl.ds(tokens, 16)
            blocks[base + b, tail, :] = jnp.zeros((16, width), jnp.bfloat16)
            blocks[base + b, tail, pl.ds(0, tokens)] = jnp.where(mine, upper, 0.0).astype(
                jnp.bfloat16
            )
            blocks[base + b, tail, pl.ds(256, tokens)] = jnp.where(
                mine, line_grad - upper, 0.0
            ).astype(jnp.bfloat16)
        a.swap(step).start()
        return carry

    lax.fori_loop(0, 8, work, 0)
    gather.finish()

    a.first(0)
    a.first(1)

    def store(step):
        chip = chip_of(step) * 2
        return pltpu.make_async_copy(
            arrived.at[pl.ds(chip, 2), pl.ds(0, tokens)],
            mixture_ref.at[pl.ds(chip, 2)],
            store_sem.at[step],
        )

    def spread(step, carry):
        for b in range(2):
            slot = chip_of(step) * 2 + b
            pick, _ = picks(slot)
            here = pl.ds(pl.multiple_of(slot * SLOTS, SLOTS), SLOTS)
            arrived[slot, pl.ds(0, tokens), :] = contract(
                pick.astype(jnp.bfloat16), weighted[here, :], 0, 0
            ).astype(jnp.bfloat16)
        store(step).start()
        return carry

    def grad_in(tile, carry):
        span = pl.ds(pl.multiple_of(tile * 256, 256), 256)
        grads_ref[span, :] = contract(rows_c[:, span], pre_c[...], 0, 0).astype(jnp.bfloat16)
        return carry

    def grad_out(tile, carry):
        span = pl.ds(pl.multiple_of(tile * 256, 256), 256)
        there = pl.ds(pl.multiple_of(width + tile * 256, 256), 256)
        grads_ref[there, :] = contract(act_c[:, span], route_c[...], 0, 0).astype(jnp.bfloat16)
        return carry

    def give_back(span, value):
        back_ref[span, :] = value

    lax.fori_loop(0, 8, spread, 0)
    a.second(0)
    lax.fori_loop(0, 1, grad_in, 0)
    a.second(1)
    lax.fori_loop(1, 4, grad_in, 0)
    a.third(0)
    lax.fori_loop(0, 2, grad_out, 0)
    a.third(1)
    a.last(give_back)
    a.finish()

    def stored(step, carry):
        store(step).wait()
        return carry

    lax.fori_loop(0, 8, stored, 0)


def expert_layer(payload, mix, w_in, w_out, collective_id):
    rows, width = payload.shape
    tokens = rows - 16
    hidden = w_out.shape[0]
    cut = (rows // 16 + 1) // 2 * 16
    kind = jnp.bfloat16
    slots = 16 * SLOTS
    dma = pltpu.SemaphoreType.DMA

    return pl.pallas_call(
        functools.partial(expert_kernel, cut),
        out_shape=(
            jax.ShapeDtypeStruct((rows, width), jnp.float32),
            jax.ShapeDtypeStruct((16, tokens, width), kind),
            jax.ShapeDtypeStruct((width + hidden, width), kind),
        ),
        in_specs=[
            pl.BlockSpec(memory_space=pl.ANY),
            pl.BlockSpec(memory_space=pl.ANY),
            pl.BlockSpec(memory_space=pl.ANY),
            pl.BlockSpec(memory_space=pl.ANY),
        ],
        out_specs=(
            pl.BlockSpec(memory_space=pltpu.VMEM),
            pl.BlockSpec(memory_space=pl.ANY),
            pl.BlockSpec(memory_space=pltpu.VMEM),
        ),
        scratch_shapes=[
            pltpu.VMEM((16, rows, width), kind),
            pltpu.VMEM((2, 2, tokens, width), kind),
            pltpu.VMEM((width, 2 * hidden), kind),
            pltpu.VMEM((hidden, width), kind),
            pltpu.VMEM((16, rows, width), kind),
            pltpu.VMEM((slots, width), kind),
            pltpu.VMEM((slots, width), kind),
            pltpu.VMEM((slots, hidden), kind),
            pltpu.VMEM((slots, width), kind),
            pltpu.VMEM((slots, 2 * hidden), kind),
            pltpu.VMEM((2 * SLOTS, width), kind),
            pltpu.VMEM((2 * SLOTS, width), kind),
            *scatter_scratch(rows, width, cut),
            dma((3,)),
            dma((2,)),
            dma((8,)),
            dma((22,)),
            dma((22,)),
        ],
        compiler_params=pltpu.CompilerParams(
            collective_id=collective_id, has_side_effects=True, vmem_limit_bytes=62 * 1024 * 1024
        ),
        cost_estimate=pl.CostEstimate(
            flops=24 * 10**9, bytes_accessed=10**8, transcendentals=10**6
        ),
    )(payload, mix, w_in, w_out)


class Spots:
    def __init__(self, axis):
        me, rep, core, y, high = place()
        self.paired = axis == "shard"
        if self.paired:
            self.bits = (high, y, core)
            device = lambda slot: (slot, rep)
        else:
            self.bits = (rep // 4, lax.rem(rep, 4), None)
            device = lambda slot: (me, slot)
        self.targets = {
            "up": device(self.slot(0, 1)),
            "down": device(self.slot(0, 3)),
            "across": device(self.slot(1, 0)),
        }
        if self.paired:
            self.targets["mate"] = device(self.slot(0, 0, True))

    def slot(self, side, rise, swapped=False):
        high, ring, core = self.bits
        chip = lax.rem(high + side, 2) * 4 + lax.rem(ring + rise, 4)
        if not self.paired:
            return chip
        return 2 * chip + (1 - core if swapped else core)

    def of_step(self, step, swapped=False):
        return self.slot(select(SIDE_OF_STEP, step), select(UP_OF_STEP, step), swapped)


def neighbours():
    return list(Spots("shard").targets.values())


class Gather:
    def __init__(self, slots, split, crossed, sems, axis="shard", own=None):
        spots = Spots(axis)
        self.spots, self.slots, self.sems, self.own = spots, slots, sems, own
        rows = slots.shape[1]
        whole, top, low = pl.ds(0, rows), pl.ds(0, split), pl.ds(split, rows - split)
        half = (rows - crossed + 16) // 32 * 16 + crossed
        cross, late = pl.ds(0, crossed), pl.ds(crossed, rows - crossed)
        late_top, late_low = pl.ds(crossed, half - crossed), pl.ds(half, rows - half)
        self.crossed = crossed
        me, other, far = spots.slot(0, 0), spots.slot(1, 0), spots.slot(0, 2)
        from_down, from_up = spots.slot(0, 3), spots.slot(0, 1)
        other_down, other_up = spots.slot(1, 3), spots.slot(1, 1)
        other_far = spots.slot(1, 2)
        self.plan = (
            (me, whole, "across"),
            (me, whole, "up"),
            (me, whole, "down"),
            (me, whole, "mate"),
            (from_down, top, "up"),
            (from_up, low, "down"),
            (other, late, "up"),
            (other, late, "down"),
            (from_down, whole, "mate"),
            (from_up, whole, "mate"),
            (other, whole, "mate"),
            (other_down, late_top, "up"),
            (other_up, late_low, "down"),
            (other_down, whole, "mate"),
            (other_up, whole, "mate"),
            (far, top, "mate"),
            (far, low, "mate"),
            (other_far, pl.ds(0, half), "mate"),
            (other_far, late_low, "mate"),
            (from_down, cross, "across"),
            (from_up, cross, "across"),
            (far, cross, "across"),
        )

    def used(self, numbers):
        skipped = () if self.crossed else (19, 20, 21)
        return [n for n in numbers if n not in skipped and self.plan[n][2] in self.spots.targets]

    def move(self, number):
        slot, span, target = self.plan[number]
        target_ref = self.slots.at[slot, span]
        return pltpu.make_async_remote_copy(
            src_ref=self.own if self.own is not None and number < 4 else target_ref,
            dst_ref=target_ref,
            send_sem=self.sems[0].at[number],
            recv_sem=self.sems[1].at[number],
            device_id=self.spots.targets[target],
            device_id_type=MESH,
        )

    def start(self, *numbers):
        for number in self.used(numbers):
            self.move(number).start()

    def arrive(self, *numbers):
        for number in self.used(numbers):
            self.move(number).wait_recv()

    def begin(self):
        self.start(0, 1, 2, 3)

    def first(self):
        self.arrive(1)
        self.start(4, 19, 8)
        self.arrive(2)
        self.start(5, 20, 9)
        self.arrive(0)
        self.start(6, 7, 10)

    def second(self):
        self.arrive(4)
        self.start(21, 15)
        self.arrive(5)
        self.start(16)
        self.arrive(6)
        self.start(11)
        self.arrive(7)
        self.start(12)
        self.arrive(19)
        self.start(13)
        self.arrive(20)
        self.start(14)

    def third(self):
        self.arrive(11, 21)
        self.start(17)
        self.arrive(12)
        self.start(18)

    def complete(self):
        self.arrive(3, 8, 9, 10, 13, 14, 15, 16, 17, 18)

    def finish(self):
        for number in self.used(range(22)):
            self.move(number).wait_send()


def rows_of(lengths_ref, shape):
    row = lax.broadcasted_iota(jnp.int32, shape, 0)
    first = lengths_ref[0, 0]
    total = first + lengths_ref[0, 1]
    start = jnp.where(row < first, 0, jnp.where(row < total, first, total))
    return row, start, row < total


def turn(value, cosine, sine):
    width = value.shape[1]
    lane = lax.rem(lax.broadcasted_iota(jnp.int32, value.shape, 1), HEAD_SIZE)
    beside = jnp.where(
        lane < HEAD_SIZE // 2,
        pltpu.roll(value, width - HEAD_SIZE // 2, 1),
        pltpu.roll(value, HEAD_SIZE // 2, 1),
    )
    return value * cosine + beside * sine


def norm_scale(value):
    return lax.rsqrt(jnp.mean(value * value, axis=1, keepdims=True) + EPS)


def unit(size):
    return (
        lax.broadcasted_iota(jnp.int32, (size, size), 0)
        == lax.broadcasted_iota(jnp.int32, (size, size), 1)
    ).astype(jnp.bfloat16)


def flat(ref, lanes):
    value = ref[:, :, lanes]
    return value.reshape(value.shape[0] * value.shape[1], value.shape[2])


class Loads:
    def __init__(self, sems):
        self.sems, self.copies = sems, []

    def add(self, source, target):
        copy = pltpu.make_async_copy(source, target, self.sems.at[len(self.copies)])
        copy.start()
        self.copies.append(copy)
        return copy

    def wait(self, *numbers):
        for number in numbers:
            self.copies[number].wait()


def front_kernel(
    tokens_any, lengths_ref, routes_any, gain_one_any, gain_two_any,
    query_any, key_any, value_any, output_any, router_any, cotangent_any,
    payload_out, hidden_out, normed_out, qkv_out, mixed_out, prob_out, gates_out,
    cosine_out, sine_out, all_qkv_out, all_out_out, all_cotangent,
    tokens_ref, routes_ref, gain_one_ref, gain_two_ref, router_ref, cotangent_ref,
    payload_ref, hidden_ref, normed_ref, qkv_ref, mixed_ref, prob_ref, gates_ref,
    cosine_ref, sine_ref, all_qkv, all_out,
    load_sem, store_sem, q_send, q_recv, o_send, o_recv, c_send, c_recv,
):
    me = lax.axis_index("shard")
    rows, width = tokens_ref.shape
    f32, bf16 = jnp.float32, jnp.bfloat16
    half = KEY_VALUE_HEADS * HEAD_SIZE
    loads, stores = Loads(load_sem), Loads(store_sem)
    loads.add(query_any, all_qkv.at[me, :, pl.ds(0, width)])
    loads.add(key_any, all_qkv.at[me, :, pl.ds(width, half)])
    loads.add(value_any, all_qkv.at[me, :, pl.ds(width + half, half)])
    loads.add(output_any, all_out.at[me, :, pl.ds(0, width)])
    loads.add(router_any, router_ref)
    loads.add(tokens_any, tokens_ref)
    loads.add(routes_any, routes_ref)
    loads.add(gain_one_any, gain_one_ref)
    loads.add(gain_two_any, gain_two_ref)
    loads.add(cotangent_any, cotangent_ref)
    greet(neighbours())
    one = Gather(all_qkv, 32, 32, (q_send, q_recv))
    two = Gather(all_out, 32, 32, (o_send, o_recv))
    three = Gather(all_cotangent, 96, 96, (c_send, c_recv), own=cotangent_ref)
    loads.wait(0, 1, 2)
    one.begin()
    loads.wait(4)
    pad = jnp.zeros((128 - E, router_ref.shape[1]), bf16)
    all_out[me, :, pl.ds(width, 128)] = contract(
        jnp.concatenate([router_ref[...], pad], axis=0), unit(128), 0, 0
    ).astype(bf16)
    all_out[me, :, pl.ds(width + 128, 128)] = jnp.zeros((router_ref.shape[1], 128), bf16)
    loads.wait(3)
    two.begin()
    loads.wait(5, 6, 7, 8, 9)
    stores.add(cotangent_ref, all_cotangent.at[me])

    inputs = tokens_ref[...].astype(f32)
    normed_ref[...] = (inputs * norm_scale(inputs) * gain_one_ref[...].astype(f32).reshape(1, width)).astype(bf16)
    row, start, _ = rows_of(lengths_ref, (rows, 128))
    lane = lax.broadcasted_iota(jnp.int32, (rows, 128), 1)
    frequency = jnp.exp(
        lax.rem(lane, HEAD_SIZE // 2).astype(f32) * (-2.0 * math.log(ROPE_BASE) / HEAD_SIZE)
    )
    angle = (row - start).astype(f32) * frequency
    cosine_ref[...] = jnp.cos(angle)
    sine = jnp.sin(angle)
    sine_ref[...] = jnp.where(lax.rem(lane, HEAD_SIZE) < HEAD_SIZE // 2, -sine, sine)
    square = (rows, rows)
    across_row = lax.broadcasted_iota(jnp.int32, square, 0)
    across_col = lax.broadcasted_iota(jnp.int32, square, 1)
    earlier = (across_row > across_col).astype(bf16)
    expert = lax.broadcasted_iota(jnp.int32, (128, rows), 0)
    named = expert < 0
    for k in range(routes_ref.shape[0]):
        named = named | (routes_ref[k : k + 1, :] == expert)
    token = lax.broadcasted_iota(jnp.int32, (128, rows), 1)
    used = named & (token < lengths_ref[0, 0] + lengths_ref[0, 1])
    rank = contract(used.astype(bf16), earlier, 1, 1)
    place_of = jnp.where(used, rank, -1.0)
    eye = unit(rows)
    named = contract(eye, named.astype(bf16), 1, 1) > 0.5
    one.first()
    two.first()
    three.begin()
    one.second()
    two.second()
    one.third()
    one.complete()
    stores.add(all_qkv, all_qkv_out)

    normed = normed_ref[...]
    cosine, signed = cosine_ref[...], sine_ref[...]
    for tile in range(4):
        lanes = pl.ds(tile * 512, 512)
        part = contract(normed, flat(all_qkv, lanes), 1, 0)
        if tile < 3:
            part = turn(part, jnp.tile(cosine, (1, 4)), jnp.tile(signed, (1, 4)))
        qkv_ref[:, lanes] = part.astype(bf16)
    two.third()
    three.first()
    _, start_row, _ = rows_of(lengths_ref, square)
    allowed = (across_col >= start_row) & (across_col <= across_row)
    both = jnp.concatenate([allowed, allowed], axis=0)
    for g in range(KEY_VALUE_HEADS):
        if g == 4:
            three.second()
        key = qkv_ref[:, pl.ds(width + g * HEAD_SIZE, HEAD_SIZE)]
        value = qkv_ref[:, pl.ds(width + half + g * HEAD_SIZE, HEAD_SIZE)]
        query = jnp.concatenate(
            [qkv_ref[:, pl.ds((2 * g + p) * HEAD_SIZE, HEAD_SIZE)] for p in range(2)], axis=0
        )
        scores = jnp.where(both, contract(query, key, 1, 1) * HEAD_SIZE**-0.5, NEGATIVE)
        raised = jnp.exp(scores - jnp.max(scores, axis=1, keepdims=True))
        prob = raised / jnp.sum(raised, axis=1, keepdims=True)
        prob_ref[g] = prob
        mixed = contract(prob.astype(bf16), value, 1, 0).astype(bf16)
        for p in range(2):
            mixed_ref[:, pl.ds((2 * g + p) * HEAD_SIZE, HEAD_SIZE)] = mixed[
                p * rows : (p + 1) * rows
            ]
    two.complete()
    three.third()
    for source, target in (
        (all_out, all_out_out), (normed_ref, normed_out), (qkv_ref, qkv_out),
        (mixed_ref, mixed_out), (prob_ref, prob_out), (cosine_ref, cosine_out),
        (sine_ref, sine_out),
    ):
        stores.add(source, target)
    _, _, live = rows_of(lengths_ref, (rows, 1))
    hidden = inputs + live.astype(f32) * contract(
        mixed_ref[...], flat(all_out, pl.ds(0, width)), 1, 0
    )
    hidden_ref[...] = hidden
    stores.add(hidden_ref, hidden_out)
    normed_two = (hidden * norm_scale(hidden) * gain_two_ref[...].astype(f32).reshape(1, width)).astype(bf16)
    payload_ref[pl.ds(0, rows), :] = normed_two
    logits = contract(normed_two, flat(all_out, pl.ds(width, 128)), 1, 0)
    logits = jnp.where(named, logits, NEGATIVE)
    raised = jnp.exp(logits - jnp.max(logits, axis=1, keepdims=True))
    gates = raised / jnp.sum(raised, axis=1, keepdims=True)
    gates_ref[...] = gates
    upper = gates.astype(bf16)
    lower = (gates - upper.astype(f32)).astype(bf16)
    tail = pl.ds(rows, E)
    payload_ref[tail, :] = jnp.zeros((E, width), bf16)
    for spot, table in enumerate((upper, lower)):
        payload_ref[tail, pl.ds(spot * 256, rows)] = contract(table, eye, 0, 0)[:E].astype(bf16)
    payload_ref[tail, pl.ds(512, rows)] = place_of[:E].astype(bf16)
    stores.add(gates_ref, gates_out)
    stores.add(payload_ref, payload_out)
    stores.wait(*range(12))
    three.complete()
    one.finish()
    two.finish()
    three.finish()


def front_layer(
    tokens, lengths, routes, gain_one, gain_two, query, key, value, output, router, cotangent,
    collective_id,
):
    rows, width = tokens.shape
    share = query.shape[0]
    f32, bf16 = jnp.float32, jnp.bfloat16
    dma = pltpu.SemaphoreType.DMA
    shape = jax.ShapeDtypeStruct
    kept = (
        shape((rows + E, width), bf16),
        shape((rows, width), f32),
        shape((rows, width), bf16),
        shape((rows, 2 * width), bf16),
        shape((rows, width), bf16),
        shape((KEY_VALUE_HEADS, 2 * rows, rows), f32),
        shape((rows, 128), f32),
        shape((rows, 128), f32),
        shape((rows, 128), f32),
        shape((16, share, 2 * width), bf16),
        shape((16, share, width + 256), bf16),
    )
    anywhere = pl.BlockSpec(memory_space=pl.ANY)
    inputs = (
        tokens, lengths, routes.T, gain_one, gain_two, query, key, value, output, router.T,
        cotangent,
    )
    taken = [inputs[place] for place in (0, 2, 3, 4, 9, 10)]
    return pl.pallas_call(
        front_kernel,
        out_shape=(*kept, shape((16, rows, width), bf16)),
        in_specs=[anywhere, pl.BlockSpec(memory_space=pltpu.SMEM)] + [anywhere] * 9,
        out_specs=(anywhere,) * 12,
        scratch_shapes=[pltpu.VMEM(value.shape, value.dtype) for value in (*taken, *kept)]
        + [dma((10,)), dma((12,))] + [dma((22,))] * 6,
        compiler_params=pltpu.CompilerParams(
            collective_id=collective_id, has_side_effects=True, vmem_limit_bytes=62 * 1024 * 1024
        ),
        cost_estimate=pl.CostEstimate(
            flops=24 * 10**9, bytes_accessed=10**8, transcendentals=10**6
        ),
    )(*inputs)


def chip_of(step):
    _, _, _, y, high = place()
    side, rise = select(SIDE_OF_STEP, step), select(UP_OF_STEP, step)
    return lax.rem(high + side, 2) * 4 + lax.rem(y + rise, 4)


class Scatter:
    def __init__(self, source, sums, bufs, sems, split, local_sem=None, axis="shard"):
        self.source, self.sums, self.bufs, self.sems = source, sums, bufs, sems
        self.count, self.split, self.local_sem = bufs[5].shape[0], split, local_sem
        self.spots = Spots(axis)
        self.pending = {}

    def block(self, step):
        if self.sums is None:
            return self.source.at[self.spots.of_step(step)]
        return self.sums.at[step]

    def load(self, step):
        return pltpu.make_async_copy(
            self.source.at[self.spots.of_step(step)], self.sums.at[step], self.local_sem.at[step]
        )

    def swap(self, step):
        return pltpu.make_async_remote_copy(
            src_ref=self.source.at[self.spots.of_step(step, True)],
            dst_ref=self.bufs[0].at[step],
            send_sem=self.sems[0].at[step],
            recv_sem=self.sems[1].at[step],
            device_id=self.spots.targets["mate"],
            device_id_type=MESH,
        )

    def begin(self):
        for step in (7, 4, 6, 5, 2, 1, 3, 0):
            if self.spots.paired:
                self.swap(jnp.int32(step)).start()
            if self.sums is not None:
                self.load(jnp.int32(step)).start()

    def settle(self, step):
        step = jnp.int32(step)
        if self.sums is not None:
            self.load(step).wait()
        if self.spots.paired:
            self.swap(step).wait_recv()
            add_rows(self.block(step), self.bufs[0].at[step], 0, self.count)

    def send(self, number, source, target_ref, target):
        copy = pltpu.make_async_remote_copy(
            src_ref=source,
            dst_ref=target_ref,
            send_sem=self.sems[0].at[number],
            recv_sem=self.sems[1].at[number],
            device_id=self.spots.targets[target],
            device_id_type=MESH,
        )
        copy.start()
        self.pending[number] = copy

    def first(self, o):
        step = (7, 4)[o]
        self.settle(step)
        block = self.block(jnp.int32(step))
        spans = pl.ds(0, self.split), pl.ds(self.split, self.count - self.split)
        self.send(8 + o, block.at[spans[0]], self.bufs[3].at[o], "up")
        self.send(10 + o, block.at[spans[1]], self.bufs[4].at[o], "down")

    def second(self, o):
        above, below = (6, 2)[o], (5, 1)[o]
        self.settle(above)
        self.settle(below)
        above, below = self.block(jnp.int32(above)), self.block(jnp.int32(below))
        self.pending[8 + o].wait_recv()
        add_rows(above, self.bufs[3].at[o], 0, self.split)
        self.send(12 + o, above, self.bufs[1].at[o], "up")
        self.pending[10 + o].wait_recv()
        add_rows(below, self.bufs[4].at[o], self.split, self.count - self.split)
        self.send(14 + o, below, self.bufs[2].at[o], "down")

    def third(self, o):
        step = (3, 0)[o]
        self.settle(step)
        block = self.block(jnp.int32(step))
        self.pending[12 + o].wait_recv()
        add_rows(block, self.bufs[1].at[o], 0, self.count)
        self.pending[14 + o].wait_recv()
        add_rows(block, self.bufs[2].at[o], 0, self.count)
        if o == 0:
            self.send(16, block, self.bufs[5], "across")

    def last(self, emit):
        self.pending[16].wait_recv()
        own, beside = self.block(jnp.int32(0)), self.bufs[5]

        def body(step, carry):
            span = pl.ds(pl.multiple_of(step * 16, 16), 16)
            emit(span, own[span, :].astype(jnp.float32) + beside[span, :].astype(jnp.float32))
            return carry

        lax.fori_loop(0, self.count // 16, body, 0)

    def finish(self):
        for step in range(8 if self.spots.paired else 0):
            self.swap(jnp.int32(step)).wait_send()
        for copy in self.pending.values():
            copy.wait_send()


def scatter_scratch(count, width, split, swapped=8):
    kind = jnp.bfloat16
    return [
        pltpu.VMEM((swapped, count, width), kind),
        pltpu.VMEM((2, count, width), kind),
        pltpu.VMEM((2, count, width), kind),
        pltpu.VMEM((2, split, width), kind),
        pltpu.VMEM((2, count - split, width), kind),
        pltpu.VMEM((count, width), kind),
        pltpu.SemaphoreType.DMA((17,)),
        pltpu.SemaphoreType.DMA((17,)),
    ]


class Total:
    def __init__(self, source, out, pieces, sems, piece):
        self.source, self.out, self.pieces = source, out, pieces
        self.sems, self.piece = sems, piece
        self.shard, self.me = lax.axis_index("shard"), lax.axis_index("replica")

    def copy(self, way, step):
        target = lax.rem(self.me + step, 8)
        if way == 0:
            source, place_of = self.piece(self.source, target), self.pieces.at[step - 1]
        else:
            source = place_of = self.piece(self.out, self.me)
        return pltpu.make_async_remote_copy(
            src_ref=source,
            dst_ref=place_of,
            send_sem=self.sems[2 * way].at[step - 1],
            recv_sem=self.sems[2 * way + 1].at[step - 1],
            device_id=(self.shard, target),
            device_id_type=MESH,
        )

    def begin(self):
        for step in range(1, 8):
            self.copy(0, step).start()

    def middle(self):
        for step in range(1, 8):
            self.copy(0, step).wait_recv()
        own = self.piece(self.source, self.me)
        result = self.piece(self.out, self.me)

        def body(turn_of, carry):
            span = pl.ds(pl.multiple_of(turn_of * 16, 16), 16)
            total = own[span, :].astype(jnp.float32)
            for step in range(7):
                total = total + self.pieces[step, span, :].astype(jnp.float32)
            result[span, :] = total.astype(jnp.bfloat16)
            return carry

        lax.fori_loop(0, self.pieces.shape[1] // 16, body, 0)
        for step in range(1, 8):
            self.copy(1, step).start()

    def end(self):
        for step in range(1, 8):
            self.copy(1, step).wait_recv()

    def finish(self):
        for step in range(1, 8):
            self.copy(0, step).wait_send()
            self.copy(1, step).wait_send()


def total_scratch(rows, width):
    dma = pltpu.SemaphoreType.DMA
    return [pltpu.VMEM((7, rows, width), jnp.bfloat16), dma((7,)), dma((7,)), dma((7,)), dma((7,))]


def quarter(ref, which):
    half = ref.shape[1] // 2
    return ref.at[
        pl.ds(pl.multiple_of((which // 2) * 16, 16), 16),
        pl.ds(pl.multiple_of(lax.rem(which, 2) * half, 128), half),
    ]


def norm_back(value, scale, gain, grad):
    gained = grad * gain
    return scale * gained - value * scale**3 * jnp.mean(gained * value, axis=1, keepdims=True)


def rear_kernel(
    lengths_ref, tokens_any, cotangent_any, gain_one_any, gain_two_any, payload_any, hidden_any,
    normed_any, qkv_any, mixed_any, prob_any, gates_any, cosine_any, sine_any, all_qkv_any,
    all_out_any, back_any, mixes_ref, grads_ref,
    output_ref, d_tokens_ref, one_total, two_total, d_expert_ref,
    tokens_ref, cotangent_ref, gain_one_ref, gain_two_ref, payload_ref, hidden_ref,
    normed_ref, qkv_ref, mixed_ref, prob_ref, gates_ref, cosine_ref, sine_ref, all_qkv,
    all_out, back_ref,
    *scratch,
):
    scratch = list(scratch)

    def take(count):
        taken = scratch[:count]
        del scratch[:count]
        return taken

    load_sem, own_sem = take(2)
    mix_sums, mix_local = take(2)
    mix_bufs, mix_sems = take(6), take(2)
    (one_blocks,) = take(1)
    one_bufs, one_sems = take(6), take(2)
    (two_blocks,) = take(1)
    two_bufs, two_sems = take(6), take(2)
    expert_sums, expert_local = take(2)
    expert_bufs, expert_sems = take(6), take(2)
    expert_own, spread_send, spread_recv = take(3)
    (one_pieces,), one_total_sems = take(1), take(4)
    (two_pieces,), two_total_sems = take(1), take(4)
    one_part, two_part = take(2)
    mixed_grad_ref, turned_ref, qkv_grad_ref, first_grad_ref, hidden_grad_ref = take(5)
    f32, bf16 = jnp.float32, jnp.bfloat16
    rows, width = tokens_ref.shape
    half = KEY_VALUE_HEADS * HEAD_SIZE
    shard, me = lax.axis_index("shard"), lax.axis_index("replica")
    loads = Loads(load_sem)
    early = (
        (back_any, back_ref), (hidden_any, hidden_ref), (gates_any, gates_ref),
        (cotangent_any, cotangent_ref), (gain_two_any, gain_two_ref), (all_out_any, all_out),
        (mixed_any, mixed_ref), (payload_any, payload_ref),
    )
    late = (
        (qkv_any, qkv_ref), (prob_any, prob_ref), (cosine_any, cosine_ref), (sine_any, sine_ref),
        (all_qkv_any, all_qkv), (normed_any, normed_ref), (tokens_any, tokens_ref),
        (gain_one_any, gain_one_ref),
    )
    for source, target in early + late:
        loads.add(source, target)
    greet(neighbours() + [(shard, lax.rem(me + step, 8)) for step in range(1, 8)])
    mixes = Scatter(mixes_ref, mix_sums, mix_bufs, mix_sems, 96, mix_local)
    one = Scatter(one_blocks, None, one_bufs, one_sems, 32)
    two = Scatter(two_blocks, None, two_bufs, two_sems, 32)
    experts = Scatter(
        grads_ref, expert_sums, expert_bufs, expert_sems, 96, expert_local, "replica"
    )
    spread = Gather(d_expert_ref, 96, 0, (spread_send, spread_recv), "replica", expert_own)
    one_sum = Total(one_part, one_total, one_pieces, one_total_sems, quarter)
    two_sum = Total(two_part, two_total, two_pieces, two_total_sems, quarter)
    mixes.begin()
    experts.begin()
    experts.first(0)
    experts.first(1)
    loads.wait(*range(len(early)))

    _, _, live = rows_of(lengths_ref, (rows, 1))
    live = live.astype(f32)
    eye = unit(rows)
    line = back_ref[pl.ds(rows, E), :]
    gap = jnp.zeros((128 - E, rows), bf16)

    def columns(part):
        return contract(eye, jnp.concatenate([part.astype(bf16), gap], axis=0), 1, 1)

    gate_grad = columns(line[:, :rows]) + columns(line[:, 256 : 256 + rows])
    gates = gates_ref[...]
    logit_grad = (gates * (gate_grad - jnp.sum(gates * gate_grad, axis=1, keepdims=True))).astype(
        bf16
    )
    second_grad = back_ref[pl.ds(0, rows), :] + contract(
        logit_grad, flat(all_out, pl.ds(width, 128)), 1, 1
    )
    hidden = hidden_ref[...]
    scale_two = norm_scale(hidden)
    d_gain_two = jnp.sum(second_grad * hidden * scale_two, axis=0, keepdims=True)
    hidden_grad = cotangent_ref[...].astype(f32) + norm_back(
        hidden, scale_two, gain_two_ref[...].astype(f32).reshape(1, width), second_grad
    )
    hidden_grad_ref[...] = hidden_grad
    attn_grad = (live * hidden_grad).astype(bf16)

    def weights_of(ref, tile, lanes):
        value = ref[4 * tile : 4 * tile + 4, :, :lanes]
        return value.reshape(256, lanes)

    for tile in range(4):
        span = pl.ds(tile * 256, 256)
        mixed_grad_ref[:, span] = contract(
            attn_grad, weights_of(all_out, tile, width), 1, 1
        ).astype(bf16)
        one_blocks[4 * tile : 4 * tile + 4, :, :width] = (
            contract(mixed_ref[:, span], attn_grad, 0, 0).astype(bf16).reshape(4, 64, width)
        )
        one_blocks[4 * tile : 4 * tile + 4, :, width : width + 128] = (
            contract(payload_ref[pl.ds(0, rows), span], logit_grad, 0, 0)
            .astype(bf16)
            .reshape(4, 64, 128)
        )
    one_blocks[:, :, width + 128 :] = jnp.zeros((16, 64, 128), bf16)
    one.begin()
    mixes.first(0)
    mixes.first(1)

    def heads(ref, g):
        return jnp.concatenate(
            [ref[:, pl.ds((2 * g + p) * HEAD_SIZE, HEAD_SIZE)] for p in range(2)], axis=0
        )

    def head_back(g):
        mixed_grad, query = heads(mixed_grad_ref, g), heads(qkv_ref, g)
        key = qkv_ref[:, pl.ds(width + g * HEAD_SIZE, HEAD_SIZE)]
        value = qkv_ref[:, pl.ds(width + half + g * HEAD_SIZE, HEAD_SIZE)]
        prob = prob_ref[g]
        prob_grad = contract(mixed_grad, value, 1, 1)
        qkv_grad_ref[:, pl.ds(width + half + g * HEAD_SIZE, HEAD_SIZE)] = contract(
            prob.astype(bf16), mixed_grad, 0, 0
        ).astype(bf16)
        score_grad = prob * (prob_grad - jnp.sum(prob * prob_grad, axis=1, keepdims=True))
        score_grad = score_grad.astype(bf16)
        query_grad = contract(score_grad, key, 1, 0) * HEAD_SIZE**-0.5
        for p in range(2):
            turned_ref[:, pl.ds((2 * g + p) * HEAD_SIZE, HEAD_SIZE)] = query_grad[
                p * rows : (p + 1) * rows
            ]
        turned_ref[:, pl.ds(width + g * HEAD_SIZE, HEAD_SIZE)] = (
            contract(score_grad, query, 0, 0) * HEAD_SIZE**-0.5
        )

    loads.wait(*range(len(early), len(early + late)))
    for g in range(2):
        head_back(g)
    experts.second(0)
    for g in range(2, 4):
        head_back(g)
    mixes.second(0)
    for g in range(4, 6):
        head_back(g)
    experts.second(1)
    mixes.second(1)
    one.first(0)
    one.first(1)
    for g in range(6, 8):
        head_back(g)
    cosine, signed = cosine_ref[...], -sine_ref[...]
    for tile in range(3):
        lanes = pl.ds(tile * 512, 512)
        qkv_grad_ref[:, lanes] = turn(
            turned_ref[:, lanes], jnp.tile(cosine, (1, 4)), jnp.tile(signed, (1, 4))
        ).astype(bf16)
    mixes.third(0)
    qkv_grad = qkv_grad_ref[...]
    for tile in range(4):
        span = pl.ds(tile * 256, 256)
        first_grad_ref[:, span] = contract(qkv_grad, weights_of(all_qkv, tile, 2 * width), 1, 1)
        two_blocks[4 * tile : 4 * tile + 4, :, : 2 * width] = (
            contract(normed_ref[:, span], qkv_grad, 0, 0).astype(bf16).reshape(4, 64, 2 * width)
        )
    inputs = tokens_ref[...].astype(f32)
    scale_one = norm_scale(inputs)
    first_grad = first_grad_ref[...]
    d_gain_one = jnp.sum(first_grad * inputs * scale_one, axis=0, keepdims=True)
    two_blocks[:, :, 2 * width :] = jnp.zeros((16, 64, 256), bf16)
    pieces = [
        gain[:, 128 * part : 128 * part + 128]
        for gain in (d_gain_one, d_gain_two)
        for part in range(8)
    ]
    gain_tile = jnp.concatenate(pieces, axis=0).astype(bf16)
    for block in range(16):
        two_blocks[block, pl.ds(0, 16), pl.ds(2 * width, 128)] = gain_tile
    two.begin()
    experts.third(0)
    one.second(0)
    mixes.third(1)
    one.second(1)
    two.first(0)
    two.first(1)
    experts.third(1)
    d_tokens_ref[...] = hidden_grad_ref[...] + norm_back(
        inputs, scale_one, gain_one_ref[...].astype(f32).reshape(1, width), first_grad
    )

    def give_output(span, value):
        row = lax.broadcasted_iota(jnp.int32, (16, 1), 0) + span.start
        alive = (row < lengths_ref[0, 0] + lengths_ref[0, 1]).astype(f32)
        output_ref[span, :] = (hidden_ref[span, :] + alive * value).astype(bf16)

    def give(ref):
        def emit(span, value):
            ref[span, :] = value.astype(bf16)

        return emit

    experts.last(give(expert_own))
    own_store = pltpu.make_async_copy(expert_own, d_expert_ref.at[me], own_sem)
    own_store.start()
    spread.begin()
    mixes.last(give_output)

    one.third(0)
    two.second(0)
    one.third(1)
    two.second(1)
    spread.first()
    one.last(give(one_part))
    one_sum.begin()
    two.third(0)
    two.third(1)
    spread.second()
    one_sum.middle()
    two.last(give(two_part))
    two_sum.begin()
    one_sum.end()
    two_sum.middle()
    spread.third()
    two_sum.end()
    spread.complete()
    own_store.wait()
    for user in (mixes, one, two, experts, spread, one_sum, two_sum):
        user.finish()


def rear_layer(
    tokens, lengths, cotangent, gain_one, gain_two, kept, back, mixes, grads, collective_id
):
    rows, width = tokens.shape
    f32, bf16 = jnp.float32, jnp.bfloat16
    vmem = pl.BlockSpec(memory_space=pltpu.VMEM)
    anywhere = pl.BlockSpec(memory_space=pl.ANY)
    dma = pltpu.SemaphoreType.DMA
    shape = jax.ShapeDtypeStruct
    wide_one, wide_two = width + 256, 2 * width + 256
    slab = grads.shape[0] // 8
    inputs = (tokens, cotangent, gain_one, gain_two, *kept, back)
    return pl.pallas_call(
        rear_kernel,
        out_shape=(
            shape((rows, width), bf16),
            shape((rows, width), f32),
            shape((64, wide_one), bf16),
            shape((64, wide_two), bf16),
            shape((8, slab, width), bf16),
        ),
        in_specs=[pl.BlockSpec(memory_space=pltpu.SMEM)] + [anywhere] * (len(inputs) + 2),
        out_specs=(vmem,) * 4 + (anywhere,),
        scratch_shapes=[
            *(pltpu.VMEM(value.shape, value.dtype) for value in inputs),
            dma((len(inputs),)),
            dma,
            pltpu.VMEM((8, rows, width), bf16),
            dma((8,)),
            *scatter_scratch(rows, width, 96),
            pltpu.VMEM((16, 64, wide_one), bf16),
            *scatter_scratch(64, wide_one, 32),
            pltpu.VMEM((16, 64, wide_two), bf16),
            *scatter_scratch(64, wide_two, 32),
            pltpu.VMEM((8, slab, width), bf16),
            dma((8,)),
            *scatter_scratch(slab, width, 96, 1),
            pltpu.VMEM((slab, width), bf16),
            dma((22,)),
            dma((22,)),
            *total_scratch(16, wide_one // 2),
            *total_scratch(16, wide_two // 2),
            pltpu.VMEM((64, wide_one), bf16),
            pltpu.VMEM((64, wide_two), bf16),
            pltpu.VMEM((rows, width), bf16),
            pltpu.VMEM((rows, width + KEY_VALUE_HEADS * HEAD_SIZE), f32),
            pltpu.VMEM((rows, 2 * width), bf16),
            pltpu.VMEM((rows, width), f32),
            pltpu.VMEM((rows, width), f32),
        ],
        compiler_params=pltpu.CompilerParams(
            collective_id=collective_id, has_side_effects=True, vmem_limit_bytes=62 * 1024 * 1024
        ),
        cost_estimate=pl.CostEstimate(
            flops=24 * 10**9, bytes_accessed=10**8, transcendentals=10**6
        ),
    )(lengths, *inputs, mixes, grads.reshape(8, slab, width))


def close_kernel(
    output_any, d_tokens_any, one_any, two_any, expert_any,
    output_out, d_tokens_out, d_gain_one_out, d_gain_two_out, d_query_out, d_key_out,
    d_value_out, d_output_out, d_router_out, d_in_out, d_out_out,
    output_ref, d_tokens_ref, one_ref, two_ref, expert_ref, query_ref, key_ref, value_ref,
    matrix_ref, wide_ref,
    router_ref, gain_one_ref, gain_two_ref, load_sem, store_sem,
):
    f32 = jnp.float32
    width = query_ref.shape[1]
    half = key_ref.shape[1]
    loads, stores = Loads(load_sem), Loads(store_sem)
    parts = expert_ref.shape[0] // 256
    spans = [pl.ds(256 * part, 256) for part in range(parts)]
    loads.add(one_any, one_ref)
    loads.add(two_any, two_ref)
    for span in spans:
        loads.add(expert_any.at[span], expert_ref.at[span])
    loads.add(output_any, output_ref)
    loads.add(d_tokens_any, d_tokens_ref)
    loads.wait(0, 1)
    query_ref[...] = two_ref[:, pl.ds(0, width)].astype(f32)
    key_ref[...] = two_ref[:, pl.ds(width, half)].astype(f32)
    value_ref[...] = two_ref[:, pl.ds(width + half, half)].astype(f32)
    matrix_ref[...] = one_ref[:, pl.ds(0, width)].astype(f32)
    router_ref[...] = contract(one_ref[:, pl.ds(width, 128)], unit(64), 0, 0)[:E]
    gains = two_ref[pl.ds(0, 16), pl.ds(2 * width, 128)].astype(f32)
    gain_one_ref[...] = gains[:8]
    gain_two_ref[...] = gains[8:]
    for source, target in (
        (query_ref, d_query_out), (key_ref, d_key_out), (value_ref, d_value_out),
        (matrix_ref, d_output_out), (router_ref, d_router_out),
        (gain_one_ref, d_gain_one_out), (gain_two_ref, d_gain_two_out),
    ):
        stores.add(source, target)
    for part, span in enumerate(spans):
        loads.wait(2 + part)
        wide_ref[span, :] = expert_ref[span, :].astype(f32)
        if part < width // 256:
            stores.add(wide_ref.at[span], d_in_out.at[span])
        else:
            stores.add(wide_ref.at[span], d_out_out.at[pl.ds(256 * part - width, 256)])
    loads.wait(2 + parts, 3 + parts)
    stores.add(output_ref, output_out)
    stores.add(d_tokens_ref, d_tokens_out)
    stores.wait(*range(9 + parts))


def close_layer(output, d_tokens, one, two, expert):
    rows, width = output.shape
    half = KEY_VALUE_HEADS * HEAD_SIZE
    hidden = expert.shape[0] - width
    f32 = jnp.float32
    shape = jax.ShapeDtypeStruct
    small = (
        (64, width), (64, half), (64, half), (64, width), (E, 64), (8, 128), (8, 128),
    )
    dma = pltpu.SemaphoreType.DMA
    anywhere = pl.BlockSpec(memory_space=pl.ANY)
    query, key, value, matrix, router, gain_one, gain_two = small
    outs = (gain_one, gain_two, query, key, value, matrix, router, (width, width), (hidden, width))
    return pl.pallas_call(
        close_kernel,
        out_shape=(
            shape(output.shape, output.dtype),
            shape(d_tokens.shape, f32),
            *(shape(extent, f32) for extent in outs),
        ),
        in_specs=[anywhere] * 5,
        out_specs=(anywhere,) * 11,
        scratch_shapes=[
            pltpu.VMEM(output.shape, output.dtype),
            pltpu.VMEM(d_tokens.shape, f32),
            pltpu.VMEM(one.shape, one.dtype),
            pltpu.VMEM(two.shape, two.dtype),
            pltpu.VMEM(expert.shape, expert.dtype),
            pltpu.VMEM(query, f32),
            pltpu.VMEM(key, f32),
            pltpu.VMEM(value, f32),
            pltpu.VMEM(matrix, f32),
            pltpu.VMEM(expert.shape, f32),
            pltpu.VMEM(router, f32),
            pltpu.VMEM(gain_one, f32),
            pltpu.VMEM(gain_two, f32),
            dma((4 + expert.shape[0] // 256,)),
            dma((9 + expert.shape[0] // 256,)),
        ],
        compiler_params=pltpu.CompilerParams(vmem_limit_bytes=62 * 1024 * 1024),
        cost_estimate=pl.CostEstimate(flops=0, bytes_accessed=12 * 10**6, transcendentals=0),
    )(output, d_tokens, one, two, expert)


def local(
    tokens,
    seq_lengths,
    routes,
    attn_gain,
    ffn_gain,
    w_query,
    key_projection,
    value_projection,
    w_output,
    w_router,
    w_in,
    w_out,
    cotangent,
):
    rows, width = tokens.shape
    payload, *kept, all_cotangent = front_layer(
        tokens, seq_lengths, routes, attn_gain, ffn_gain,
        w_query, key_projection, value_projection, w_output, w_router, cotangent, 1,
    )
    back, mixes, expert_grads = expert_layer(payload, all_cotangent, w_in[0], w_out[0], 2)
    output, d_tokens, one, two, expert_grads = rear_layer(
        tokens, seq_lengths, cotangent, attn_gain, ffn_gain, (payload, *kept), back, mixes,
        expert_grads, 3,
    )
    (
        output, d_tokens, d_attn_gain, d_ffn_gain, d_query, d_key, d_value, d_output, d_router,
        d_in, d_out,
    ) = close_layer(output, d_tokens, one, two, expert_grads.reshape(-1, width))
    return (
        output,
        d_tokens,
        d_attn_gain.reshape(width),
        d_ffn_gain.reshape(width),
        d_query,
        d_key,
        d_value,
        d_output,
        d_router.T,
        d_in[None],
        d_out[None],
    )


def solution(mesh):
    return jax.shard_map(
        local,
        mesh=mesh,
        in_specs=(
            P(("shard", "replica"), None),
            P(("shard", "replica"), None),
            P(("shard", "replica"), None),
            P(),
            P(),
            P("shard", None),
            P("shard", None),
            P("shard", None),
            P("shard", None),
            P("shard", None),
            P("shard", None, None),
            P("shard", None, None),
            P(("shard", "replica"), None),
        ),
        out_specs=(
            P(("shard", "replica"), None),
            P(("shard", "replica"), None),
            P(),
            P(),
            P("shard", None),
            P("shard", None),
            P("shard", None),
            P("shard", None),
            P("shard", None),
            P("shard", None, None),
            P("shard", None, None),
        ),
        check_vma=False,
    )
```

```python
import functools
import math

import jax
import jax.numpy as jnp
from jax import lax
from jax.experimental import pallas as pl
from jax.experimental.pallas import tpu as pltpu
from jax.sharding import PartitionSpec as P

QUERY_HEADS = 16
KEY_VALUE_HEADS = 8
HEAD_SIZE = 64
H = 512
E = 16
CAP = 120

EPS = 1e-06
ROPE_BASE = 10000.0
NEGATIVE = -1e30

MESH = pl.DeviceIdType.MESH


def place():
    me = lax.axis_index("shard")
    rep = lax.axis_index("replica")
    core = lax.rem(me, 2)
    y = lax.rem(me // 2, 4)
    high = me // 8
    return me, rep, core, y, high


def index_of(high, y, core):
    return (high * 4 + lax.rem(y, 4)) * 2 + core


def greet(targets):
    barrier = pltpu.get_barrier_semaphore()
    for target in targets:
        pl.semaphore_signal(barrier, inc=1, device_id=target, device_id_type=MESH)
    pl.semaphore_wait(barrier, len(targets))


def add_rows(target, source, start, count):
    def body(step, carry):
        at = pl.ds(pl.multiple_of(start + step * 16, 16), 16)
        here = pl.ds(pl.multiple_of(step * 16, 16), 16)
        target[at, :] = (
            target[at, :].astype(jnp.float32) + source[here, :].astype(jnp.float32)
        ).astype(target.dtype)
        return carry

    lax.fori_loop(0, count // 16, body, 0)


def contract(a, b, left, right):
    return lax.dot_general(
        a, b, (((left,), (right,)), ((), ())), preferred_element_type=jnp.float32
    )


UP_OF_STEP = (0, 3, 1, 0, 2, 3, 1, 2)
SIDE_OF_STEP = (0, 0, 0, 1, 0, 1, 1, 1)
SLOTS = 128


def select(table, step):
    value = jnp.int32(table[0])
    for place in range(1, len(table)):
        if table[place] != table[place - 1]:
            value = value + (table[place] - table[place - 1]) * jnp.minimum(
                jnp.maximum(step - (place - 1), 0), 1
            )
    return value


def expert_kernel(
    cut, payload_ref, mix_ref, w_in_ref, w_out_ref, back_ref, mixture_ref, grads_in_ref, grads_out_ref,
    arrived, mix_buf, w_in, w_out, blocks, weighted, rows_c, act_c, route_c, pre_c, mix_c, row_c,
    near_mate, near_up, near_down, far_up, far_down, cross, crossing,
    a_send, a_recv, sums_in, in_up, in_down, in_far_up, in_far_down, in_send, in_recv,
    half_sem, local_sem, mix_sem, store_sem, send_sem, recv_sem,
):
    me = lax.axis_index("shard")
    width = payload_ref.shape[1]
    rows = payload_ref.shape[0]
    tokens = rows - 16
    load_in = pltpu.make_async_copy(w_in_ref, w_in, local_sem.at[0])
    load_out = pltpu.make_async_copy(w_out_ref, w_out, local_sem.at[1])
    load_own = pltpu.make_async_copy(payload_ref, arrived.at[me], local_sem.at[2])
    load_in.start()
    load_out.start()
    load_own.start()

    def load_mix(step):
        slot = lax.rem(step, 2)
        return pltpu.make_async_copy(
            mix_ref.at[pl.ds(chip_of(step) * 2, 2)], mix_buf.at[slot], mix_sem.at[slot]
        )

    load_mix(0).start()
    ring = Spots("replica").targets
    greet(neighbours() + [ring["up"], ring["down"]])
    gather = Gather(arrived, cut, 96, (send_sem, recv_sem), own=payload_ref)
    gather.begin()
    load_in.wait()
    load_out.wait()
    load_own.wait()

    def picks(slot):
        side = arrived[slot, pl.ds(tokens, 16), :].astype(jnp.float32)
        line = lax.broadcasted_iota(jnp.int32, side.shape, 0)
        own = jnp.sum(jnp.where(line == me, side, 0.0), axis=0, keepdims=True)
        gates = own[:, :tokens] + own[:, 256 : 256 + tokens]
        place_of = own[:, 512 : 512 + tokens].astype(jnp.int32)
        pick = place_of == lax.broadcasted_iota(jnp.int32, (SLOTS, tokens), 0)
        return pick, gates

    a = Scatter(
        blocks, None, (near_mate, near_up, near_down, far_up, far_down, cross, crossing), (a_send, a_recv),
        cut, 96,
    )

    def work(step, carry):
        @pl.when(step == 0)
        def _():
            gather.arrive(3)

        @pl.when(step == 1)
        def _():
            gather.first()
            gather.arrive(8)

        @pl.when(step == 2)
        def _():
            gather.arrive(9)

        @pl.when(step == 3)
        def _():
            gather.arrive(10)

        @pl.when(step == 4)
        def _():
            gather.second()
            gather.arrive(15, 16)

        @pl.when(step == 5)
        def _():
            gather.arrive(13)

        @pl.when(step == 6)
        def _():
            gather.arrive(14)

        @pl.when(step == 7)
        def _():
            gather.third()
            gather.arrive(17, 18)

        @pl.when(step < 7)
        def _():
            load_mix(step + 1).start()

        load_mix(step).wait()
        buffer = lax.rem(step, 2)
        base = chip_of(step) * 2
        both = 2 * SLOTS
        at = pl.ds(pl.multiple_of(chip_of(step) * both, both), both)
        kept = []
        for b in range(2):
            pick, gates = picks(base + b)
            pick_b = pick.astype(jnp.bfloat16)
            slot_gates = jnp.sum(jnp.where(pick, gates, 0.0), axis=1, keepdims=True)
            here = pl.ds(b * SLOTS, SLOTS)
            there = pl.ds(pl.multiple_of(chip_of(step) * both + b * SLOTS, SLOTS), SLOTS)
            rows_c[there, :] = contract(
                pick_b, arrived[base + b, pl.ds(0, tokens), :], 1, 0
            ).astype(jnp.bfloat16)
            mix_rows = contract(pick_b, mix_buf[buffer, b], 1, 0)
            mix_c[here, :] = mix_rows.astype(jnp.bfloat16)
            route_c[there, :] = (slot_gates * mix_rows).astype(jnp.bfloat16)
            kept.append((pick, pick_b, slot_gates))
        slot_gates = jnp.concatenate([kept[0][2], kept[1][2]], axis=0)
        x, route = rows_c[at, :], route_c[at, :]

        def inner(tile, carry):
            left = pl.ds(pl.multiple_of(tile * 256, 256), 256)
            right = pl.ds(pl.multiple_of(512 + tile * 256, 256), 256)
            gate = contract(x, w_in[:, left], 1, 0)
            raised = contract(x, w_in[:, right], 1, 0)
            grad = contract(route, w_out[left, :], 1, 1)
            sig = 1.0 / (1.0 + jnp.exp(-gate))
            silu = gate * sig
            act_c[at, left] = (silu * raised).astype(jnp.bfloat16)
            pre_c[at, left] = (grad * raised * sig * (1.0 + gate * (1.0 - sig))).astype(
                jnp.bfloat16
            )
            pre_c[at, right] = (grad * silu).astype(jnp.bfloat16)
            return carry

        lax.fori_loop(0, 2, inner, 0)
        act, pre = act_c[at, :], pre_c[at, :]

        def outer(tile, total):
            span = pl.ds(pl.multiple_of(tile * 256, 256), 256)
            result = contract(act, w_out[:, span], 1, 0).astype(jnp.bfloat16).astype(jnp.float32)
            weighted[at, span] = (slot_gates * result).astype(jnp.bfloat16)
            row_c[:, span] = contract(pre, w_in[span, :], 1, 1).astype(jnp.bfloat16)
            return total + jnp.sum(
                result * mix_c[:, span].astype(jnp.float32), axis=1, keepdims=True
            )

        gate_grad = lax.fori_loop(0, 4, outer, jnp.zeros((both, 1), jnp.float32))
        for b in range(2):
            pick, pick_b, _ = kept[b]
            here = pl.ds(b * SLOTS, SLOTS)
            blocks[base + b, pl.ds(0, tokens), :] = contract(pick_b, row_c[here, :], 0, 0).astype(
                jnp.bfloat16
            )
            line_grad = jnp.sum(
                jnp.where(pick, gate_grad[b * SLOTS : (b + 1) * SLOTS], 0.0), axis=0, keepdims=True
            )
            upper = line_grad.astype(jnp.bfloat16).astype(jnp.float32)
            mine = lax.broadcasted_iota(jnp.int32, (16, tokens), 0) == me
            tail = pl.ds(tokens, 16)
            blocks[base + b, tail, :] = jnp.zeros((16, width), jnp.bfloat16)
            blocks[base + b, tail, pl.ds(0, tokens)] = jnp.where(mine, upper, 0.0).astype(
                jnp.bfloat16
            )
            blocks[base + b, tail, pl.ds(256, tokens)] = jnp.where(
                mine, line_grad - upper, 0.0
            ).astype(jnp.bfloat16)
        a.swap(step).start()
        return carry

    lax.fori_loop(0, 8, work, 0)
    gather.finish()

    matrix = Scatter(
        sums_in, None, (None, in_up, in_down, in_far_up, in_far_down, None, None),
        (in_send, in_recv), sums_in.shape[1] // 2, 0, None, "replica",
    )
    a.first(0)
    a.first(1)

    def store(step):
        chip = chip_of(step) * 2
        return pltpu.make_async_copy(
            arrived.at[pl.ds(chip, 2), pl.ds(0, tokens)],
            mixture_ref.at[pl.ds(chip, 2)],
            store_sem.at[step],
        )

    def spread(step, carry):
        for b in range(2):
            slot = chip_of(step) * 2 + b
            pick, _ = picks(slot)
            here = pl.ds(pl.multiple_of(slot * SLOTS, SLOTS), SLOTS)
            arrived[slot, pl.ds(0, tokens), :] = contract(
                pick.astype(jnp.bfloat16), weighted[here, :], 0, 0
            ).astype(jnp.bfloat16)
        store(step).start()
        return carry

    def grad_in(tile, carry):
        span = pl.ds(pl.multiple_of(tile * 256, 256), 256)
        slab = sums_in.shape[1]
        sums_in[pl.ds(tile * (256 // slab), 256 // slab)] = (
            contract(rows_c[:, span], pre_c[...], 0, 0)
            .astype(jnp.bfloat16)
            .reshape(256 // slab, slab, width)
        )
        return carry

    def grad_out(tile, carry):
        span = pl.ds(pl.multiple_of(tile * 256, 256), 256)
        grads_out_ref[span, :] = contract(act_c[:, span], route_c[...], 0, 0).astype(jnp.bfloat16)
        return carry

    def give_back(span, value):
        back_ref[span, :] = value

    lax.fori_loop(0, 4, grad_in, 0)
    matrix.first(0)
    matrix.first(1)
    a.second(0)
    a.second(1)
    lax.fori_loop(0, 8, spread, 0)
    matrix.second(0)
    matrix.second(1)
    lax.fori_loop(0, 2, grad_out, 0)
    a.third(0)
    matrix.third(0)
    matrix.third(1)
    halves = [
        pltpu.make_async_copy(
            matrix.block(jnp.int32(step)), grads_in_ref.at[place_of], half_sem.at[place_of]
        )
        for place_of, step in enumerate((0, 3))
    ]
    for copy in halves:
        copy.start()
    a.third(1)
    a.last(give_back)
    a.finish()
    matrix.finish()
    for copy in halves:
        copy.wait()

    def stored(step, carry):
        store(step).wait()
        return carry

    lax.fori_loop(0, 8, stored, 0)


def expert_layer(payload, mix, w_in, w_out, collective_id):
    rows, width = payload.shape
    tokens = rows - 16
    hidden = w_out.shape[0]
    cut = (rows // 16 + 1) // 2 * 16
    kind = jnp.bfloat16
    slots = 16 * SLOTS
    dma = pltpu.SemaphoreType.DMA

    return pl.pallas_call(
        functools.partial(expert_kernel, cut),
        out_shape=(
            jax.ShapeDtypeStruct((rows, width), jnp.float32),
            jax.ShapeDtypeStruct((16, tokens, width), kind),
            jax.ShapeDtypeStruct((2, width // 8, width), kind),
            jax.ShapeDtypeStruct((hidden, width), kind),
        ),
        in_specs=[
            pl.BlockSpec(memory_space=pl.ANY),
            pl.BlockSpec(memory_space=pl.ANY),
            pl.BlockSpec(memory_space=pl.ANY),
            pl.BlockSpec(memory_space=pl.ANY),
        ],
        out_specs=(
            pl.BlockSpec(memory_space=pltpu.VMEM),
            pl.BlockSpec(memory_space=pl.ANY),
            pl.BlockSpec(memory_space=pl.ANY),
            pl.BlockSpec(memory_space=pltpu.VMEM),
        ),
        scratch_shapes=[
            pltpu.VMEM((16, rows, width), kind),
            pltpu.VMEM((2, 2, tokens, width), kind),
            pltpu.VMEM((width, 2 * hidden), kind),
            pltpu.VMEM((hidden, width), kind),
            pltpu.VMEM((16, rows, width), kind),
            pltpu.VMEM((slots, width), kind),
            pltpu.VMEM((slots, width), kind),
            pltpu.VMEM((slots, hidden), kind),
            pltpu.VMEM((slots, width), kind),
            pltpu.VMEM((slots, 2 * hidden), kind),
            pltpu.VMEM((2 * SLOTS, width), kind),
            pltpu.VMEM((2 * SLOTS, width), kind),
            *scatter_scratch(rows, width, cut, 96),
            pltpu.VMEM((8, width // 8, width), kind),
            pltpu.VMEM((2, width // 8, width), kind),
            pltpu.VMEM((2, width // 8, width), kind),
            pltpu.VMEM((2, width // 16, width), kind),
            pltpu.VMEM((2, width // 16, width), kind),
            dma((20,)),
            dma((20,)),
            dma((2,)),
            dma((3,)),
            dma((2,)),
            dma((8,)),
            dma((22,)),
            dma((22,)),
        ],
        compiler_params=pltpu.CompilerParams(
            collective_id=collective_id, has_side_effects=True, vmem_limit_bytes=62 * 1024 * 1024
        ),
        cost_estimate=pl.CostEstimate(
            flops=24 * 10**9, bytes_accessed=10**8, transcendentals=10**6
        ),
    )(payload, mix, w_in, w_out)


class Spots:
    def __init__(self, axis):
        me, rep, core, y, high = place()
        self.paired = axis == "shard"
        if self.paired:
            self.bits = (high, y, core)
            device = lambda slot: (slot, rep)
        else:
            self.bits = (rep // 4, lax.rem(rep, 4), None)
            device = lambda slot: (me, slot)
        self.targets = {
            "up": device(self.slot(0, 1)),
            "down": device(self.slot(0, 3)),
            "across": device(self.slot(1, 0)),
        }
        if self.paired:
            self.targets["mate"] = device(self.slot(0, 0, True))

    def slot(self, side, rise, swapped=False):
        high, ring, core = self.bits
        chip = lax.rem(high + side, 2) * 4 + lax.rem(ring + rise, 4)
        if not self.paired:
            return chip
        return 2 * chip + (1 - core if swapped else core)

    def of_step(self, step, swapped=False):
        return self.slot(select(SIDE_OF_STEP, step), select(UP_OF_STEP, step), swapped)


def neighbours():
    return list(Spots("shard").targets.values())


class Gather:
    def __init__(self, slots, split, crossed, sems, axis="shard", own=None):
        spots = Spots(axis)
        self.spots, self.slots, self.sems, self.own = spots, slots, sems, own
        rows = slots.shape[1]
        whole, top, low = pl.ds(0, rows), pl.ds(0, split), pl.ds(split, rows - split)
        half = (rows - crossed + 16) // 32 * 16 + crossed
        cross, late = pl.ds(0, crossed), pl.ds(crossed, rows - crossed)
        late_top, late_low = pl.ds(crossed, half - crossed), pl.ds(half, rows - half)
        self.crossed = crossed
        me, other, far = spots.slot(0, 0), spots.slot(1, 0), spots.slot(0, 2)
        from_down, from_up = spots.slot(0, 3), spots.slot(0, 1)
        other_down, other_up = spots.slot(1, 3), spots.slot(1, 1)
        other_far = spots.slot(1, 2)
        self.plan = (
            (me, whole, "across"),
            (me, whole, "up"),
            (me, whole, "down"),
            (me, whole, "mate"),
            (from_down, top, "up"),
            (from_up, low, "down"),
            (other, late, "up"),
            (other, late, "down"),
            (from_down, whole, "mate"),
            (from_up, whole, "mate"),
            (other, whole, "mate"),
            (other_down, late_top, "up"),
            (other_up, late_low, "down"),
            (other_down, whole, "mate"),
            (other_up, whole, "mate"),
            (far, top, "mate"),
            (far, low, "mate"),
            (other_far, pl.ds(0, half), "mate"),
            (other_far, late_low, "mate"),
            (from_down, cross, "across"),
            (from_up, cross, "across"),
            (far, cross, "across"),
        )

    def used(self, numbers):
        skipped = () if self.crossed else (19, 20, 21)
        return [n for n in numbers if n not in skipped and self.plan[n][2] in self.spots.targets]

    def move(self, number):
        slot, span, target = self.plan[number]
        target_ref = self.slots.at[slot, span]
        return pltpu.make_async_remote_copy(
            src_ref=self.own if self.own is not None and number < 4 else target_ref,
            dst_ref=target_ref,
            send_sem=self.sems[0].at[number],
            recv_sem=self.sems[1].at[number],
            device_id=self.spots.targets[target],
            device_id_type=MESH,
        )

    def start(self, *numbers):
        for number in self.used(numbers):
            self.move(number).start()

    def arrive(self, *numbers):
        for number in self.used(numbers):
            self.move(number).wait_recv()

    def begin(self):
        self.start(0, 1, 2, 3)

    def first(self):
        self.arrive(1)
        self.start(4, 19, 8)
        self.arrive(2)
        self.start(5, 20, 9)
        self.arrive(0)
        self.start(6, 7, 10)

    def second(self):
        self.arrive(4)
        self.start(21, 15)
        self.arrive(5)
        self.start(16)
        self.arrive(6)
        self.start(11)
        self.arrive(7)
        self.start(12)
        self.arrive(19)
        self.start(13)
        self.arrive(20)
        self.start(14)

    def third(self):
        self.arrive(11, 21)
        self.start(17)
        self.arrive(12)
        self.start(18)

    def complete(self):
        self.arrive(3, 8, 9, 10, 13, 14, 15, 16, 17, 18)

    def finish(self):
        for number in self.used(range(22)):
            self.move(number).wait_send()


def rows_of(lengths_ref, shape):
    row = lax.broadcasted_iota(jnp.int32, shape, 0)
    first = lengths_ref[0, 0]
    total = first + lengths_ref[0, 1]
    start = jnp.where(row < first, 0, jnp.where(row < total, first, total))
    return row, start, row < total


def turn(value, cosine, sine):
    width = value.shape[1]
    lane = lax.rem(lax.broadcasted_iota(jnp.int32, value.shape, 1), HEAD_SIZE)
    beside = jnp.where(
        lane < HEAD_SIZE // 2,
        pltpu.roll(value, width - HEAD_SIZE // 2, 1),
        pltpu.roll(value, HEAD_SIZE // 2, 1),
    )
    return value * cosine + beside * sine


def norm_scale(value):
    return lax.rsqrt(jnp.mean(value * value, axis=1, keepdims=True) + EPS)


def unit(size):
    return (
        lax.broadcasted_iota(jnp.int32, (size, size), 0)
        == lax.broadcasted_iota(jnp.int32, (size, size), 1)
    ).astype(jnp.bfloat16)


def flat(ref, lanes):
    value = ref[:, :, lanes]
    return value.reshape(value.shape[0] * value.shape[1], value.shape[2])


class Loads:
    def __init__(self, sems):
        self.sems, self.copies = sems, []

    def add(self, source, target):
        copy = pltpu.make_async_copy(source, target, self.sems.at[len(self.copies)])
        copy.start()
        self.copies.append(copy)
        return copy

    def wait(self, *numbers):
        for number in numbers:
            self.copies[number].wait()


def front_kernel(
    tokens_any, lengths_ref, routes_any, gain_one_any, gain_two_any,
    query_any, key_any, value_any, output_any, router_any, cotangent_any,
    payload_out, hidden_out, normed_out, qkv_out, mixed_out, prob_out, gates_out,
    cosine_out, sine_out, all_qkv_out, all_out_out, all_cotangent,
    tokens_ref, routes_ref, gain_one_ref, gain_two_ref, router_ref, cotangent_ref,
    payload_ref, hidden_ref, normed_ref, qkv_ref, mixed_ref, prob_ref, gates_ref,
    cosine_ref, sine_ref, all_qkv, all_out,
    load_sem, store_sem, q_send, q_recv, o_send, o_recv, c_send, c_recv,
):
    me = lax.axis_index("shard")
    rows, width = tokens_ref.shape
    f32, bf16 = jnp.float32, jnp.bfloat16
    half = KEY_VALUE_HEADS * HEAD_SIZE
    loads, stores = Loads(load_sem), Loads(store_sem)
    loads.add(query_any, all_qkv.at[me, :, pl.ds(0, width)])
    loads.add(key_any, all_qkv.at[me, :, pl.ds(width, half)])
    loads.add(value_any, all_qkv.at[me, :, pl.ds(width + half, half)])
    loads.add(output_any, all_out.at[me, :, pl.ds(0, width)])
    loads.add(router_any, router_ref)
    loads.add(tokens_any, tokens_ref)
    loads.add(routes_any, routes_ref)
    loads.add(gain_one_any, gain_one_ref)
    loads.add(gain_two_any, gain_two_ref)
    loads.add(cotangent_any, cotangent_ref)
    greet(neighbours())
    one = Gather(all_qkv, 32, 32, (q_send, q_recv))
    two = Gather(all_out, 32, 32, (o_send, o_recv))
    three = Gather(all_cotangent, 96, 64, (c_send, c_recv), own=cotangent_ref)
    loads.wait(0, 1, 2)
    one.begin()
    loads.wait(4)
    pad = jnp.zeros((128 - E, router_ref.shape[1]), bf16)
    all_out[me, :, pl.ds(width, 128)] = contract(
        jnp.concatenate([router_ref[...], pad], axis=0), unit(128), 0, 0
    ).astype(bf16)
    all_out[me, :, pl.ds(width + 128, 128)] = jnp.zeros((router_ref.shape[1], 128), bf16)
    loads.wait(3)
    two.begin()
    loads.wait(5, 6, 7, 8, 9)
    three.begin()
    stores.add(cotangent_ref, all_cotangent.at[me])

    inputs = tokens_ref[...].astype(f32)
    normed_ref[...] = (inputs * norm_scale(inputs) * gain_one_ref[...].astype(f32).reshape(1, width)).astype(bf16)
    row, start, _ = rows_of(lengths_ref, (rows, 128))
    lane = lax.broadcasted_iota(jnp.int32, (rows, 128), 1)
    frequency = jnp.exp(
        lax.rem(lane, HEAD_SIZE // 2).astype(f32) * (-2.0 * math.log(ROPE_BASE) / HEAD_SIZE)
    )
    angle = (row - start).astype(f32) * frequency
    cosine_ref[...] = jnp.cos(angle)
    sine = jnp.sin(angle)
    sine_ref[...] = jnp.where(lax.rem(lane, HEAD_SIZE) < HEAD_SIZE // 2, -sine, sine)
    square = (rows, rows)
    across_row = lax.broadcasted_iota(jnp.int32, square, 0)
    across_col = lax.broadcasted_iota(jnp.int32, square, 1)
    earlier = (across_row > across_col).astype(bf16)
    expert = lax.broadcasted_iota(jnp.int32, (128, rows), 0)
    named = expert < 0
    for k in range(routes_ref.shape[0]):
        named = named | (routes_ref[k : k + 1, :] == expert)
    token = lax.broadcasted_iota(jnp.int32, (128, rows), 1)
    used = named & (token < lengths_ref[0, 0] + lengths_ref[0, 1])
    rank = contract(used.astype(bf16), earlier, 1, 1)
    place_of = jnp.where(used, rank, -1.0)
    eye = unit(rows)
    named = contract(eye, named.astype(bf16), 1, 1) > 0.5
    one.first()
    two.first()
    three.first()
    one.second()
    two.second()
    one.third()
    one.complete()
    stores.add(all_qkv, all_qkv_out)

    normed = normed_ref[...]
    cosine, signed = cosine_ref[...], sine_ref[...]
    for tile in range(4):
        lanes = pl.ds(tile * 512, 512)
        part = contract(normed, flat(all_qkv, lanes), 1, 0)
        if tile < 3:
            part = turn(part, jnp.tile(cosine, (1, 4)), jnp.tile(signed, (1, 4)))
        qkv_ref[:, lanes] = part.astype(bf16)
    two.third()
    _, start_row, _ = rows_of(lengths_ref, square)
    allowed = (across_col >= start_row) & (across_col <= across_row)
    both = jnp.concatenate([allowed, allowed], axis=0)
    for g in range(KEY_VALUE_HEADS):
        if g == 0:
            three.second()
        if g == 4:
            three.third()
        key = qkv_ref[:, pl.ds(width + g * HEAD_SIZE, HEAD_SIZE)]
        value = qkv_ref[:, pl.ds(width + half + g * HEAD_SIZE, HEAD_SIZE)]
        query = jnp.concatenate(
            [qkv_ref[:, pl.ds((2 * g + p) * HEAD_SIZE, HEAD_SIZE)] for p in range(2)], axis=0
        )
        scores = jnp.where(both, contract(query, key, 1, 1) * HEAD_SIZE**-0.5, NEGATIVE)
        raised = jnp.exp(scores - jnp.max(scores, axis=1, keepdims=True))
        prob = raised / jnp.sum(raised, axis=1, keepdims=True)
        prob_ref[g] = prob
        mixed = contract(prob.astype(bf16), value, 1, 0).astype(bf16)
        for p in range(2):
            mixed_ref[:, pl.ds((2 * g + p) * HEAD_SIZE, HEAD_SIZE)] = mixed[
                p * rows : (p + 1) * rows
            ]
    two.complete()
    for source, target in (
        (all_out, all_out_out), (normed_ref, normed_out), (qkv_ref, qkv_out),
        (mixed_ref, mixed_out), (prob_ref, prob_out), (cosine_ref, cosine_out),
        (sine_ref, sine_out),
    ):
        stores.add(source, target)
    _, _, live = rows_of(lengths_ref, (rows, 1))
    hidden = inputs + live.astype(f32) * contract(
        mixed_ref[...], flat(all_out, pl.ds(0, width)), 1, 0
    )
    hidden_ref[...] = hidden
    stores.add(hidden_ref, hidden_out)
    normed_two = (hidden * norm_scale(hidden) * gain_two_ref[...].astype(f32).reshape(1, width)).astype(bf16)
    payload_ref[pl.ds(0, rows), :] = normed_two
    logits = contract(normed_two, flat(all_out, pl.ds(width, 128)), 1, 0)
    logits = jnp.where(named, logits, NEGATIVE)
    raised = jnp.exp(logits - jnp.max(logits, axis=1, keepdims=True))
    gates = raised / jnp.sum(raised, axis=1, keepdims=True)
    gates_ref[...] = gates
    upper = gates.astype(bf16)
    lower = (gates - upper.astype(f32)).astype(bf16)
    tail = pl.ds(rows, E)
    payload_ref[tail, :] = jnp.zeros((E, width), bf16)
    for spot, table in enumerate((upper, lower)):
        payload_ref[tail, pl.ds(spot * 256, rows)] = contract(table, eye, 0, 0)[:E].astype(bf16)
    payload_ref[tail, pl.ds(512, rows)] = place_of[:E].astype(bf16)
    stores.add(gates_ref, gates_out)
    stores.add(payload_ref, payload_out)
    stores.wait(*range(12))
    three.complete()
    one.finish()
    two.finish()
    three.finish()


def front_layer(
    tokens, lengths, routes, gain_one, gain_two, query, key, value, output, router, cotangent,
    collective_id,
):
    rows, width = tokens.shape
    share = query.shape[0]
    f32, bf16 = jnp.float32, jnp.bfloat16
    dma = pltpu.SemaphoreType.DMA
    shape = jax.ShapeDtypeStruct
    kept = (
        shape((rows + E, width), bf16),
        shape((rows, width), f32),
        shape((rows, width), bf16),
        shape((rows, 2 * width), bf16),
        shape((rows, width), bf16),
        shape((KEY_VALUE_HEADS, 2 * rows, rows), f32),
        shape((rows, 128), f32),
        shape((rows, 128), f32),
        shape((rows, 128), f32),
        shape((16, share, 2 * width), bf16),
        shape((16, share, width + 256), bf16),
    )
    anywhere = pl.BlockSpec(memory_space=pl.ANY)
    inputs = (
        tokens, lengths, routes.T, gain_one, gain_two, query, key, value, output, router.T,
        cotangent,
    )
    taken = [inputs[place] for place in (0, 2, 3, 4, 9, 10)]
    return pl.pallas_call(
        front_kernel,
        out_shape=(*kept, shape((16, rows, width), bf16)),
        in_specs=[anywhere, pl.BlockSpec(memory_space=pltpu.SMEM)] + [anywhere] * 9,
        out_specs=(anywhere,) * 12,
        scratch_shapes=[pltpu.VMEM(value.shape, value.dtype) for value in (*taken, *kept)]
        + [dma((10,)), dma((12,))] + [dma((22,))] * 6,
        compiler_params=pltpu.CompilerParams(
            collective_id=collective_id, has_side_effects=True, vmem_limit_bytes=62 * 1024 * 1024
        ),
        cost_estimate=pl.CostEstimate(
            flops=24 * 10**9, bytes_accessed=10**8, transcendentals=10**6
        ),
    )(*inputs)


def chip_of(step):
    _, _, _, y, high = place()
    side, rise = select(SIDE_OF_STEP, step), select(UP_OF_STEP, step)
    return lax.rem(high + side, 2) * 4 + lax.rem(y + rise, 4)


class Scatter:
    def __init__(
        self, source, sums, bufs, sems, split, crossed, local_sem=None, axis="shard"
    ):
        self.source, self.sums, self.bufs, self.sems = source, sums, bufs, sems
        self.count, self.split, self.local_sem = bufs[1].shape[1], split, local_sem
        self.crossed = crossed
        self.half = (self.count - crossed + 16) // 32 * 16 + crossed
        self.spots = Spots(axis)
        self.pending = {}

    def block(self, step):
        if self.sums is None:
            return self.source.at[self.spots.of_step(step)]
        return self.sums.at[step]

    def load(self, step):
        return pltpu.make_async_copy(
            self.source.at[self.spots.of_step(step)], self.sums.at[step], self.local_sem.at[step]
        )

    def swap(self, step):
        return pltpu.make_async_remote_copy(
            src_ref=self.source.at[self.spots.of_step(step, True)],
            dst_ref=self.bufs[0].at[step],
            send_sem=self.sems[0].at[step],
            recv_sem=self.sems[1].at[step],
            device_id=self.spots.targets["mate"],
            device_id_type=MESH,
        )

    def begin(self):
        for step in (7, 4, 6, 5, 2, 1, 3, 0):
            if self.spots.paired:
                self.swap(jnp.int32(step)).start()
            if self.sums is not None:
                self.load(jnp.int32(step)).start()

    def settle(self, step):
        step = jnp.int32(step)
        if self.sums is not None:
            self.load(step).wait()
        if self.spots.paired:
            self.swap(step).wait_recv()
            add_rows(self.block(step), self.bufs[0].at[step], 0, self.count)

    def send(self, number, source, target_ref, target):
        copy = pltpu.make_async_remote_copy(
            src_ref=source,
            dst_ref=target_ref,
            send_sem=self.sems[0].at[number],
            recv_sem=self.sems[1].at[number],
            device_id=self.spots.targets[target],
            device_id_type=MESH,
        )
        copy.start()
        self.pending[number] = copy

    def first(self, o):
        rows, count = self.crossed, self.count
        if o == 0:
            self.settle(7)
            far = self.block(jnp.int32(7))
            ends = (rows, self.half, count)
        else:
            self.settle(4)
            far = self.block(jnp.int32(4))
            ends = (0, self.split, count)
            self.meet(17, far)
        upper, lower = ends[1] - ends[0], ends[2] - ends[1]
        self.send(8 + o, far.at[pl.ds(ends[0], upper)], self.bufs[3].at[o, pl.ds(0, upper)], "up")
        self.send(
            10 + o, far.at[pl.ds(ends[1], lower)], self.bufs[4].at[o, pl.ds(0, lower)], "down"
        )
        if o == 0:
            for place_of, step in enumerate((7, 6, 5)):
                if place_of > 0:
                    self.settle(step)
                if rows > 0:
                    self.send(
                        17 + place_of,
                        self.block(jnp.int32(step)).at[pl.ds(0, rows)],
                        self.bufs[6].at[place_of],
                        "across",
                    )

    def meet(self, number, block):
        if self.crossed > 0:
            self.pending[number].wait_recv()
            add_rows(block, self.bufs[6].at[number - 17], 0, self.crossed)

    def second(self, o):
        above, below = (6, 2)[o], (5, 1)[o]
        first, middle = (self.crossed, 0)[o], (self.half, self.split)[o]
        count = self.count - first
        if o == 1:
            self.settle(above)
            self.settle(below)
        above, below = self.block(jnp.int32(above)), self.block(jnp.int32(below))
        if o == 1:
            self.meet(18, above)
            self.meet(19, below)
        part, here = pl.ds(first, count), pl.ds(0, count)
        self.pending[8 + o].wait_recv()
        add_rows(above, self.bufs[3].at[o], first, middle - first)
        self.send(12 + o, above.at[part], self.bufs[1].at[o, here], "up")
        self.pending[10 + o].wait_recv()
        add_rows(below, self.bufs[4].at[o], middle, self.count - middle)
        self.send(14 + o, below.at[part], self.bufs[2].at[o, here], "down")

    def third(self, o):
        step = (3, 0)[o]
        self.settle(step)
        block = self.block(jnp.int32(step))
        first = (self.crossed, 0)[o]
        self.pending[12 + o].wait_recv()
        add_rows(block, self.bufs[1].at[o], first, self.count - first)
        self.pending[14 + o].wait_recv()
        add_rows(block, self.bufs[2].at[o], first, self.count - first)
        if o == 0 and self.bufs[5] is not None:
            self.send(16, block, self.bufs[5], "across")

    def last(self, emit):
        self.pending[16].wait_recv()
        own, beside = self.block(jnp.int32(0)), self.bufs[5]

        def body(step, carry):
            span = pl.ds(pl.multiple_of(step * 16, 16), 16)
            emit(span, own[span, :].astype(jnp.float32) + beside[span, :].astype(jnp.float32))
            return carry

        lax.fori_loop(0, self.count // 16, body, 0)

    def finish(self):
        for step in range(8 if self.spots.paired else 0):
            self.swap(jnp.int32(step)).wait_send()
        for copy in self.pending.values():
            copy.wait_send()


def scatter_scratch(count, width, split, crossed, swapped=8):
    kind = jnp.bfloat16
    return [
        pltpu.VMEM((swapped, count, width), kind),
        pltpu.VMEM((2, count, width), kind),
        pltpu.VMEM((2, count, width), kind),
        pltpu.VMEM((2, split, width), kind),
        pltpu.VMEM((2, count - split, width), kind),
        pltpu.VMEM((count, width), kind),
        pltpu.VMEM((3, max(crossed, 16), width), kind),
        pltpu.SemaphoreType.DMA((20,)),
        pltpu.SemaphoreType.DMA((20,)),
    ]


class Expert:
    def __init__(self, source, total, loads, bufs, sems, rest):
        (sums, local_sem), (own, own_sem, send, recv) = loads, rest
        count = own.shape[0]
        self.own = own
        self.sums = Scatter(source, sums, bufs, sems, count // 2, 0, local_sem, "replica")
        self.spread = Gather(total, count // 2, 0, (send, recv), "replica", own)
        self.store = pltpu.make_async_copy(own, total.at[lax.axis_index("replica")], own_sem)

    def turn_round(self):
        def emit(span, value):
            self.own[span, :] = value.astype(jnp.bfloat16)

        self.sums.last(emit)
        self.store.start()
        self.spread.begin()

    def finish(self):
        self.store.wait()
        self.sums.finish()
        self.spread.finish()


class Joined:
    def __init__(self, source, total, loads, rest):
        (self.cross, join_sems), (own, own_sem, send, recv) = loads, rest
        self.own = own
        load_sem, send_sem, recv_sem = join_sems
        self.load = pltpu.make_async_copy(source.at[0], own, load_sem)
        self.copy = pltpu.make_async_remote_copy(
            src_ref=source.at[1],
            dst_ref=self.cross,
            send_sem=send_sem,
            recv_sem=recv_sem,
            device_id=Spots("replica").targets["across"],
            device_id_type=MESH,
        )
        self.spread = Gather(total, own.shape[0] // 2, 0, (send, recv), "replica", own)
        self.store = pltpu.make_async_copy(own, total.at[lax.axis_index("replica")], own_sem)

    def begin(self):
        self.load.start()
        self.copy.start()

    def turn_round(self):
        self.load.wait()
        self.copy.wait_recv()
        add_rows(self.own, self.cross, 0, self.own.shape[0])
        self.store.start()
        self.spread.begin()

    def finish(self):
        self.copy.wait_send()
        self.store.wait()
        self.spread.finish()


class Total:
    def __init__(self, source, out, pieces, sems, piece):
        self.source, self.out, self.pieces = source, out, pieces
        self.sems, self.piece = sems, piece
        self.shard, self.me = lax.axis_index("shard"), lax.axis_index("replica")

    def copy(self, way, step):
        target = lax.rem(self.me + step, 8)
        if way == 0:
            source, place_of = self.piece(self.source, target), self.pieces.at[step - 1]
        else:
            source = place_of = self.piece(self.out, self.me)
        return pltpu.make_async_remote_copy(
            src_ref=source,
            dst_ref=place_of,
            send_sem=self.sems[2 * way].at[step - 1],
            recv_sem=self.sems[2 * way + 1].at[step - 1],
            device_id=(self.shard, target),
            device_id_type=MESH,
        )

    def begin(self):
        for step in range(1, 8):
            self.copy(0, step).start()

    def middle(self):
        for step in range(1, 8):
            self.copy(0, step).wait_recv()
        own = self.piece(self.source, self.me)
        result = self.piece(self.out, self.me)

        def body(turn_of, carry):
            span = pl.ds(pl.multiple_of(turn_of * 16, 16), 16)
            total = own[span, :].astype(jnp.float32)
            for step in range(7):
                total = total + self.pieces[step, span, :].astype(jnp.float32)
            result[span, :] = total.astype(jnp.bfloat16)
            return carry

        lax.fori_loop(0, self.pieces.shape[1] // 16, body, 0)
        for step in range(1, 8):
            self.copy(1, step).start()

    def end(self):
        for step in range(1, 8):
            self.copy(1, step).wait_recv()

    def finish(self):
        for step in range(1, 8):
            self.copy(0, step).wait_send()
            self.copy(1, step).wait_send()


def total_scratch(rows, width):
    dma = pltpu.SemaphoreType.DMA
    return [pltpu.VMEM((7, rows, width), jnp.bfloat16), dma((7,)), dma((7,)), dma((7,)), dma((7,))]


def expert_scratch(slab, width):
    kind, dma = jnp.bfloat16, pltpu.SemaphoreType.DMA
    return [
        pltpu.VMEM((8, slab, width), kind),
        dma((8,)),
        *scatter_scratch(slab, width, slab // 2, 0, 1),
        pltpu.VMEM((slab, width), kind),
        dma,
        dma((22,)),
        dma((22,)),
    ]


def quarter(ref, which):
    half = ref.shape[1] // 2
    return ref.at[
        pl.ds(pl.multiple_of((which // 2) * 16, 16), 16),
        pl.ds(pl.multiple_of(lax.rem(which, 2) * half, 128), half),
    ]


def norm_back(value, scale, gain, grad):
    gained = grad * gain
    return scale * gained - value * scale**3 * jnp.mean(gained * value, axis=1, keepdims=True)


def rear_kernel(
    lengths_ref, tokens_any, cotangent_any, gain_one_any, gain_two_any, payload_any, hidden_any,
    normed_any, qkv_any, mixed_any, prob_any, gates_any, cosine_any, sine_any, all_qkv_any,
    all_out_any, back_any, mixes_ref, grads_in_ref, grads_out_ref,
    output_ref, d_tokens_ref, one_total, two_total, d_in_ref, d_out_ref,
    tokens_ref, cotangent_ref, gain_one_ref, gain_two_ref, payload_ref, hidden_ref,
    normed_ref, qkv_ref, mixed_ref, prob_ref, gates_ref, cosine_ref, sine_ref, all_qkv,
    all_out, back_ref,
    *scratch,
):
    scratch = list(scratch)

    def take(count):
        taken = scratch[:count]
        del scratch[:count]
        return taken

    (load_sem,) = take(1)
    mix_sums, mix_local = take(2)
    mix_bufs, mix_sems = take(7), take(2)
    (one_blocks,) = take(1)
    one_bufs, one_sems = take(7), take(2)
    (two_blocks,) = take(1)
    two_bufs, two_sems = take(7), take(2)
    (join_cross,), join_sems, in_rest = take(1), take(3), take(4)
    out_parts = (take(2), take(7), take(2), take(4))
    (one_pieces,), one_total_sems = take(1), take(4)
    (two_pieces,), two_total_sems = take(1), take(4)
    one_part, two_part = take(2)
    mixed_grad_ref, turned_ref, qkv_grad_ref, first_grad_ref, hidden_grad_ref = take(5)
    f32, bf16 = jnp.float32, jnp.bfloat16
    rows, width = tokens_ref.shape
    half = KEY_VALUE_HEADS * HEAD_SIZE
    shard, me = lax.axis_index("shard"), lax.axis_index("replica")
    loads = Loads(load_sem)
    early = (
        (back_any, back_ref), (hidden_any, hidden_ref), (gates_any, gates_ref),
        (cotangent_any, cotangent_ref), (gain_two_any, gain_two_ref), (all_out_any, all_out),
        (mixed_any, mixed_ref), (payload_any, payload_ref),
    )
    late = (
        (qkv_any, qkv_ref), (prob_any, prob_ref), (cosine_any, cosine_ref), (sine_any, sine_ref),
        (all_qkv_any, all_qkv), (normed_any, normed_ref), (tokens_any, tokens_ref),
        (gain_one_any, gain_one_ref),
    )
    for source, target in early + late:
        loads.add(source, target)
    greet(neighbours() + [(shard, lax.rem(me + step, 8)) for step in range(1, 8)])
    mixes = Scatter(mixes_ref, mix_sums, mix_bufs, mix_sems, 96, 0, mix_local)
    one = Scatter(one_blocks, None, one_bufs, one_sems, 32, 0)
    two = Scatter(two_blocks, None, two_bufs, two_sems, 32, 0)
    matrix_in = Joined(grads_in_ref, d_in_ref, (join_cross, join_sems), in_rest)
    matrix_out = Expert(grads_out_ref, d_out_ref, *out_parts)
    one_sum = Total(one_part, one_total, one_pieces, one_total_sems, quarter)
    two_sum = Total(two_part, two_total, two_pieces, two_total_sems, quarter)
    mixes.begin()
    matrix_in.begin()
    matrix_out.sums.begin()
    matrix_out.sums.first(0)
    matrix_out.sums.first(1)
    mixes.first(0)
    mixes.first(1)
    loads.wait(*range(len(early)))

    _, _, live = rows_of(lengths_ref, (rows, 1))
    live = live.astype(f32)
    eye = unit(rows)
    line = back_ref[pl.ds(rows, E), :]
    gap = jnp.zeros((128 - E, rows), bf16)

    def columns(part):
        return contract(eye, jnp.concatenate([part.astype(bf16), gap], axis=0), 1, 1)

    gate_grad = columns(line[:, :rows]) + columns(line[:, 256 : 256 + rows])
    gates = gates_ref[...]
    logit_grad = (gates * (gate_grad - jnp.sum(gates * gate_grad, axis=1, keepdims=True))).astype(
        bf16
    )
    second_grad = back_ref[pl.ds(0, rows), :] + contract(
        logit_grad, flat(all_out, pl.ds(width, 128)), 1, 1
    )
    hidden = hidden_ref[...]
    scale_two = norm_scale(hidden)
    d_gain_two = jnp.sum(second_grad * hidden * scale_two, axis=0, keepdims=True)
    hidden_grad = cotangent_ref[...].astype(f32) + norm_back(
        hidden, scale_two, gain_two_ref[...].astype(f32).reshape(1, width), second_grad
    )
    hidden_grad_ref[...] = hidden_grad
    attn_grad = (live * hidden_grad).astype(bf16)

    def weights_of(ref, tile, lanes):
        value = ref[4 * tile : 4 * tile + 4, :, :lanes]
        return value.reshape(256, lanes)

    for tile in range(4):
        span = pl.ds(tile * 256, 256)
        mixed_grad_ref[:, span] = contract(
            attn_grad, weights_of(all_out, tile, width), 1, 1
        ).astype(bf16)
        one_blocks[4 * tile : 4 * tile + 4, :, :width] = (
            contract(mixed_ref[:, span], attn_grad, 0, 0).astype(bf16).reshape(4, 64, width)
        )
        one_blocks[4 * tile : 4 * tile + 4, :, width : width + 128] = (
            contract(payload_ref[pl.ds(0, rows), span], logit_grad, 0, 0)
            .astype(bf16)
            .reshape(4, 64, 128)
        )
    one_blocks[:, :, width + 128 :] = jnp.zeros((16, 64, 128), bf16)
    one.begin()
    one.first(0)
    matrix_in.turn_round()

    def heads(ref, g):
        return jnp.concatenate(
            [ref[:, pl.ds((2 * g + p) * HEAD_SIZE, HEAD_SIZE)] for p in range(2)], axis=0
        )

    def head_back(g):
        mixed_grad, query = heads(mixed_grad_ref, g), heads(qkv_ref, g)
        key = qkv_ref[:, pl.ds(width + g * HEAD_SIZE, HEAD_SIZE)]
        value = qkv_ref[:, pl.ds(width + half + g * HEAD_SIZE, HEAD_SIZE)]
        prob = prob_ref[g]
        prob_grad = contract(mixed_grad, value, 1, 1)
        qkv_grad_ref[:, pl.ds(width + half + g * HEAD_SIZE, HEAD_SIZE)] = contract(
            prob.astype(bf16), mixed_grad, 0, 0
        ).astype(bf16)
        score_grad = prob * (prob_grad - jnp.sum(prob * prob_grad, axis=1, keepdims=True))
        score_grad = score_grad.astype(bf16)
        query_grad = contract(score_grad, key, 1, 0) * HEAD_SIZE**-0.5
        for p in range(2):
            turned_ref[:, pl.ds((2 * g + p) * HEAD_SIZE, HEAD_SIZE)] = query_grad[
                p * rows : (p + 1) * rows
            ]
        turned_ref[:, pl.ds(width + g * HEAD_SIZE, HEAD_SIZE)] = (
            contract(score_grad, query, 0, 0) * HEAD_SIZE**-0.5
        )

    loads.wait(*range(len(early), len(early + late)))
    for g in range(4):
        head_back(g)
    matrix_out.sums.second(0)
    matrix_out.sums.second(1)
    mixes.second(0)
    one.first(1)
    for g in range(4, 8):
        head_back(g)
    matrix_in.spread.first()
    cosine, signed = cosine_ref[...], -sine_ref[...]
    for tile in range(3):
        lanes = pl.ds(tile * 512, 512)
        qkv_grad_ref[:, lanes] = turn(
            turned_ref[:, lanes], jnp.tile(cosine, (1, 4)), jnp.tile(signed, (1, 4))
        ).astype(bf16)
    qkv_grad = qkv_grad_ref[...]
    for tile in range(4):
        span = pl.ds(tile * 256, 256)
        first_grad_ref[:, span] = contract(qkv_grad, weights_of(all_qkv, tile, 2 * width), 1, 1)
        two_blocks[4 * tile : 4 * tile + 4, :, : 2 * width] = (
            contract(normed_ref[:, span], qkv_grad, 0, 0).astype(bf16).reshape(4, 64, 2 * width)
        )
    inputs = tokens_ref[...].astype(f32)
    scale_one = norm_scale(inputs)
    first_grad = first_grad_ref[...]
    d_gain_one = jnp.sum(first_grad * inputs * scale_one, axis=0, keepdims=True)
    two_blocks[:, :, 2 * width :] = jnp.zeros((16, 64, 256), bf16)
    pieces = [
        gain[:, 128 * part : 128 * part + 128]
        for gain in (d_gain_one, d_gain_two)
        for part in range(8)
    ]
    gain_tile = jnp.concatenate(pieces, axis=0).astype(bf16)
    for block in range(16):
        two_blocks[block, pl.ds(0, 16), pl.ds(2 * width, 128)] = gain_tile
    two.begin()
    mixes.second(1)
    one.second(0)
    two.first(0)
    one.second(1)
    two.first(1)
    matrix_out.sums.third(0)
    matrix_out.sums.third(1)
    d_tokens_ref[...] = hidden_grad_ref[...] + norm_back(
        inputs, scale_one, gain_one_ref[...].astype(f32).reshape(1, width), first_grad
    )

    def give_output(span, value):
        row = lax.broadcasted_iota(jnp.int32, (16, 1), 0) + span.start
        alive = (row < lengths_ref[0, 0] + lengths_ref[0, 1]).astype(f32)
        output_ref[span, :] = (hidden_ref[span, :] + alive * value).astype(bf16)

    def give(ref):
        def emit(span, value):
            ref[span, :] = value.astype(bf16)

        return emit

    mixes.third(0)
    one.third(0)
    matrix_in.spread.second()
    matrix_out.turn_round()
    two.second(0)
    two.second(1)
    one.third(1)
    matrix_in.spread.third()
    matrix_out.spread.first()
    one.last(give(one_part))
    one_sum.begin()
    mixes.third(1)
    matrix_out.spread.second()
    two.third(0)
    mixes.last(give_output)
    matrix_out.spread.third()
    two.third(1)
    one_sum.middle()
    two.last(give(two_part))
    two_sum.begin()
    two_sum.middle()
    one_sum.end()
    two_sum.end()
    for user in (mixes, one, two, matrix_in, matrix_out, one_sum, two_sum):
        user.finish()


def rear_layer(
    tokens, lengths, cotangent, gain_one, gain_two, kept, back, mixes, grads_in, grads_out, collective_id
):
    rows, width = tokens.shape
    f32, bf16 = jnp.float32, jnp.bfloat16
    vmem = pl.BlockSpec(memory_space=pltpu.VMEM)
    anywhere = pl.BlockSpec(memory_space=pl.ANY)
    dma = pltpu.SemaphoreType.DMA
    shape = jax.ShapeDtypeStruct
    wide_one, wide_two = width + 256, 2 * width + 256
    slabs = (grads_in.shape[1], grads_out.shape[0] // 8)
    inputs = (tokens, cotangent, gain_one, gain_two, *kept, back)
    return pl.pallas_call(
        rear_kernel,
        out_shape=(
            shape((rows, width), bf16),
            shape((rows, width), f32),
            shape((64, wide_one), bf16),
            shape((64, wide_two), bf16),
            *(shape((8, slab, width), bf16) for slab in slabs),
        ),
        in_specs=[pl.BlockSpec(memory_space=pltpu.SMEM)] + [anywhere] * (len(inputs) + 3),
        out_specs=(vmem,) * 4 + (anywhere,) * 2,
        scratch_shapes=[
            *(pltpu.VMEM(value.shape, value.dtype) for value in inputs),
            dma((len(inputs),)),
            pltpu.VMEM((8, rows, width), bf16),
            dma((8,)),
            *scatter_scratch(rows, width, 96, 0),
            pltpu.VMEM((16, 64, wide_one), bf16),
            *scatter_scratch(64, wide_one, 32, 0),
            pltpu.VMEM((16, 64, wide_two), bf16),
            *scatter_scratch(64, wide_two, 32, 0),
            pltpu.VMEM((slabs[0], width), bf16),
            dma,
            dma,
            dma,
            pltpu.VMEM((slabs[0], width), bf16),
            dma,
            dma((22,)),
            dma((22,)),
            *expert_scratch(slabs[1], width),
            *total_scratch(16, wide_one // 2),
            *total_scratch(16, wide_two // 2),
            pltpu.VMEM((64, wide_one), bf16),
            pltpu.VMEM((64, wide_two), bf16),
            pltpu.VMEM((rows, width), bf16),
            pltpu.VMEM((rows, width + KEY_VALUE_HEADS * HEAD_SIZE), f32),
            pltpu.VMEM((rows, 2 * width), bf16),
            pltpu.VMEM((rows, width), f32),
            pltpu.VMEM((rows, width), f32),
        ],
        compiler_params=pltpu.CompilerParams(
            collective_id=collective_id, has_side_effects=True, vmem_limit_bytes=62 * 1024 * 1024
        ),
        cost_estimate=pl.CostEstimate(
            flops=24 * 10**9, bytes_accessed=10**8, transcendentals=10**6
        ),
    )(lengths, *inputs, mixes, grads_in, grads_out.reshape(8, slabs[1], width))


def close_kernel(
    output_any, d_tokens_any, one_any, two_any, in_any, out_any,
    output_out, d_tokens_out, d_gain_one_out, d_gain_two_out, d_query_out, d_key_out,
    d_value_out, d_output_out, d_router_out, d_in_out, d_out_out,
    output_ref, d_tokens_ref, one_ref, two_ref, expert_ref, query_ref, key_ref, value_ref,
    matrix_ref, wide_ref,
    router_ref, gain_one_ref, gain_two_ref, load_sem, store_sem,
):
    f32 = jnp.float32
    width = query_ref.shape[1]
    half = key_ref.shape[1]
    loads, stores = Loads(load_sem), Loads(store_sem)
    parts = expert_ref.shape[0] // 256
    spans = [pl.ds(256 * part, 256) for part in range(parts)]
    loads.add(one_any, one_ref)
    loads.add(two_any, two_ref)
    for span in spans:
        if span.start < width:
            loads.add(in_any.at[span], expert_ref.at[span])
        else:
            loads.add(out_any.at[pl.ds(span.start - width, 256)], expert_ref.at[span])
    loads.add(output_any, output_ref)
    loads.add(d_tokens_any, d_tokens_ref)
    loads.wait(0, 1)
    query_ref[...] = two_ref[:, pl.ds(0, width)].astype(f32)
    key_ref[...] = two_ref[:, pl.ds(width, half)].astype(f32)
    value_ref[...] = two_ref[:, pl.ds(width + half, half)].astype(f32)
    matrix_ref[...] = one_ref[:, pl.ds(0, width)].astype(f32)
    router_ref[...] = contract(one_ref[:, pl.ds(width, 128)], unit(64), 0, 0)[:E]
    gains = two_ref[pl.ds(0, 16), pl.ds(2 * width, 128)].astype(f32)
    gain_one_ref[...] = gains[:8]
    gain_two_ref[...] = gains[8:]
    for source, target in (
        (query_ref, d_query_out), (key_ref, d_key_out), (value_ref, d_value_out),
        (matrix_ref, d_output_out), (router_ref, d_router_out),
        (gain_one_ref, d_gain_one_out), (gain_two_ref, d_gain_two_out),
    ):
        stores.add(source, target)
    for part, span in enumerate(spans):
        loads.wait(2 + part)
        wide_ref[span, :] = expert_ref[span, :].astype(f32)
        if part < width // 256:
            stores.add(wide_ref.at[span], d_in_out.at[span])
        else:
            stores.add(wide_ref.at[span], d_out_out.at[pl.ds(256 * part - width, 256)])
    loads.wait(2 + parts, 3 + parts)
    stores.add(output_ref, output_out)
    stores.add(d_tokens_ref, d_tokens_out)
    stores.wait(*range(9 + parts))


def close_layer(output, d_tokens, one, two, d_in, d_out):
    rows, width = output.shape
    half = KEY_VALUE_HEADS * HEAD_SIZE
    hidden = d_out.shape[0]
    f32 = jnp.float32
    shape = jax.ShapeDtypeStruct
    small = (
        (64, width), (64, half), (64, half), (64, width), (E, 64), (8, 128), (8, 128),
    )
    dma = pltpu.SemaphoreType.DMA
    anywhere = pl.BlockSpec(memory_space=pl.ANY)
    query, key, value, matrix, router, gain_one, gain_two = small
    outs = (gain_one, gain_two, query, key, value, matrix, router, (width, width), (hidden, width))
    return pl.pallas_call(
        close_kernel,
        out_shape=(
            shape(output.shape, output.dtype),
            shape(d_tokens.shape, f32),
            *(shape(extent, f32) for extent in outs),
        ),
        in_specs=[anywhere] * 6,
        out_specs=(anywhere,) * 11,
        scratch_shapes=[
            pltpu.VMEM(output.shape, output.dtype),
            pltpu.VMEM(d_tokens.shape, f32),
            pltpu.VMEM(one.shape, one.dtype),
            pltpu.VMEM(two.shape, two.dtype),
            pltpu.VMEM((width + hidden, width), d_in.dtype),
            pltpu.VMEM(query, f32),
            pltpu.VMEM(key, f32),
            pltpu.VMEM(value, f32),
            pltpu.VMEM(matrix, f32),
            pltpu.VMEM((width + hidden, width), f32),
            pltpu.VMEM(router, f32),
            pltpu.VMEM(gain_one, f32),
            pltpu.VMEM(gain_two, f32),
            dma((4 + (width + hidden) // 256,)),
            dma((9 + (width + hidden) // 256,)),
        ],
        compiler_params=pltpu.CompilerParams(vmem_limit_bytes=62 * 1024 * 1024),
        cost_estimate=pl.CostEstimate(flops=0, bytes_accessed=12 * 10**6, transcendentals=0),
    )(output, d_tokens, one, two, d_in, d_out)


def local(
    tokens,
    seq_lengths,
    routes,
    attn_gain,
    ffn_gain,
    w_query,
    key_projection,
    value_projection,
    w_output,
    w_router,
    w_in,
    w_out,
    cotangent,
):
    rows, width = tokens.shape
    payload, *kept, all_cotangent = front_layer(
        tokens, seq_lengths, routes, attn_gain, ffn_gain,
        w_query, key_projection, value_projection, w_output, w_router, cotangent, 1,
    )
    back, mixes, *grads = expert_layer(payload, all_cotangent, w_in[0], w_out[0], 2)
    output, d_tokens, one, two, d_in, d_out = rear_layer(
        tokens, seq_lengths, cotangent, attn_gain, ffn_gain, (payload, *kept), back, mixes,
        *grads, 3,
    )
    (
        output, d_tokens, d_attn_gain, d_ffn_gain, d_query, d_key, d_value, d_output, d_router,
        d_in, d_out,
    ) = close_layer(output, d_tokens, one, two, d_in.reshape(-1, width), d_out.reshape(-1, width))
    return (
        output,
        d_tokens,
        d_attn_gain.reshape(width),
        d_ffn_gain.reshape(width),
        d_query,
        d_key,
        d_value,
        d_output,
        d_router.T,
        d_in[None],
        d_out[None],
    )


def solution(mesh):
    return jax.shard_map(
        local,
        mesh=mesh,
        in_specs=(
            P(("shard", "replica"), None),
            P(("shard", "replica"), None),
            P(("shard", "replica"), None),
            P(),
            P(),
            P("shard", None),
            P("shard", None),
            P("shard", None),
            P("shard", None),
            P("shard", None),
            P("shard", None, None),
            P("shard", None, None),
            P(("shard", "replica"), None),
        ),
        out_specs=(
            P(("shard", "replica"), None),
            P(("shard", "replica"), None),
            P(),
            P(),
            P("shard", None),
            P("shard", None),
            P("shard", None),
            P("shard", None),
            P("shard", None),
            P("shard", None, None),
            P("shard", None, None),
        ),
        check_vma=False,
    )
```
